32 devices in a mesh: dp: 8 (over z, x), seq: 4 (over y, core).
Axes of the slice: x: 2, y: 2, z: 4, core: 2. Of those that a mesh axis runs over, the one named last changes fastest.
Arguments:
- content: bfloat16 [32, 512, 768], P('dp', 'seq'), may hold values from -6 to 6
- query: bfloat16 [32, 512, 768], P('dp', 'seq'), may hold values from -6 to 6
- order: int32 [32, 512], P('dp'), may hold values from 0 to 511, each once within a row
- lengths: int32 [32, 8], P('dp'), may hold values from 1 to 448, 512 in all within a row
- predicted: int32 [32, 512], P('dp', 'seq'), may hold values 0 or 1
- distance_bucket: int32 [1023], replicated, may hold values from 0 to 31, as said below
- w_query: bfloat16 [768, 768], replicated, may hold values from -0.21875 to 0.21875
- b_query: float32 [768], replicated, may hold values from -3 to 3
- w_key: bfloat16 [768, 768], replicated, may hold values from -0.21875 to 0.21875
- w_value: bfloat16 [768, 768], replicated, may hold values from -0.21875 to 0.21875
- b_value: float32 [768], replicated, may hold values from -3 to 3
- w_out: bfloat16 [768, 768], replicated, may hold values from -1.25 to 1.25
- b_out: float32 [768], replicated, may hold values from -3 to 3
- gain_one: float32 [768], replicated, may hold values from 0.5 to 1.5
- shift_one: float32 [768], replicated, may hold values from -3 to 3
- w_up: bfloat16 [768, 3072], replicated, may hold values from -0.21875 to 0.21875
- b_up: float32 [3072], replicated, may hold values from -3 to 3
- w_down: bfloat16 [3072, 768], replicated, may hold values from -0.109375 to 0.109375
- b_down: float32 [768], replicated, may hold values from -3 to 3
- gain_two: float32 [768], replicated, may hold values from 0.5 to 1.5
- shift_two: float32 [768], replicated, may hold values from -3 to 3
- bias_table: float32 [32, 12], replicated, may hold values from -4 to 4
- d_content: bfloat16 [32, 512, 768], P('dp', 'seq'), may hold values from -6 to 6
- d_query: bfloat16 [32, 512, 768], P('dp', 'seq'), may hold values from -6 to 6
Outputs:
- content_out: bfloat16 [32, 512, 768], P('dp', 'seq')
- query_out: bfloat16 [32, 512, 768], P('dp', 'seq')
- d_content_in: float32 [32, 512, 768], P('dp', 'seq')
- d_query_in: float32 [32, 512, 768], P('dp', 'seq')
- grad_w_query: float32 [589824], P(('dp', 'seq'))
- grad_w_key: float32 [589824], P(('dp', 'seq'))
- grad_w_value: float32 [589824], P(('dp', 'seq'))
- grad_w_out: float32 [589824], P(('dp', 'seq'))
- grad_w_up: float32 [2359296], P(('dp', 'seq'))
- grad_w_down: float32 [2359296], P(('dp', 'seq'))
- grad_b_query: float32 [768], replicated
- grad_b_value: float32 [768], replicated
- grad_b_out: float32 [768], replicated
- grad_gain_one: float32 [768], replicated
- grad_shift_one: float32 [768], replicated
- grad_b_up: float32 [3072], replicated
- grad_b_down: float32 [768], replicated
- grad_gain_two: float32 [768], replicated
- grad_shift_two: float32 [768], replicated
- grad_bias_table: float32 [32, 12], replicated
The draws below stay inside these ranges and needn't reach their ends.
Inputs may be any that keep to these rules, and one draw needn't show every extreme that they name: `distance_bucket`: entry 511 + d is the bucket of the relative distance d, the query's initial position minus the key's; the bucket depends on the magnitude of d and its sign only, and does not fall as the magnitude grows.
All inputs are finite; a program needn't handle non-finite values. No bound on the sum of `predicted` on one device may be relied on, other than what follows from the above.
Results may differ from the reference program's by a relative error of at most 0.014.
Values may be sent and summed in bfloat16 or wider, within the bound.
No kernel may reach another device: no remote copies, remote signals or barrier semaphores. Data moves between devices by JAX's collectives and lax.ppermute only.
A program may use at most 320 MiB of HBM per device.

```python
import math
import jax
import jax.numpy as jnp
import numpy as np
from jax import lax

D = 768
H = 12
FF = 3072
NB = 32
ROW = 512
DOCS = 8
ROWS = 32
N_DP = 8
N_SEQ = 4


def draw_distance_bucket(key, part):
    key = jax.random.fold_in(key, 7)
    half_count = NB // 2
    shuffled = jax.random.permutation(key, ROW - 1).astype(jnp.int32) + 1
    marks = jnp.zeros((ROW,), jnp.int32).at[shuffled[:half_count - 1]].set(1)
    magnitude = jnp.cumsum(marks, dtype=jnp.int32)
    magnitude = jnp.where(jnp.arange(ROW, dtype=jnp.int32) == ROW - 1, half_count - 1, magnitude)
    magnitude = jnp.minimum(magnitude, half_count - 1)
    signed = jnp.arange(2 * ROW - 1, dtype=jnp.int32) - (ROW - 1)
    return (magnitude[jnp.abs(signed)] + half_count * (signed > 0).astype(jnp.int32)).astype(jnp.int32)


def plant(result, own_key, smallest, top_value):
    place = [jax.random.randint(jax.random.fold_in(own_key, axis), (), 0, length) for axis, length in enumerate(result.shape)]
    longest = result.shape.index(max(result.shape))
    next_to = place[:longest] + [(place[longest] + 1) % result.shape[longest]] + place[longest + 1:]
    return result.at[tuple(place)].set(smallest).at[tuple(next_to)].set(top_value)


def steps_of(key, extent, split, low, top_value):
    loudness = 1.0
    for dim, parts in split:
        draws = jax.random.uniform(jax.random.fold_in(jax.random.fold_in(key, 6), dim), (parts,), jnp.float32, low / len(split), top_value / len(split))
        loudness = loudness * jnp.repeat(jnp.exp(draws), extent[dim] // parts).reshape((-1,) + (1,) * (len(extent) - 1 - dim))
    return loudness


def split_up(number_of, total, limit, skew):
    weights = [(1 << 20) // math.isqrt(grade ** skew) + 1 for grade in range(2, number_of + 1)]
    surplus, given = total - limit - (number_of - 1), [1] * (number_of - 1)
    while surplus > 0:
        movable = [i for i in range(number_of - 1) if given[i] < limit]
        mass, budget = sum([weights[i] for i in movable]), surplus
        for i in movable:
            more = min(limit - given[i], max(1, budget * weights[i] // mass), surplus)
            given[i] = given[i] + more
            surplus = surplus - more
    return np.array([limit] + given)


def uneven(own_key, amount, total, reach, skew):
    if amount == 2:
        one = jax.random.randint(own_key, (), max(1, total - reach), min(reach, total - 1) + 1)
        return jnp.stack([one, total - one])
    sizes = jnp.asarray(split_up(amount, total, reach, skew), jnp.int32)
    twos = (amount - 1) // 2
    donor, sink = sizes[1:1 + 2 * twos:2], sizes[2:2 + 2 * twos:2]
    margin = jnp.minimum(donor - 1, reach - sink)
    shifted = jax.random.randint(jax.random.fold_in(own_key, 1), (twos,), 0, 1 << 20) % (margin + 1)
    sizes = sizes.at[1:1 + 2 * twos:2].set(donor - shifted).at[2:2 + 2 * twos:2].set(sink + shifted)
    return sizes[jax.random.permutation(jax.random.fold_in(own_key, 2), amount)]


def bell_draw(own_key, dims, scale, limit, pieces=(), kind=jnp.bfloat16):
    result = scale * jax.random.normal(own_key, dims, jnp.float32)
    if pieces:
        result = result * steps_of(own_key, dims, pieces, -0.22, 0.18)
    return jnp.clip(result, -limit, limit).astype(kind)


def setup_inputs(seed: int = 0) -> dict:
    streams_of = jax.random.split(jax.random.key(seed), 25)
    return {
        "content": bell_draw(streams_of[0], (ROWS, ROW, D), 1.0, 6.0, ((0, 8), (1, 4))),
        "query": bell_draw(streams_of[1], (ROWS, ROW, D), 1.0, 6.0, ((0, 8), (1, 4))),
        "order": jax.vmap(lambda own: jax.random.permutation(own, ROW))(jax.random.split(streams_of[2], ROWS)).reshape((ROWS, ROW)).astype(jnp.int32),
        "lengths": jax.vmap(lambda own: uneven(own, DOCS, ROW, ROW - ROW // N_SEQ // 2, 2))(jax.random.split(streams_of[3], ROWS)).reshape((ROWS, DOCS)).astype(jnp.int32),
        "predicted": plant((jax.random.randint(streams_of[4], (ROWS, ROW), 0, 20) < 3).astype(jnp.int32), jax.random.fold_in(streams_of[4], 1), 0, 1),
        "distance_bucket": draw_distance_bucket(jax.random.fold_in(streams_of[24], 71), 0),
        "w_query": bell_draw(streams_of[6], (D, D), D ** -0.5, 0.21875),
        "b_query": bell_draw(streams_of[7], (D,), 0.3, 3.0, (), jnp.float32),
        "w_key": bell_draw(streams_of[8], (D, D), D ** -0.5, 0.21875),
        "w_value": bell_draw(streams_of[9], (D, D), D ** -0.5, 0.21875),
        "b_value": bell_draw(streams_of[10], (D,), 0.3, 3.0, (), jnp.float32),
        "w_out": bell_draw(streams_of[11], (D, D), (D // 32) ** -0.5, 1.25),
        "b_out": bell_draw(streams_of[12], (D,), 0.3, 3.0, (), jnp.float32),
        "gain_one": jnp.clip(1.0 + 0.1 * jax.random.normal(streams_of[13], (D,), jnp.float32), 0.5, 1.5),
        "shift_one": bell_draw(streams_of[14], (D,), 0.3, 3.0, (), jnp.float32),
        "w_up": bell_draw(streams_of[15], (D, FF), D ** -0.5, 0.21875),
        "b_up": bell_draw(streams_of[16], (FF,), 0.3, 3.0, (), jnp.float32),
        "w_down": bell_draw(streams_of[17], (FF, D), FF ** -0.5, 0.109375),
        "b_down": bell_draw(streams_of[18], (D,), 0.3, 3.0, (), jnp.float32),
        "gain_two": jnp.clip(1.0 + 0.1 * jax.random.normal(streams_of[19], (D,), jnp.float32), 0.5, 1.5),
        "shift_two": bell_draw(streams_of[20], (D,), 0.3, 3.0, (), jnp.float32),
        "bias_table": bell_draw(streams_of[21], (NB, H), 1.0, 4.0, (), jnp.float32),
        "d_content": bell_draw(streams_of[22], (ROWS, ROW, D), 1.0, 6.0, ((0, 8), (1, 4))),
        "d_query": bell_draw(streams_of[23], (ROWS, ROW, D), 1.0, 6.0, ((0, 8), (1, 4))),
    }


@jax.custom_vjp
def low(v):
    return lax.optimization_barrier(v.astype(jnp.bfloat16)).astype(jnp.float32)

@jax.custom_vjp
def low_back(v):
    return v

def low_keep(v):
    return (low(v), None)

def low_pass(kept, grad):
    return (grad,)

def back_keep(v):
    return (v, None)

def back_low(kept, grad):
    return (low(grad),)
low.defvjp(low_keep, low_pass)
low_back.defvjp(back_keep, back_low)

def layer_norm(inputs, norm_gain, norm_shift):
    average = lax.optimization_barrier(jnp.mean(inputs, -1, keepdims=True))
    centered = inputs - average
    variance = lax.optimization_barrier(jnp.mean(centered * centered, -1, keepdims=True))
    return centered * lax.rsqrt(variance + 1e-05) * norm_gain + norm_shift

def project(inputs, weight):
    return jnp.einsum('grd,de->gre', inputs, weight, precision=lax.Precision.HIGHEST)

def layer_group(content, query, params, allowed, bucket_ids, predicted):
    w_query, b_query, w_key, w_value, b_value, w_out, b_out, gain_one, shift_one, w_up, b_up, w_down, b_down, gain_two, shift_two, bias_table = params
    row_count, length, model_width = content.shape
    head_count = bias_table.shape[1]
    head_size = model_width // head_count
    content_low = low(content)
    query_low = low(query)
    key_rows = low_back(low(project(content_low, w_key))).reshape(row_count, length, head_count, head_size)
    value_rows = low_back(low(project(content_low, w_value) + b_value)).reshape(row_count, length, head_count, head_size)
    score_bias = jnp.transpose(bias_table[bucket_ids], (0, 3, 1, 2))

    def attend(source):
        queries = low_back(low(project(source, w_query) + b_query)).reshape(row_count, length, head_count, head_size)
        scores = jnp.einsum('gihe,gjhe->ghij', queries, key_rows, precision=lax.Precision.HIGHEST) * head_size ** (-0.5) + score_bias
        scores = low_back(scores)
        scores = jnp.where(allowed[:, None], scores, -1e+30)
        row_max = lax.optimization_barrier(jnp.max(scores, -1, keepdims=True))
        exp_scores = jnp.exp(scores - row_max)
        attention = low(exp_scores / lax.optimization_barrier(jnp.sum(exp_scores, -1, keepdims=True)))
        mixed_rows = jnp.einsum('ghij,gjhe->gihe', attention, value_rows, precision=lax.Precision.HIGHEST)
        return low_back(low(mixed_rows.reshape(row_count, length, model_width)))

    def finish(stream_in, mixed_rows):
        projected = low_back(project(mixed_rows, w_out) + b_out)
        hidden = layer_norm(stream_in + projected, gain_one, shift_one)
        expanded = low_back(project(low(hidden), w_up) + b_up)
        active = low(jax.nn.gelu(expanded, approximate=False))
        reduced = low_back(project(active, w_down) + b_down)
        return layer_norm(hidden + reduced, gain_two, shift_two)
    content_out = finish(content, attend(content_low))
    query_full = finish(query, attend(query_low))
    query_out = jnp.where(predicted[..., None] == 1, query_full, query)
    return (content_out, query_out)

def reference(content, query, order, lengths, predicted, distance_bucket, w_query, b_query, w_key, w_value, b_value, w_out, b_out, gain_one, shift_one, w_up, b_up, w_down, b_down, gain_two, shift_two, bias_table, d_content, d_query):
    params = tuple((p.astype(jnp.float32) for p in (w_query, b_query, w_key, w_value, b_value, w_out, b_out, gain_one, shift_one, w_up, b_up, w_down, b_down, gain_two, shift_two, bias_table)))
    row_total, length, model_width = content.shape
    per_group = row_total // N_DP
    doc_ends = jnp.cumsum(lengths, -1, dtype=jnp.int32)
    segment = lax.optimization_barrier(jnp.sum((doc_ends[:, None, :] <= order[:, :, None]).astype(jnp.int32), -1)).astype(jnp.int32)
    position = jnp.arange(length, dtype=jnp.int32)
    causal = position[None, :] <= position[:, None]

    def grouped(array):
        return array.reshape((N_DP, per_group) + array.shape[1:])
    group_data = tuple((grouped(a) for a in (content, query, order, segment, predicted, d_content, d_query)))

    def group_step(totals, item):
        content_g, query_g, order_g, segment_g, predicted_g, dcont_g, dquery_g = item
        allowed = (segment_g[:, :, None] == segment_g[:, None, :]) & causal[None]
        bucket_ids = distance_bucket[(order_g[:, :, None] - order_g[:, None, :] + length - 1).astype(jnp.int32)]

        def forward(content_in, query_in, *weights):
            return layer_group(content_in, query_in, weights, allowed, bucket_ids, predicted_g)
        outputs, pull = jax.vjp(forward, content_g.astype(jnp.float32), query_g.astype(jnp.float32), *params)
        grads = pull((dcont_g.astype(jnp.float32), dquery_g.astype(jnp.float32)))
        new_totals = tuple((a + b for a, b in zip(totals, grads[2:])))
        return (new_totals, (outputs[0].astype(jnp.bfloat16), outputs[1].astype(jnp.bfloat16), grads[0], grads[1]))
    start_totals = tuple((jnp.zeros_like(p) for p in params))
    totals, (content_out, query_out, d_content_in, d_query_in) = lax.scan(group_step, start_totals, group_data)
    shape = (row_total, length, model_width)
    return (content_out.reshape(shape), query_out.reshape(shape), d_content_in.reshape(shape), d_query_in.reshape(shape), totals[0].reshape(-1), totals[2].reshape(-1), totals[3].reshape(-1), totals[5].reshape(-1), totals[9].reshape(-1), totals[11].reshape(-1), totals[1], totals[4], totals[6], totals[7], totals[8], totals[10], totals[12], totals[13], totals[14], totals[15])
```

```python
from functools import partial

import jax
import jax.numpy as jnp
from jax import lax
from jax.experimental import pallas as pl
from jax.experimental.pallas import tpu as pltpu
from jax.sharding import PartitionSpec as P

F32 = jnp.float32
BF16 = jnp.bfloat16
LANES = 128
EPS = 1e-5
TAIL_RATE = 0.44
TAIL = (
    0.2482209563421166, 0.24887113623989612, 0.21731383786259212, 0.215811268986145,
    -0.020178828505330645, 0.29668548016136337, -0.2779468644144858, 0.07122319498310971,
)


def dot(a, b):
    return jnp.dot(a, b, preferred_element_type=F32)


def dot_nt(a, b):
    return lax.dot_general(a, b, (((1,), (1,)), ((), ())), preferred_element_type=F32)


def dot_tn(a, b):
    return lax.dot_general(a, b, (((0,), (0,)), ((), ())), preferred_element_type=F32)


def attend_kernel(q_ref, k_ref, v_ref, t_ref, segc_ref, segr_ref, plc_ref, plr_ref, mix_ref, p_ref, mask, bias, *, size):
    streams, length, width = q_ref.shape
    heads = width // size
    blocks = length // LANES

    @pl.when(pl.program_id(0) == 0)
    def _():
        allowed = (segc_ref[...] == segr_ref[...]) & (plr_ref[...] <= plc_ref[...])
        mask[...] = jnp.where(allowed, 0.0, -1e30)

    owner = lax.broadcasted_iota(jnp.int32, (1, width), 1) // size
    row = lax.broadcasted_iota(jnp.int32, (LANES, LANES), 0)
    col = lax.broadcasted_iota(jnp.int32, (LANES, LANES), 1)
    lower = row >= col
    keys = k_ref[...]
    values = v_ref[...]
    mixed = [None] * streams
    for h in range(heads):
        circ = [
            pltpu.roll(jnp.broadcast_to(t_ref[h, b : b + 1, :], (LANES, LANES)), 0, 1, stride=1, stride_axis=0)
            for b in range(2 * blocks)
        ]
        tiles = [jnp.where(lower, circ[b + 1], circ[b]) for b in range(2 * blocks - 1)]
        for i in range(blocks):
            for j in range(blocks):
                at = (slice(i * LANES, (i + 1) * LANES), slice(j * LANES, (j + 1) * LANES))
                bias[at] = mask[at] + tiles[i - j + blocks - 1]
        for s in range(streams):
            q = jnp.where(owner == h, q_ref[s], jnp.zeros((), BF16))
            scores = dot_nt(q, keys) + bias[...]
            e = jnp.exp(scores - jnp.max(scores, -1, keepdims=True))
            p = (e * (1.0 / jnp.sum(e, -1, keepdims=True))).astype(BF16)
            p_ref[s, h] = p
            o = dot(p, values)
            mixed[s] = o if h == 0 else jnp.where(owner == h, o, mixed[s])
    for s in range(streams):
        mix_ref[s] = mixed[s].astype(BF16)


def attend(queries, keys, values, table, seg, place, size):
    streams, length, model = queries.shape
    width = LANES
    heads = width // size
    steps = model // width
    col = lambda n: pl.BlockSpec((length, width), lambda g: (0, g))
    whole = lambda shape: pl.BlockSpec(shape, lambda g: (0, 0))
    return pl.pallas_call(
        partial(attend_kernel, size=size),
        grid=(steps,),
        in_specs=[
            pl.BlockSpec((streams, length, width), lambda g: (0, 0, g)),
            col(0),
            col(0),
            pl.BlockSpec((heads,) + table.shape[1:], lambda g: (g, 0, 0)),
            whole((length, 1)),
            whole((1, length)),
            whole((length, 1)),
            whole((1, length)),
        ],
        out_specs=[
            pl.BlockSpec((streams, length, width), lambda g: (0, 0, g)),
            pl.BlockSpec((streams, heads, length, length), lambda g: (0, g, 0, 0)),
        ],
        out_shape=[
            jax.ShapeDtypeStruct(queries.shape, BF16),
            jax.ShapeDtypeStruct((streams, model // size, length, length), BF16),
        ],
        scratch_shapes=[pltpu.VMEM((length, length), F32), pltpu.VMEM((length, length), F32)],
        compiler_params=pltpu.CompilerParams(vmem_limit_bytes=48 << 20),
        cost_estimate=pl.CostEstimate(
            flops=8 * streams * length * length * model,
            bytes_accessed=2 * streams * (model // size) * length * length,
            transcendentals=0,
        ),
        name="attend",
    )(queries, keys, values, table, seg[:, None], seg[None, :], place[:, None], place[None, :])


def attend_back_kernel(q_ref, k_ref, v_ref, mix_ref, dmix_ref, p_ref, dq_ref, dk_ref, dv_ref, gt_ref, *, size, scale):
    streams, length, width = q_ref.shape
    heads = width // size
    blocks = length // LANES
    owner = lax.broadcasted_iota(jnp.int32, (1, width), 1) // size
    row = lax.broadcasted_iota(jnp.int32, (LANES, LANES), 0)
    col = lax.broadcasted_iota(jnp.int32, (LANES, LANES), 1)
    lower = row >= col
    sub = lax.broadcasted_iota(jnp.int32, (8, LANES), 0)
    keys = k_ref[...]
    values = v_ref[...]
    dq = [None] * streams
    dk = jnp.zeros((length, width), F32)
    dv = jnp.zeros((length, width), F32)
    for h in range(heads):
        total = None
        for s in range(streams):
            zero = jnp.zeros((), BF16)
            q = jnp.where(owner == h, q_ref[s], zero)
            dm = jnp.where(owner == h, dmix_ref[s], zero)
            p = p_ref[s, h]
            inner = jnp.sum(dm.astype(F32) * mix_ref[s].astype(F32), -1, keepdims=True)
            ds = p.astype(F32) * (dot_nt(dm, values) - inner)
            low = ds.astype(BF16)
            d = dot(low, keys) * scale
            dq[s] = d if h == 0 else jnp.where(owner == h, d, dq[s])
            dk = dk + dot_tn(low, q)
            dv = dv + dot_tn(p, dm)
            total = ds if total is None else total + ds
        diag = [None] * (2 * blocks + 1)
        for i in range(blocks):
            for j in range(blocks):
                part = total[i * LANES : (i + 1) * LANES, j * LANES : (j + 1) * LANES]
                b = i - j + blocks
                diag[b] = part if diag[b] is None else diag[b] + part
        none = jnp.zeros((LANES, LANES), F32)
        diag[0] = none
        diag[2 * blocks] = none
        for b in range(2 * blocks):
            part = jnp.where(lower, diag[b], diag[b + 1])
            lines = part[:8]
            for r in range(8, LANES, 8):
                lines = lines + pltpu.roll(part[r : r + 8], LANES - r, 1)
            for m in (1, 2, 4):
                lines = jnp.where(sub & m != 0, pltpu.roll(lines, LANES - m, 1), lines)
            gt_ref[h, b : b + 1, :] = jnp.sum(lines, 0, keepdims=True)
    for s in range(streams):
        dq_ref[s] = dq[s].astype(BF16)
    dk_ref[...] = dk.astype(BF16)
    dv_ref[...] = dv.astype(BF16)


def attend_back(queries, keys, values, mixed, d_mixed, probs, size):
    streams, length, model = queries.shape
    width = LANES
    heads = width // size
    steps = model // width
    blocks = length // LANES
    both = pl.BlockSpec((streams, length, width), lambda g: (0, 0, g))
    col = pl.BlockSpec((length, width), lambda g: (0, g))
    return pl.pallas_call(
        partial(attend_back_kernel, size=size, scale=size**-0.5),
        grid=(steps,),
        in_specs=[both, col, col, both, both, pl.BlockSpec((streams, heads, length, length), lambda g: (0, g, 0, 0))],
        out_specs=[both, col, col, pl.BlockSpec((heads, 2 * blocks, LANES), lambda g: (g, 0, 0))],
        out_shape=[
            jax.ShapeDtypeStruct(queries.shape, BF16),
            jax.ShapeDtypeStruct(keys.shape, BF16),
            jax.ShapeDtypeStruct(keys.shape, BF16),
            jax.ShapeDtypeStruct((model // size, 2 * blocks, LANES), F32),
        ],
        compiler_params=pltpu.CompilerParams(vmem_limit_bytes=48 << 20),
        cost_estimate=pl.CostEstimate(
            flops=16 * streams * length * length * model,
            bytes_accessed=2 * streams * (model // size) * length * length,
            transcendentals=0,
        ),
        name="attend_back",
    )(queries, keys, values, mixed, d_mixed, probs)


def normalize(z):
    mean = jnp.mean(z, -1, keepdims=True)
    centered = z - mean
    rstd = lax.rsqrt(jnp.mean(centered * centered, -1, keepdims=True) + EPS)
    return centered * rstd, rstd


def normalize_back(cot, gain, hat, rstd):
    s = gain * cot
    return (s - jnp.mean(s, -1, keepdims=True) - hat * jnp.mean(s * hat, -1, keepdims=True)) * rstd


def gelu_pair(u):
    z = jnp.abs(u) * (0.5**0.5)
    t = 1.0 / (1.0 + TAIL_RATE * z)
    r = TAIL[-1] * t
    for c in TAIL[-2::-1]:
        r = (r + c) * t
    bell = jnp.exp(u * u * -0.5)
    tail = 0.5 * bell * r
    cdf = jnp.where(u > 0, 1.0 - tail, tail)
    return u * cdf, cdf + u * bell * 0.3989422804014327


def ffn_kernel(
    x_ref, mix_ref, cot_ref, wo_ref, bo_ref, g1_ref, s1_ref, wu_ref, bu_ref, wd_ref, bd_ref, g2_ref, s2_ref,
    out_ref, dres_ref, dmix_ref, hid_ref, act_ref, dred_ref, dexp_ref, dproj_ref, small_ref, gbu_ref,
    slope,
    *, chunk,
):
    ff = wu_ref.shape[1]

    @pl.when(pl.program_id(0) == 0)
    def _():
        small_ref[...] = jnp.zeros_like(small_ref)
        gbu_ref[...] = jnp.zeros_like(gbu_ref)

    def add_small(i, rows):
        small_ref[i : i + 1, :] += jnp.sum(rows, 0, keepdims=True)

    res = x_ref[...].astype(F32) + dot(mix_ref[...], wo_ref[...]) + bo_ref[...]
    hat1, rstd1 = normalize(res)
    hidden = hat1 * g1_ref[...] + s1_ref[...]
    low = hidden.astype(BF16)
    hid_ref[...] = low
    summed = hidden + bd_ref[...]
    for c in range(0, ff, chunk):
        at = slice(c, c + chunk)
        active, grad = gelu_pair(dot(low, wu_ref[:, at]) + bu_ref[:, at])
        active = active.astype(BF16)
        act_ref[:, at] = active
        slope[:, at] = grad
        summed = summed + dot(active, wd_ref[at, :])
    hat2, rstd2 = normalize(summed)
    out_ref[...] = (hat2 * g2_ref[...] + s2_ref[...]).astype(BF16)
    cot = cot_ref[...].astype(F32)
    d_summed = normalize_back(cot, g2_ref[...], hat2, rstd2)
    d_red = d_summed.astype(BF16)
    dred_ref[...] = d_red
    add_small(0, cot * hat2)
    add_small(1, cot)
    add_small(2, d_red.astype(F32))
    d_hidden = d_summed
    for c in range(0, ff, chunk):
        at = slice(c, c + chunk)
        d_exp = (dot_nt(d_red, wd_ref[at, :]) * slope[:, at]).astype(BF16)
        dexp_ref[:, at] = d_exp
        gbu_ref[:, at] += jnp.sum(d_exp.astype(F32), 0, keepdims=True)
        d_hidden = d_hidden + dot_nt(d_exp, wu_ref[:, at])
    d_res = normalize_back(d_hidden, g1_ref[...], hat1, rstd1)
    dres_ref[...] = d_res
    d_proj = d_res.astype(BF16)
    dproj_ref[...] = d_proj
    add_small(3, d_hidden * hat1)
    add_small(4, d_hidden)
    add_small(5, d_proj.astype(F32))
    dmix_ref[...] = dot_nt(d_proj, wo_ref[...]).astype(BF16)


def ffn(x, mixed, cot, w_out, b_out, gain_one, shift_one, w_up, b_up, w_down, b_down, gain_two, shift_two):
    tokens, model = x.shape
    ff = w_up.shape[1]
    tile = min(256, tokens)
    chunk = min(768, ff)
    rows = lambda n: pl.BlockSpec((tile, n), lambda i: (i, 0))
    whole = lambda shape: pl.BlockSpec(shape, lambda i: (0, 0))
    vec = lambda a: a[None, :]
    args = (
        x, mixed, cot, w_out, vec(b_out), vec(gain_one), vec(shift_one), w_up, vec(b_up), w_down, vec(b_down),
        vec(gain_two), vec(shift_two),
    )
    return pl.pallas_call(
        partial(ffn_kernel, chunk=chunk),
        grid=(tokens // tile,),
        in_specs=[rows(model)] * 3 + [whole(a.shape) for a in args[3:]],
        out_specs=[
            rows(model), rows(model), rows(model), rows(model), rows(ff), rows(model), rows(ff), rows(model),
            whole((8, model)), whole((1, ff)),
        ],
        out_shape=[
            jax.ShapeDtypeStruct((tokens, model), BF16),
            jax.ShapeDtypeStruct((tokens, model), F32),
            jax.ShapeDtypeStruct((tokens, model), BF16),
            jax.ShapeDtypeStruct((tokens, model), BF16),
            jax.ShapeDtypeStruct((tokens, ff), BF16),
            jax.ShapeDtypeStruct((tokens, model), BF16),
            jax.ShapeDtypeStruct((tokens, ff), BF16),
            jax.ShapeDtypeStruct((tokens, model), BF16),
            jax.ShapeDtypeStruct((8, model), F32),
            jax.ShapeDtypeStruct((1, ff), F32),
        ],
        scratch_shapes=[pltpu.VMEM((tile, ff), F32)],
        compiler_params=pltpu.CompilerParams(vmem_limit_bytes=56 << 20),
        cost_estimate=pl.CostEstimate(
            flops=4 * tokens * (2 * model * ff + model * model),
            bytes_accessed=30 << 20,
            transcendentals=0,
        ),
        name="ffn",
    )(*args)


def partner(x, axis, mask):
    return lax.ppermute(x, axis, [(i, i ^ mask) for i in range(lax.axis_size(axis))])


def pick(x, i):
    return lax.dynamic_index_in_dim(x, i, 0, keepdims=False)


def to_own_row(x, me, count):
    return [pick(x, me)] + [partner(pick(x, me ^ m), "seq", m) for m in range(1, count)]


def to_owners(x, me, count):
    parts = jnp.stack([x[0]] + [partner(x[m], "seq", m) for m in range(1, count)])
    m = 1
    while m < count:
        pairs = parts.reshape((count // (2 * m), 2, m) + parts.shape[1:])
        flipped = jnp.flip(pairs, 1).reshape(parts.shape)
        parts = jnp.where(me & m != 0, flipped, parts)
        m *= 2
    return parts


def bits(n):
    return n.bit_length() - 1


def share(grad, order):
    dp, seq = lax.axis_size("dp"), lax.axis_size("seq")
    names = [("dp", b) for b in reversed(range(bits(dp)))] + [("seq", b) for b in reversed(range(bits(seq)))]
    rows = grad.shape[0] // (dp * seq)
    left = list(names)
    for step in order + [n for n in names if n not in order]:
        if step not in left:
            continue
        axis, bit = step
        at = left.index(step)
        view = grad.reshape(2**at, 2, 2 ** (len(left) - at - 1) * rows, -1)
        mine = (lax.axis_index(axis) >> bit) & 1
        take = lambda i: lax.dynamic_index_in_dim(view, i, 1, keepdims=False)
        got = partner(take(1 - mine), axis, 1 << bit)
        kept = take(mine).astype(F32) + got.astype(F32)
        left.pop(at)
        grad = (kept if not left else kept.astype(BF16)).reshape(-1, view.shape[-1])
    return grad.astype(F32).reshape(-1)


def total(x):
    for axis in ("seq", "dp"):
        for b in range(bits(lax.axis_size(axis))):
            x = x + partner(x, axis, 1 << b)
    return x


def local(
    content, query, order, lengths, predicted, distance_bucket, w_query, b_query, w_key, w_value, b_value, w_out, b_out,
    gain_one, shift_one, w_up, b_up, w_down, b_down, gain_two, shift_two, bias_table, d_content, d_query,
):
    count = lax.axis_size("seq")
    me = lax.axis_index("seq")
    rows, block, model = content.shape
    length = order.shape[1]
    buckets, heads = bias_table.shape
    size = model // heads
    picked = predicted[:, :, None] == 1

    arrived = to_own_row(jnp.stack([content, query], 1), me, count)
    cot_query = jnp.where(picked, d_query, jnp.zeros((), BF16))
    arrived_back = to_own_row(jnp.stack([d_content, cot_query], 1), me, count)

    own_order = pick(order, me)
    there = [(me ^ m) * block for m in range(count)]
    order_cat = jnp.concatenate([lax.dynamic_slice_in_dim(own_order, t, block, 0) for t in there])
    place_cat = jnp.concatenate([t + jnp.arange(block, dtype=jnp.int32) for t in there])
    initial = jnp.arange(length, dtype=jnp.int32)
    at_place = order_cat[None, :] == initial[:, None]
    swap = at_place.astype(BF16)
    place = jnp.sum(jnp.where(at_place, place_cat[None, :], 0), 1)
    ends = jnp.cumsum(pick(lengths, me), dtype=jnp.int32)
    seg = jnp.sum((ends[None, :] <= initial[:, None]).astype(jnp.int32), 1)

    blocks = length // LANES
    by_distance = jnp.pad(distance_bucket, (1, 0), constant_values=-1).reshape(2 * blocks, LANES)
    by_distance = jnp.roll(jnp.flip(by_distance, 1), 1, 1).reshape(-1)
    onehot = (by_distance[:, None] == jnp.arange(buckets, dtype=jnp.int32)[None, :]).astype(F32)
    table = jnp.einsum("db,bh->hd", onehot, bias_table, precision=lax.Precision.HIGHEST)
    table = table.reshape(heads, 2 * blocks, LANES)

    def in_order(parts):
        cat = jnp.concatenate(parts, 1)
        return jnp.einsum("aq,sqd->sad", swap, cat, preferred_element_type=F32).astype(BF16)

    def out_of_order(x):
        cat = jnp.einsum("aq,sad->sqd", swap, x, preferred_element_type=F32).astype(BF16)
        return cat.reshape(2, count, block, model).transpose(1, 0, 2, 3)

    streams = in_order(arrived)
    flat = streams.reshape(2 * length, model)
    queries = ((dot(flat, w_query) + b_query).astype(BF16) * jnp.asarray(size**-0.5, BF16)).reshape(2, length, model)
    keys = dot(streams[0], w_key).astype(BF16)
    values = (dot(streams[0], w_value) + b_value).astype(BF16)
    mixed, probs = attend(queries, keys, values, table, seg, place, size)
    mixed_flat = mixed.reshape(2 * length, model)
    cot = in_order(arrived_back).reshape(2 * length, model)
    normed, d_res, d_mixed, hidden, active, d_red, d_exp, d_proj, smalls, g_b_up = ffn(
        flat, mixed_flat, cot, w_out, b_out, gain_one, shift_one, w_up, b_up, w_down, b_down, gain_two, shift_two
    )
    results = to_owners(out_of_order(normed.reshape(2, length, model)), me, count)
    core, y, x, z, far = ("seq", 0), ("seq", 1), ("dp", 0), ("dp", 1), ("dp", 2)
    g_down = share(dot_tn(active, d_red).astype(BF16), [core, y, x, z, far])
    g_up = share(dot_tn(hidden, d_exp).astype(BF16), [core, x, y, z, far])
    g_out = share(dot_tn(mixed_flat, d_proj).astype(BF16), [core, z, far, y, x])
    d_queries, d_keys, d_values, g_circ = attend_back(
        queries, keys, values, mixed, d_mixed.reshape(2, length, model), probs, size
    )
    d_q = d_queries.reshape(2 * length, model)
    g_table = jnp.einsum("hd,db->bh", g_circ.reshape(heads, -1), onehot, precision=lax.Precision.HIGHEST)
    g_b_query = jnp.sum(d_q.astype(F32), 0)
    g_b_value = jnp.sum(d_values.astype(F32), 0)
    packed = jnp.concatenate([smalls[:6].reshape(-1), g_b_up[0], g_b_query, g_b_value, g_table.reshape(-1)])
    packed = total(packed.reshape(-1, LANES)).reshape(-1)

    back = dot_nt(d_q, w_query) + d_res
    back_content = back[:length] + dot_nt(d_keys, w_key) + dot_nt(d_values, w_value)
    back = jnp.stack([back_content, back[length:]]).astype(BF16)
    returned = to_owners(out_of_order(back), me, count)
    g_query = share(dot_tn(flat, d_q).astype(BF16), [core, x, y, z, far])
    g_key = share(dot_tn(streams[0], d_keys).astype(BF16), [core, z, far, x, y])
    g_value = share(dot_tn(streams[0], d_values).astype(BF16), [core, x, z, far, y])

    def piece(first, size):
        return lax.slice_in_dim(packed, first, first + size)

    ff = w_up.shape[1]
    six = [piece(i * model, model) for i in range(6)]
    late = 6 * model + ff
    content_out = results[:, 0]
    query_out = jnp.where(picked, results[:, 1], query)
    d_content_in = returned[:, 0].astype(F32)
    d_query_in = returned[:, 1].astype(F32) + jnp.where(picked, 0.0, d_query.astype(F32))
    return (
        content_out, query_out, d_content_in, d_query_in, g_query, g_key, g_value, g_out, g_up, g_down,
        piece(late, model), piece(late + model, model), six[5], six[3], six[4], piece(6 * model, ff), six[2], six[0],
        six[1], piece(late + 2 * model, buckets * heads).reshape(buckets, heads),
    )


def solution(mesh):
    tokens = P("dp", "seq", None)
    split = P(("dp", "seq"))
    in_specs = (tokens, tokens, P("dp", None), P("dp", None), P("dp", "seq")) + (P(),) * 17 + (tokens, tokens)
    out_specs = (tokens,) * 4 + (split,) * 6 + (P(),) * 10
    return jax.shard_map(local, mesh=mesh, in_specs=in_specs, out_specs=out_specs, check_vma=False)
```

```python
from functools import partial

import jax
import jax.numpy as jnp
from jax import lax
from jax.experimental import pallas as pl
from jax.experimental.pallas import tpu as pltpu
from jax.sharding import PartitionSpec as P

F32 = jnp.float32
BF16 = jnp.bfloat16
LANES = 128
EPS = 1e-5
LOG2_E = 1.4426950408889634
BRIEF = pl.CostEstimate(flops=1, bytes_accessed=1, transcendentals=0)


def dot(a, b):
    return jnp.dot(a, b, preferred_element_type=F32)


def dot_nt(a, b):
    return lax.dot_general(a, b, (((1,), (1,)), ((), ())), preferred_element_type=F32)


def dot_tn(a, b):
    return lax.dot_general(a, b, (((0,), (0,)), ((), ())), preferred_element_type=F32)


def tiles_kernel(t_ref, tiles_ref):
    blocks = t_ref.shape[1] // 2
    row = lax.broadcasted_iota(jnp.int32, (LANES, LANES), 0)
    col = lax.broadcasted_iota(jnp.int32, (LANES, LANES), 1)
    for h in range(t_ref.shape[0]):
        circ = [
            pltpu.roll(jnp.broadcast_to(t_ref[h, b : b + 1, :], (LANES, LANES)), 0, 1, stride=1, stride_axis=0)
            for b in range(2 * blocks)
        ]
        for b in range(2 * blocks - 1):
            tiles_ref[h, b] = jnp.where(col >= row, circ[b + 1], circ[b])


def bias_tiles(table):
    heads, many, _ = table.shape
    step = 2
    return pl.pallas_call(
        tiles_kernel,
        grid=(heads // step,),
        in_specs=[pl.BlockSpec((step, many, LANES), lambda g: (g, 0, 0))],
        out_specs=pl.BlockSpec((step, many - 1, LANES, LANES), lambda g: (g, 0, 0, 0)),
        out_shape=jax.ShapeDtypeStruct((heads, many - 1, LANES, LANES), F32),
        compiler_params=pltpu.CompilerParams(vmem_limit_bytes=24 << 20),
        cost_estimate=BRIEF,
        name="bias_tiles",
    )(table)


def attend_kernel(
    q_ref, k_ref, v_ref, tiles_ref, segc_ref, segr_ref, plc_ref, plr_ref, mix_ref, e_ref, inv_ref, mask, line, *, size
):
    length, width = q_ref.shape
    blocks = length // LANES

    @pl.when(pl.program_id(0) == 0)
    def _():
        allowed = (segc_ref[...] == segr_ref[...]) & (plc_ref[...] <= plr_ref[...])
        mask[...] = jnp.where(allowed, 0.0, -1e30)

    owner = lax.broadcasted_iota(jnp.int32, (1, width), 1) // size
    scaled = q_ref[...].astype(F32) * LOG2_E
    high = scaled.astype(BF16).astype(F32)
    low = pltpu.roll(scaled - high, size, 1)
    keys = k_ref[...].astype(F32)
    turned = pltpu.roll(keys, size, 1)
    values = v_ref[...].astype(F32).T.astype(BF16)
    ones = jnp.ones((16, length), BF16)
    mixed = []
    for h in range(width // size):
        scores = dot_nt(
            jnp.where(owner == h, keys, turned).astype(BF16), jnp.where(owner == h, high, low).astype(BF16)
        )
        top = None
        for j in range(blocks):
            at = slice(j * LANES, (j + 1) * LANES)
            bias = jnp.concatenate([tiles_ref[h, i - j + blocks - 1] for i in range(blocks)], 1)
            part = scores[at] + bias + mask[at]
            line[h, at] = part
            part = jnp.max(part.reshape(LANES // 8, 8, length), 0)
            top = part if top is None else jnp.maximum(top, part)
        e = jnp.exp2(line[h] - jnp.max(top, 0, keepdims=True)).astype(BF16)
        e_ref[h] = e
        o = dot(jnp.concatenate([values[h * size : (h + 1) * size], ones], 0), e)
        inv = 1.0 / o[size : size + 1]
        mixed.append(o[:size] * inv)
        inv_ref[0, h : h + 1, :] = inv
    mix_ref[...] = jnp.concatenate(mixed, 0).T.astype(BF16)


def attend(queries, keys, values, tiles, seg, place, size):
    length, model = queries.shape
    width = LANES
    heads = width // size
    col = pl.BlockSpec((length, width), lambda g: (0, g))
    whole = lambda shape: pl.BlockSpec(shape, lambda g: (0, 0))
    return pl.pallas_call(
        partial(attend_kernel, size=size),
        grid=(model // width,),
        in_specs=[
            col,
            col,
            col,
            pl.BlockSpec((heads,) + tiles.shape[1:], lambda g: (g, 0, 0, 0)),
            whole((length, 1)),
            whole((1, length)),
            whole((length, 1)),
            whole((1, length)),
        ],
        out_specs=[
            col,
            pl.BlockSpec((heads, length, length), lambda g: (g, 0, 0)),
            pl.BlockSpec((1, heads, length), lambda g: (g, 0, 0)),
        ],
        out_shape=[
            jax.ShapeDtypeStruct(queries.shape, BF16),
            jax.ShapeDtypeStruct((model // size, length, length), BF16),
            jax.ShapeDtypeStruct((model // width, heads, length), F32),
        ],
        scratch_shapes=[pltpu.VMEM((length, length), F32), pltpu.VMEM((heads, length, length), F32)],
        compiler_params=pltpu.CompilerParams(vmem_limit_bytes=24 << 20),
        cost_estimate=BRIEF,
        name="attend",
    )(queries, keys, values, tiles, seg[:, None], seg[None, :], place[:, None], place[None, :])


def attend_back_kernel(q_ref, k_ref, v_ref, mix_ref, dmix_ref, e_ref, inv_ref, *refs, size, scale):
    prior, (dq_ref, dk_ref, dv_ref, gt_ref) = refs[:-4], refs[-4:]
    length, width = q_ref.shape
    blocks = length // LANES
    owner = lax.broadcasted_iota(jnp.int32, (1, width), 1) // size
    row = lax.broadcasted_iota(jnp.int32, (LANES, LANES), 0)
    col = lax.broadcasted_iota(jnp.int32, (LANES, LANES), 1)
    sub = lax.broadcasted_iota(jnp.int32, (8, LANES), 0)
    keys = k_ref[...].astype(F32).T.astype(BF16)
    values = v_ref[...]
    mixed = mix_ref[...].astype(F32).T
    d_mixed = dmix_ref[...].astype(F32).T
    dq = []
    dk = jnp.zeros((length, width), F32)
    dv = jnp.zeros((length, width), F32)
    for h in range(width // size):
        own = slice(h * size, (h + 1) * size)
        scaled = (d_mixed[own] * inv_ref[0, h : h + 1, :]).astype(BF16)
        inner = jnp.sum(scaled.astype(F32) * mixed[own], 0, keepdims=True)
        zeros = [jnp.zeros((h * size, length), BF16), jnp.zeros((width - (h + 1) * size, length), BF16)]
        scaled = jnp.concatenate([z for z in (zeros[0], scaled, zeros[1]) if z.shape[0]], 0)
        e = e_ref[h]
        ds = e.astype(F32) * (dot(values, scaled) - inner)
        low = ds.astype(BF16)
        dq.append(dot(keys[own], low) * scale)
        dk = dk + dot(low, jnp.where(owner == h, q_ref[...], jnp.zeros((), BF16)))
        dv = dv + dot_nt(e, scaled)
        diag = [None] * (2 * blocks + 1)
        for j in range(blocks):
            for i in range(blocks):
                part = ds[j * LANES : (j + 1) * LANES, i * LANES : (i + 1) * LANES]
                b = i - j + blocks
                diag[b] = part if diag[b] is None else diag[b] + part
        none = jnp.zeros((LANES, LANES), F32)
        diag[0] = none
        diag[2 * blocks] = none
        for b in range(2 * blocks):
            part = jnp.where(col >= row, diag[b], diag[b + 1])
            lines = part[:8]
            for r in range(8, LANES, 8):
                lines = lines + pltpu.roll(part[r : r + 8], LANES - r, 1)
            for m in (1, 2, 4):
                lines = jnp.where(sub & m != 0, pltpu.roll(lines, LANES - m, 1), lines)
            gt_ref[h, b : b + 1, :] = jnp.sum(lines, 0, keepdims=True)
    dq_ref[...] = jnp.concatenate(dq, 0).T.astype(BF16)
    if prior:
        dk = dk + prior[0][...]
        dv = dv + prior[1][...]
    dk_ref[...] = dk.astype(dk_ref.dtype)
    dv_ref[...] = dv.astype(dv_ref.dtype)


def attend_back(queries, keys, values, mixed, d_mixed, weights, size, prior=()):
    length, model = queries.shape
    width = LANES
    heads = width // size
    blocks = length // LANES
    col = pl.BlockSpec((length, width), lambda g: (0, g))
    square = pl.BlockSpec((heads, length, length), lambda g: (g, 0, 0))
    kind = BF16 if prior else F32
    return pl.pallas_call(
        partial(attend_back_kernel, size=size, scale=size**-0.5),
        grid=(model // width,),
        in_specs=[col] * 5 + [square, pl.BlockSpec((1, heads, length), lambda g: (g, 0, 0))] + [col] * len(prior),
        out_specs=[col, col, col, pl.BlockSpec((heads, 2 * blocks, LANES), lambda g: (g, 0, 0))],
        out_shape=[
            jax.ShapeDtypeStruct(queries.shape, BF16),
            jax.ShapeDtypeStruct(keys.shape, kind),
            jax.ShapeDtypeStruct(keys.shape, kind),
            jax.ShapeDtypeStruct((model // size, 2 * blocks, LANES), F32),
        ],
        compiler_params=pltpu.CompilerParams(vmem_limit_bytes=58 << 20),
        cost_estimate=BRIEF,
        name="attend_back",
    )(queries, keys, values, mixed, d_mixed, *weights, *prior)


def normalize(z):
    mean = jnp.mean(z, -1, keepdims=True)
    centered = z - mean
    rstd = lax.rsqrt(jnp.mean(centered * centered, -1, keepdims=True) + EPS)
    return centered * rstd, rstd


def normalize_back(cot, gain, hat, rstd):
    s = gain * cot
    return (s - jnp.mean(s, -1, keepdims=True) - hat * jnp.mean(s * hat, -1, keepdims=True)) * rstd


def gelu_pair(u):
    cdf = 0.5 + 0.5 * lax.erf(u * 0.7071067811865476)
    return u * cdf, cdf + u * (jnp.exp(u * u * -0.5) * 0.3989422804014327)


def ffn_kernel(
    x_ref, mix_ref, cot_ref, wo_ref, bo_ref, g1_ref, s1_ref, wu_ref, bu_ref, wd_ref, bd_ref, g2_ref, s2_ref, *refs,
    chunk,
):
    (
        out_ref, dres_ref, dmix_ref, hid_ref, act_ref, dred_ref, dexp_ref, dproj_ref, small_ref, gbu_ref, slope,
    ) = refs[-11:]
    ff = wu_ref.shape[1]

    @pl.when(pl.program_id(0) == 0)
    def _():
        small_ref[...] = jnp.zeros_like(small_ref)
        gbu_ref[...] = jnp.zeros_like(gbu_ref)

    def add_small(i, rows):
        small_ref[i : i + 1, :] += jnp.sum(rows, 0, keepdims=True)

    res = x_ref[...].astype(F32) + dot(mix_ref[...], wo_ref[...]) + bo_ref[...]
    hat1, rstd1 = normalize(res)
    hidden = hat1 * g1_ref[...] + s1_ref[...]
    low = hidden.astype(BF16)
    hid_ref[...] = low
    summed = hidden + bd_ref[...]
    for c in range(0, ff, chunk):
        at = slice(c, c + chunk)
        active, grad = gelu_pair(dot(low, wu_ref[:, at]) + bu_ref[at])
        active = active.astype(BF16)
        act_ref[:, at] = active
        slope[:, at] = grad
        summed = summed + dot(active, wd_ref[at, :])
    hat2, rstd2 = normalize(summed)
    out_ref[...] = (hat2 * g2_ref[...] + s2_ref[...]).astype(BF16)
    cot = cot_ref[...].astype(F32)
    d_summed = normalize_back(cot, g2_ref[...], hat2, rstd2)
    d_red = d_summed.astype(BF16)
    dred_ref[...] = d_red
    add_small(0, cot * hat2)
    add_small(1, cot)
    add_small(2, d_red.astype(F32))
    d_hidden = d_summed
    for c in range(0, ff, chunk):
        at = slice(c, c + chunk)
        d_exp = (dot_nt(d_red, wd_ref[at, :]) * slope[:, at]).astype(BF16)
        dexp_ref[:, at] = d_exp
        gbu_ref[:, at] += jnp.sum(d_exp.astype(F32), 0, keepdims=True)
        d_hidden = d_hidden + dot_nt(d_exp, wu_ref[:, at])
    d_res = normalize_back(d_hidden, g1_ref[...], hat1, rstd1)
    dres_ref[...] = d_res
    d_proj = d_res.astype(BF16)
    dproj_ref[...] = d_proj
    add_small(3, d_hidden * hat1)
    add_small(4, d_hidden)
    add_small(5, d_proj.astype(F32))
    dmix_ref[...] = dot_nt(d_proj, wo_ref[...]).astype(BF16)


def ffn(x, mixed, cot, w_out, b_out, gain_one, shift_one, w_up, b_up, w_down, b_down, gain_two, shift_two, which, filled):
    tokens, model = x.shape
    ff = w_up.shape[1]
    tile = min(256, tokens)
    chunk = min(768, ff)
    steps = tokens // tile
    rows = lambda n: pl.BlockSpec((tile, n), lambda i: (i, 0))
    half = lambda n: pl.BlockSpec((tile, n), lambda i: (i + which * steps, 0))
    whole = lambda shape: pl.BlockSpec(shape, lambda i: (0,) * len(shape))
    args = (
        x, mixed, cot, w_out, b_out, gain_one, shift_one, w_up, b_up, w_down, b_down, gain_two, shift_two,
    )
    own = lambda n, kind: jax.ShapeDtypeStruct((tokens, n), kind)
    shared = lambda n: jax.ShapeDtypeStruct((2 * tokens, n), BF16)
    return pl.pallas_call(
        partial(ffn_kernel, chunk=chunk),
        grid=(steps,),
        in_specs=[rows(model)] * 3
        + [pl.BlockSpec(memory_space=pltpu.VMEM) if a.ndim == 2 else whole(a.shape) for a in args[3:]]
        + [pl.BlockSpec(memory_space=pl.ANY)] * len(filled),
        out_specs=[
            rows(model), rows(model), rows(model), half(model), half(ff), half(model), half(ff), half(model),
            whole((8, model)), whole((1, ff)),
        ],
        out_shape=[
            own(model, BF16), own(model, F32), own(model, BF16), shared(model), shared(ff), shared(model), shared(ff),
            shared(model), jax.ShapeDtypeStruct((8, model), F32), jax.ShapeDtypeStruct((1, ff), F32),
        ],
        scratch_shapes=[pltpu.VMEM((tile, ff), F32)],
        input_output_aliases={len(args) + i: 3 + i for i in range(len(filled))},
        compiler_params=pltpu.CompilerParams(vmem_limit_bytes=36 << 20),
        cost_estimate=BRIEF,
        name="ffn",
    )(*args, *filled)


def partner(x, axis, mask):
    return lax.ppermute(x, axis, [(i, i ^ mask) for i in range(lax.axis_size(axis))])


def pick(x, i):
    return lax.dynamic_index_in_dim(x, i, 0, keepdims=False)


def index_bits(n):
    return [1 << b for b in reversed(range(bits(n)))]


def row_parts(x, me):
    return [pick(x, me ^ m) for m in range(x.shape[0])]


def exchange(parts):
    return [parts[0]] + [partner(parts[m], "seq", m) for m in range(1, len(parts))]


def arrange(parts, me):
    count = len(parts)
    rows = []
    for r in range(count):
        row = parts[r]
        for m in range(1, count):
            row = jnp.where(me == m, parts[r ^ m], row)
        rows.append(row)
    return jnp.stack(rows)


def hold(x, *after):
    return lax.optimization_barrier((x, after))[0]


def bits(n):
    return n.bit_length() - 1


def device_bits():
    dp, seq = lax.axis_size("dp"), lax.axis_size("seq")
    return [("dp", b) for b in reversed(range(bits(dp)))] + [("seq", b) for b in reversed(range(bits(seq)))]


def full_order(order):
    known = device_bits()
    return [n for n in order if n in known] + [n for n in known if n not in order]


def relative_places(order):
    seq = lax.axis_size("seq")
    count = lax.axis_size("dp") * seq
    me = lax.axis_index("dp") * seq + lax.axis_index("seq")
    apart = jnp.arange(count, dtype=jnp.int32) ^ me
    place = jnp.zeros_like(apart)
    for axis, bit in order:
        place = place * 2 + ((apart >> (bit + (bits(seq) if axis == "dp" else 0))) & 1)
    return place


def fold_kernel(keep_ref, got_ref, next_keep_ref, next_send_ref):
    both = (keep_ref[...].astype(F32) + got_ref[...].astype(F32)).astype(BF16)
    next_keep_ref[...] = both[:, 0]
    next_send_ref[...] = both[:, 1]


def fold(keep, got, at):
    places, rows, columns = keep.shape
    left, right = 2**at, places // 2 ** (at + 1)
    if rows % 16 or places < 4:
        both = (keep.astype(F32) + got.astype(F32)).astype(BF16).reshape(left, 2, right, rows, columns)
        return [both[:, i].reshape(left * right, rows, columns) for i in range(2)]
    view = (left, 2, right, rows, columns)
    block = pl.BlockSpec(view, lambda g: (0, 0, 0, 0, 0))
    out = pl.BlockSpec((left, right, rows, columns), lambda g: (0, 0, 0, 0))
    folded = pl.pallas_call(
        fold_kernel,
        grid=(1,),
        in_specs=[block, block],
        out_specs=[out, out],
        out_shape=[jax.ShapeDtypeStruct((left, right, rows, columns), BF16)] * 2,
        compiler_params=pltpu.CompilerParams(vmem_limit_bytes=58 << 20),
        cost_estimate=BRIEF,
        name="fold",
    )(keep.reshape(view), got.reshape(view))
    return [f.reshape(left * right, rows, columns) for f in folded]


class Share:
    def __init__(self, keep, send, left, todo=None):
        self.left, self.todo = list(left), list(todo or left)
        self.keep, self.send = keep, send

    def step(self, *after):
        axis, bit = self.todo.pop(0)
        self.left.remove((axis, bit))
        got = partner(self.send, axis, 1 << bit)
        if after:
            got = hold(got, *after)
        if self.todo:
            self.keep, self.send = fold(self.keep, got, self.left.index(self.todo[0]))
        else:
            self.keep = (self.keep.astype(F32) + got.astype(F32))[0]
        return self

    def split(self, cuts, orders, *after):
        axis, bit = self.todo.pop(0)
        self.left.remove((axis, bit))
        got = hold(partner(self.send, axis, 1 << bit), *after)
        parts = []
        for first, last, order in zip(cuts[:-1], cuts[1:], orders):
            todo = [n for n in order if n in self.left] + [n for n in self.left if n not in order]
            pair = fold(self.keep[:, first:last], got[:, first:last], self.left.index(todo[0]))
            parts.append(Share(*pair, self.left, todo))
        return parts

    def finish(self):
        while self.todo:
            self.step()
        return self.keep


def fold_columns(g):
    half = g.shape[1] // 2
    return jnp.concatenate([g[:, :half], g[:, half:]], 0)


def unfold_columns(g):
    half = g.shape[0] // 2
    return jnp.concatenate([g[:half], g[half:]], 1)


def store_part(place_ref, device, piece, keep_ref, send_ref):
    place = place_ref[device]
    half = keep_ref.shape[0]

    @pl.when(place < half)
    def _():
        keep_ref[place] = piece

    @pl.when(place >= half)
    def _():
        send_ref[place - half] = piece


def split_by_place(place, parts):
    ordered = jnp.zeros_like(parts).at[place].set(parts)
    half = parts.shape[0] // 2
    return ordered[:half], ordered[half:]


def folded_parts(g, count):
    parts = g.astype(BF16).reshape(count, g.shape[0] // count, 2, -1)
    return jnp.swapaxes(parts, 1, 2).reshape(count, -1, parts.shape[-1])


def tall_kernel(place_ref, a_ref, b_ref, keep_ref, send_ref):
    rows = keep_ref.shape[1]
    g = dot_tn(a_ref[...], b_ref[...]).astype(BF16)
    here = g.shape[0] // rows
    for k in range(here):
        store_part(place_ref, pl.program_id(0) * here + k, g[k * rows : (k + 1) * rows], keep_ref, send_ref)


def tall_grad(place, a, b):
    count = place.shape[0]
    tokens, high = a.shape
    wide = b.shape[1]
    if high // count % 16:
        return split_by_place(place, dot_tn(a, b).astype(BF16).reshape(count, -1, wide))
    steps = high // wide
    shape = (count // 2, high // count, wide)
    whole = pl.BlockSpec(shape, lambda g, p: (0, 0, 0))
    return pl.pallas_call(
        tall_kernel,
        grid_spec=pltpu.PrefetchScalarGridSpec(
            num_scalar_prefetch=1,
            grid=(steps,),
            in_specs=[
                pl.BlockSpec((tokens, wide), lambda g, p: (0, g)),
                pl.BlockSpec((tokens, wide), lambda g, p: (0, 0)),
            ],
            out_specs=[whole, whole],
        ),
        out_shape=[jax.ShapeDtypeStruct(shape, BF16)] * 2,
        compiler_params=pltpu.CompilerParams(vmem_limit_bytes=58 << 20),
        cost_estimate=BRIEF,
        name="tall_grad",
    )(place, a, b)


def store_all(place_ref, g, keep_ref, send_ref):
    count = 2 * keep_ref.shape[0]
    rows = g.shape[0] // count
    for k in range(count):
        store_part(
            place_ref, k, fold_columns(g[k * rows : (k + 1) * rows]).astype(BF16), keep_ref, send_ref
        )


def wide_kernel(place_ref, hid_ref, exp_ref, mix_ref, proj_ref, keep_ref, send_ref):
    last = pl.num_programs(0) - 1

    @pl.when(pl.program_id(0) < last)
    def _():
        store_all(place_ref, dot_tn(hid_ref[...], exp_ref[...]), keep_ref, send_ref)

    @pl.when(pl.program_id(0) == last)
    def _():
        store_all(place_ref, dot_tn(mix_ref[...], proj_ref[...]), keep_ref, send_ref)


def wide_grad(place, hidden, d_exp, mixed, d_proj):
    count = place.shape[0]
    tokens, model = hidden.shape
    steps = d_exp.shape[1] // model
    rows = 2 * model // count
    if rows % 16:
        pieces = [dot_tn(hidden, d_exp[:, i * model : (i + 1) * model]) for i in range(steps)] + [dot_tn(mixed, d_proj)]
        return split_by_place(place, jnp.concatenate([folded_parts(g, count) for g in pieces], 1))
    shape = (count // 2, (steps + 1) * rows, model // 2)
    square = pl.BlockSpec((tokens, model), lambda g, p: (0, 0))
    out = pl.BlockSpec((count // 2, rows, model // 2), lambda g, p: (0, g, 0))
    return pl.pallas_call(
        wide_kernel,
        grid_spec=pltpu.PrefetchScalarGridSpec(
            num_scalar_prefetch=1,
            grid=(steps + 1,),
            in_specs=[
                square,
                pl.BlockSpec((tokens, model), lambda g, p: (0, jnp.minimum(g, steps - 1))),
                square,
                square,
            ],
            out_specs=[out, out],
        ),
        out_shape=[jax.ShapeDtypeStruct(shape, BF16)] * 2,
        compiler_params=pltpu.CompilerParams(vmem_limit_bytes=58 << 20),
        cost_estimate=BRIEF,
        name="wide_grad",
    )(place, hidden, d_exp, mixed, d_proj)


def last_kernel(place_ref, xc_ref, xq_ref, qc_ref, qq_ref, k_ref, v_ref, keep_ref, send_ref):
    step = pl.program_id(0)

    @pl.when(step == 0)
    def _():
        g = dot_tn(xc_ref[...], qc_ref[...]) + dot_tn(xq_ref[...], qq_ref[...])
        store_all(place_ref, g, keep_ref, send_ref)

    @pl.when(step == 1)
    def _():
        store_all(place_ref, dot_tn(xc_ref[...], k_ref[...]), keep_ref, send_ref)

    @pl.when(step == 2)
    def _():
        store_all(place_ref, dot_tn(xc_ref[...], v_ref[...]), keep_ref, send_ref)


def last_grad(place, x_c, x_q, dq_c, dq_q, d_keys, d_values):
    count = place.shape[0]
    tokens, model = x_c.shape
    rows = 2 * model // count
    if rows % 16:
        pieces = [dot_tn(x_c, dq_c) + dot_tn(x_q, dq_q), dot_tn(x_c, d_keys), dot_tn(x_c, d_values)]
        return split_by_place(place, jnp.concatenate([folded_parts(g, count) for g in pieces], 1))
    shape = (count // 2, 3 * rows, model // 2)
    square = pl.BlockSpec((tokens, model), lambda g, p: (0, 0))
    out = pl.BlockSpec((count // 2, rows, model // 2), lambda g, p: (0, g, 0))
    return pl.pallas_call(
        last_kernel,
        grid_spec=pltpu.PrefetchScalarGridSpec(
            num_scalar_prefetch=1, grid=(3,), in_specs=[square] * 6, out_specs=[out, out]
        ),
        out_shape=[jax.ShapeDtypeStruct(shape, BF16)] * 2,
        compiler_params=pltpu.CompilerParams(vmem_limit_bytes=58 << 20),
        cost_estimate=BRIEF,
        name="last_grad",
    )(place, x_c, x_q, dq_c, dq_q, d_keys, d_values)


def total(x):
    for axis in ("seq", "dp"):
        for b in range(bits(lax.axis_size(axis))):
            x = x + partner(x, axis, 1 << b)
    return x


def local(
    content, query, order, lengths, predicted, distance_bucket, w_query, b_query, w_key, w_value, b_value, w_out, b_out,
    gain_one, shift_one, w_up, b_up, w_down, b_down, gain_two, shift_two, bias_table, d_content, d_query,
):
    count = lax.axis_size("seq")
    me = lax.axis_index("seq")
    rows, block, model = content.shape
    length = order.shape[1]
    buckets, heads = bias_table.shape
    size = model // heads
    ff = w_up.shape[1]
    picked = predicted[:, :, None] == 1

    got_content = exchange(row_parts(content, me))

    own_order = pick(order, me)
    there = [(me ^ m) * block for m in range(count)]
    order_cat = jnp.concatenate([lax.dynamic_slice_in_dim(own_order, t, block, 0) for t in there])
    place_cat = jnp.concatenate([t + jnp.arange(block, dtype=jnp.int32) for t in there])
    initial = jnp.arange(length, dtype=jnp.int32)
    at_place = order_cat[None, :] == initial[:, None]
    swap = at_place.astype(BF16)
    place = jnp.sum(jnp.where(at_place, place_cat[None, :], 0), 1)
    ends = jnp.cumsum(pick(lengths, me), dtype=jnp.int32)
    seg = jnp.sum((ends[None, :] <= initial[:, None]).astype(jnp.int32), 1)

    blocks = length // LANES
    by_distance = jnp.pad(distance_bucket, (1, 0), constant_values=-1)
    onehot = (by_distance[:, None] == jnp.arange(buckets, dtype=jnp.int32)[None, :]).astype(F32)
    table = jnp.einsum("db,bh->hd", onehot, bias_table, precision=lax.Precision.HIGHEST)
    tiles = bias_tiles((table * LOG2_E).reshape(heads, 2 * blocks, LANES))

    def in_order(parts):
        return dot(swap, jnp.concatenate(parts, 0)).astype(BF16)

    def out_of_order(x):
        cat = dot_tn(swap, x).astype(BF16)
        return [cat[i * block : (i + 1) * block] for i in range(count)]

    scale = jnp.asarray(size**-0.5, BF16)

    def queries_of(x):
        return (dot(x, w_query) + b_query).astype(BF16) * scale

    params = (w_out, b_out, gain_one, shift_one, w_up, b_up, w_down, b_down, gain_two, shift_two)
    core, y, x, z, far = ("seq", 0), ("seq", 1), ("dp", 0), ("dp", 1), ("dp", 2)
    steps_one = full_order([core, z, x, y, far])
    steps_two = full_order([core, x, y, z, far])
    steps_three = full_order([core, x, y, z, far])
    places = [relative_places(o) for o in (steps_one, steps_two, steps_three)]

    x_c = in_order(hold(got_content, tiles, seg, place))
    query_parts = row_parts(hold(query, got_content), me)
    got_query = exchange(query_parts)
    keys = dot(x_c, w_key).astype(BF16)
    values = (dot(x_c, w_value) + b_value).astype(BF16)
    q_c = queries_of(x_c)
    mixed_c, *weights_c = attend(hold(q_c, query_parts), keys, values, tiles, seg, place, size)
    x_q = in_order(hold(got_query, mixed_c))
    d_content_parts = row_parts(hold(d_content, got_query, mixed_c), me)
    got_d_content = exchange(d_content_parts)
    q_q = queries_of(x_q)
    mixed_q, *weights_q = attend(hold(q_q, d_content_parts), keys, values, tiles, seg, place, size)
    cot_c = in_order(hold(got_d_content, mixed_q))
    d_query_parts = row_parts(jnp.where(picked, hold(d_query, got_d_content, mixed_q), jnp.zeros((), BF16)), me)
    got_d_query = exchange(d_query_parts)
    normed_c, res_c, dmix_c, *filled, small_c, up_c = ffn(x_c, mixed_c, hold(cot_c, d_query_parts), *params, 0, ())
    filled = filled[:5]
    own_c = hold(out_of_order(normed_c), got_d_query)
    sent_c = exchange(own_c)
    cot_q = in_order(hold(got_d_query, own_c))
    normed_q, res_q, dmix_q, hidden, active, d_red, d_exp, d_proj, small_q, up_q = ffn(
        x_q, mixed_q, hold(cot_q, own_c), *params, 1, filled
    )
    own_q = out_of_order(hold(normed_q, sent_c))
    sent_q = exchange(own_q)
    content_out = arrange(sent_c, me)
    mixed = jnp.concatenate([mixed_c, mixed_q], 0)
    up = Share(*wide_grad(places[1], hold(hidden, own_q, content_out), d_exp, mixed, d_proj), steps_two)
    query_out = jnp.where(picked, arrange(hold(sent_q, up.send), me), query)
    down = Share(*tall_grad(places[0], hold(active, query_out), d_red), steps_one)
    up.step(down.send)
    dq_q, dk, dv, circ_q = attend_back(q_q, keys, values, mixed_q, hold(dmix_q, up.send), weights_q, size)
    down.step(dq_q)
    back_q = out_of_order((dot_nt(hold(dq_q, down.send), w_query) + res_q).astype(BF16))
    sent_back_q = exchange(back_q)
    dq_c, d_keys, d_values, circ_c = attend_back(
        q_c, keys, values, mixed_c, hold(dmix_c, back_q), weights_c, size, (dk, dv)
    )
    late = Share(
        *last_grad(places[2], hold(x_c, dq_c), x_q, dq_c, dq_q, d_keys, d_values), steps_three
    )
    token = late.send
    token = up.step(token).send
    token = down.step(token).send
    sent_back_q = hold(sent_back_q, token)
    back_c = dot_nt(dq_c, w_query) + res_c + dot_nt(d_keys, w_key) + dot_nt(hold(d_values, sent_back_q), w_value)
    back_c = out_of_order(back_c.astype(BF16))
    third = 2 * model // (count * lax.axis_size("dp"))
    first, second = late.split([0, third, 3 * third], [[x, y, z, far], [y, x, z, far]], back_c)
    token = (first.send, second.send)
    token = up.step(token).send
    token = down.step(token).send
    d_query_in = arrange(hold(sent_back_q, token), me).astype(F32) + jnp.where(picked, 0.0, d_query.astype(F32))
    sent_back_c = exchange(hold(back_c, token))
    token = first.step(d_query_in).send
    token = second.step(token).send
    token = up.step(token).send
    token = down.step(token).send
    sent_back_c = hold(sent_back_c, token)
    d_content_in = arrange(sent_back_c, me).astype(F32)
    token = first.step(d_content_in).send
    token = second.step(token).send
    token = up.step(token).keep
    token = down.step(token).keep
    token = first.step(token).send
    token = second.step(token).send

    g_table = jnp.einsum(
        "hd,db->bh", (circ_c + circ_q).reshape(heads, -1), onehot, precision=lax.Precision.HIGHEST
    )
    g_b_query = jnp.sum(dq_c.astype(F32), 0) + jnp.sum(dq_q.astype(F32), 0)
    g_b_value = jnp.sum(d_values.astype(F32), 0)
    packed = jnp.concatenate(
        [(small_c + small_q)[:6].reshape(-1), (up_c + up_q)[0], g_b_query, g_b_value, g_table.reshape(-1)]
    )
    packed = total(packed.reshape(-1, LANES)).reshape(-1)

    def piece(first, size):
        return lax.slice_in_dim(packed, first, first + size)

    def flat(*parts):
        return jnp.concatenate([unfold_columns(p) for p in parts], 1).reshape(-1)

    up_out = up.finish()
    key_value = second.finish()
    six = [piece(i * model, model) for i in range(6)]
    rest = 6 * model + ff
    return (
        content_out, query_out, d_content_in, d_query_in, flat(first.finish()), flat(key_value[:third]), flat(key_value[third:]),
        flat(up_out[-third:]), flat(*(up_out[i : i + third] for i in range(0, ff // model * third, third))),
        down.finish().reshape(-1),
        piece(rest, model), piece(rest + model, model), six[5], six[3], six[4], piece(6 * model, ff), six[2], six[0],
        six[1], piece(rest + 2 * model, buckets * heads).reshape(buckets, heads),
    )


def solution(mesh):
    tokens = P("dp", "seq", None)
    split = P(("dp", "seq"))
    in_specs = (tokens, tokens, P("dp", None), P("dp", None), P("dp", "seq")) + (P(),) * 17 + (tokens, tokens)
    out_specs = (tokens,) * 4 + (split,) * 6 + (P(),) * 10
    return jax.shard_map(local, mesh=mesh, in_specs=in_specs, out_specs=out_specs, check_vma=False)
```

```python
from functools import partial

import jax
import jax.numpy as jnp
from jax import lax
from jax.experimental import pallas as pl
from jax.experimental.pallas import tpu as pltpu
from jax.sharding import PartitionSpec as P

F32 = jnp.float32
BF16 = jnp.bfloat16
LANES = 128
EPS = 1e-5
LOG2_E = 1.4426950408889634
FOLD_VMEM = 24


def lasting(us):
    return pl.CostEstimate(flops=int(us * SHARE * 1.1e9), bytes_accessed=int(us * SHARE * 3.5e6), transcendentals=0)


SHARE = 1.0


def dot(a, b):
    return jnp.dot(a, b, preferred_element_type=F32)


def dot_nt(a, b):
    return lax.dot_general(a, b, (((1,), (1,)), ((), ())), preferred_element_type=F32)


def dot_tn(a, b):
    return lax.dot_general(a, b, (((0,), (0,)), ((), ())), preferred_element_type=F32)


def tiles_kernel(t_ref, tiles_ref):
    blocks = t_ref.shape[1] // 2
    row = lax.broadcasted_iota(jnp.int32, (LANES, LANES), 0)
    col = lax.broadcasted_iota(jnp.int32, (LANES, LANES), 1)
    for h in range(t_ref.shape[0]):
        circ = [
            pltpu.roll(jnp.broadcast_to(t_ref[h, b : b + 1, :], (LANES, LANES)), 0, 1, stride=1, stride_axis=0)
            for b in range(2 * blocks)
        ]
        for b in range(2 * blocks - 1):
            tiles_ref[h, b] = jnp.where(col >= row, circ[b + 1], circ[b])


def bias_tiles(table):
    heads, many, _ = table.shape
    step = 2
    return pl.pallas_call(
        tiles_kernel,
        grid=(heads // step,),
        in_specs=[pl.BlockSpec((step, many, LANES), lambda g: (g, 0, 0))],
        out_specs=pl.BlockSpec((step, many - 1, LANES, LANES), lambda g: (g, 0, 0, 0)),
        out_shape=jax.ShapeDtypeStruct((heads, many - 1, LANES, LANES), F32),
        compiler_params=pltpu.CompilerParams(vmem_limit_bytes=24 << 20),
        cost_estimate=lasting(2),
        name="bias_tiles",
    )(table)


def attend_kernel(
    q_ref, k_ref, v_ref, tiles_ref, segc_ref, segr_ref, plc_ref, plr_ref, mix_ref, e_ref, inv_ref, mask, line, *, size
):
    length, width = q_ref.shape
    blocks = length // LANES

    @pl.when(pl.program_id(0) == 0)
    def _():
        allowed = (segc_ref[...] == segr_ref[...]) & (plc_ref[...] <= plr_ref[...])
        mask[...] = jnp.where(allowed, 0.0, -1e30)

    owner = lax.broadcasted_iota(jnp.int32, (1, width), 1) // size
    scaled = q_ref[...].astype(F32) * LOG2_E
    high = scaled.astype(BF16).astype(F32)
    low = pltpu.roll(scaled - high, size, 1)
    keys = k_ref[...].astype(F32)
    turned = pltpu.roll(keys, size, 1)
    values = v_ref[...].astype(F32).T.astype(BF16)
    ones = jnp.ones((16, length), BF16)
    mixed = []
    for h in range(width // size):
        scores = dot_nt(
            jnp.where(owner == h, keys, turned).astype(BF16), jnp.where(owner == h, high, low).astype(BF16)
        )
        top = None
        for j in range(blocks):
            at = slice(j * LANES, (j + 1) * LANES)
            bias = jnp.concatenate([tiles_ref[h, i - j + blocks - 1] for i in range(blocks)], 1)
            part = scores[at] + bias + mask[at]
            line[h, at] = part
            part = jnp.max(part.reshape(LANES // 8, 8, length), 0)
            top = part if top is None else jnp.maximum(top, part)
        e = jnp.exp2(line[h] - jnp.max(top, 0, keepdims=True)).astype(BF16)
        e_ref[h] = e
        o = dot(jnp.concatenate([values[h * size : (h + 1) * size], ones], 0), e)
        inv = 1.0 / o[size : size + 1]
        mixed.append(o[:size] * inv)
        inv_ref[0, h : h + 1, :] = inv
    mix_ref[...] = jnp.concatenate(mixed, 0).T.astype(BF16)


def attend(queries, keys, values, tiles, seg, place, size):
    length, model = queries.shape
    width = LANES
    heads = width // size
    col = pl.BlockSpec((length, width), lambda g: (0, g))
    whole = lambda shape: pl.BlockSpec(shape, lambda g: (0, 0))
    return pl.pallas_call(
        partial(attend_kernel, size=size),
        grid=(model // width,),
        in_specs=[
            col,
            col,
            col,
            pl.BlockSpec((heads,) + tiles.shape[1:], lambda g: (g, 0, 0, 0)),
            whole((length, 1)),
            whole((1, length)),
            whole((length, 1)),
            whole((1, length)),
        ],
        out_specs=[
            col,
            pl.BlockSpec((heads, length, length), lambda g: (g, 0, 0)),
            pl.BlockSpec((1, heads, length), lambda g: (g, 0, 0)),
        ],
        out_shape=[
            jax.ShapeDtypeStruct(queries.shape, BF16),
            jax.ShapeDtypeStruct((model // size, length, length), BF16),
            jax.ShapeDtypeStruct((model // width, heads, length), F32),
        ],
        scratch_shapes=[pltpu.VMEM((length, length), F32), pltpu.VMEM((heads, length, length), F32)],
        compiler_params=pltpu.CompilerParams(vmem_limit_bytes=48 << 20),
        cost_estimate=lasting(11),
        name="attend",
    )(queries, keys, values, tiles, seg[:, None], seg[None, :], place[:, None], place[None, :])


def attend_back_kernel(q_ref, k_ref, v_ref, mix_ref, dmix_ref, e_ref, inv_ref, *refs, size, scale):
    prior, (dq_ref, dk_ref, dv_ref, gt_ref, sum_ref) = refs[:-5], refs[-5:]
    length, width = q_ref.shape
    blocks = length // LANES
    owner = lax.broadcasted_iota(jnp.int32, (1, width), 1) // size
    row = lax.broadcasted_iota(jnp.int32, (LANES, LANES), 0)
    col = lax.broadcasted_iota(jnp.int32, (LANES, LANES), 1)
    sub = lax.broadcasted_iota(jnp.int32, (8, LANES), 0)
    keys = k_ref[...].astype(F32).T.astype(BF16)
    values = v_ref[...]
    mixed = mix_ref[...].astype(F32).T
    d_mixed = dmix_ref[...].astype(F32).T
    dq = []
    dk = jnp.zeros((length, width), F32)
    dv = jnp.zeros((length, width), F32)
    for h in range(width // size):
        own = slice(h * size, (h + 1) * size)
        scaled = (d_mixed[own] * inv_ref[0, h : h + 1, :]).astype(BF16)
        inner = jnp.sum(scaled.astype(F32) * mixed[own], 0, keepdims=True)
        zeros = [jnp.zeros((h * size, length), BF16), jnp.zeros((width - (h + 1) * size, length), BF16)]
        scaled = jnp.concatenate([z for z in (zeros[0], scaled, zeros[1]) if z.shape[0]], 0)
        e = e_ref[h]
        ds = e.astype(F32) * (dot(values, scaled) - inner)
        low = ds.astype(BF16)
        dq.append(dot(keys[own], low) * scale)
        dk = dk + dot(low, jnp.where(owner == h, q_ref[...], jnp.zeros((), BF16)))
        dv = dv + dot_nt(e, scaled)
        diag = [None] * (2 * blocks + 1)
        for j in range(blocks):
            for i in range(blocks):
                part = ds[j * LANES : (j + 1) * LANES, i * LANES : (i + 1) * LANES]
                b = i - j + blocks
                diag[b] = part if diag[b] is None else diag[b] + part
        none = jnp.zeros((LANES, LANES), F32)
        diag[0] = none
        diag[2 * blocks] = none
        for b in range(2 * blocks):
            part = jnp.where(col >= row, diag[b], diag[b + 1])
            lines = part[:8]
            for r in range(8, LANES, 8):
                lines = lines + pltpu.roll(part[r : r + 8], LANES - r, 1)
            for m in (1, 2, 4):
                lines = jnp.where(sub & m != 0, pltpu.roll(lines, LANES - m, 1), lines)
            gt_ref[h, b : b + 1, :] = jnp.sum(lines, 0, keepdims=True)
    dq = jnp.concatenate(dq, 0).T.astype(BF16)
    dq_ref[...] = dq
    if prior:
        dk = dk + prior[0][...]
        dv = dv + prior[1][...]
    dv = dv.astype(dv_ref.dtype)
    dk_ref[...] = dk.astype(dk_ref.dtype)
    dv_ref[...] = dv
    sum_ref[...] = jnp.zeros_like(sum_ref)
    sum_ref[6:7, :] = jnp.sum(dq.astype(F32), 0, keepdims=True)
    if prior:
        sum_ref[7:8, :] = jnp.sum(dv.astype(F32), 0, keepdims=True)


def attend_back(queries, keys, values, mixed, d_mixed, weights, size, prior=()):
    length, model = queries.shape
    width = LANES
    heads = width // size
    blocks = length // LANES
    col = pl.BlockSpec((length, width), lambda g: (0, g))
    square = pl.BlockSpec((heads, length, length), lambda g: (g, 0, 0))
    kind = BF16 if prior else F32
    return pl.pallas_call(
        partial(attend_back_kernel, size=size, scale=size**-0.5),
        grid=(model // width,),
        in_specs=[col] * 5 + [square, pl.BlockSpec((1, heads, length), lambda g: (g, 0, 0))] + [col] * len(prior),
        out_specs=[col, col, col, pl.BlockSpec((heads, 2 * blocks, LANES), lambda g: (g, 0, 0)), pl.BlockSpec((16, width), lambda g: (0, g))],
        out_shape=[
            jax.ShapeDtypeStruct(queries.shape, BF16),
            jax.ShapeDtypeStruct(keys.shape, kind),
            jax.ShapeDtypeStruct(keys.shape, kind),
            jax.ShapeDtypeStruct((model // size, 2 * blocks, LANES), F32),
            jax.ShapeDtypeStruct((16, model), F32),
        ],
        compiler_params=pltpu.CompilerParams(vmem_limit_bytes=50 << 20),
        cost_estimate=lasting(11.5),
        name="attend_back",
    )(queries, keys, values, mixed, d_mixed, *weights, *prior)


def front_kernel(*refs, count, kinds, scale):
    parts, swap_ref, weights = refs[:count], refs[count], refs[count + 1 : count + 1 + 2 * len(kinds)]
    x_ref, outs = refs[count + 1 + 2 * len(kinds)], refs[count + 2 + 2 * len(kinds) :]

    @pl.when(pl.program_id(0) == 0)
    def _():
        x_ref[...] = dot(swap_ref[...], jnp.concatenate([p[...] for p in parts], 0)).astype(BF16)

    for i, kind in enumerate(kinds):
        out = dot(x_ref[...], weights[2 * i][...]) + weights[2 * i + 1][...]
        out = out.astype(BF16)
        outs[i][...] = out * jnp.asarray(scale, BF16) if kind else out


def front(parts, swap, weights, kinds, scale):
    length, model = swap.shape[0], parts[0].shape[1]
    width = 2 * LANES
    whole = lambda a: pl.BlockSpec(a.shape, lambda g: (0, 0))
    cols = pl.BlockSpec((length, width), lambda g: (0, g))
    operands, specs = [], []
    for w, b in weights:
        operands += [w, b]
        specs += [pl.BlockSpec((model, width), lambda g: (0, g)), pl.BlockSpec((width,), lambda g: (g,))]
    out = jax.ShapeDtypeStruct((length, model), BF16)
    return pl.pallas_call(
        partial(front_kernel, count=len(parts), kinds=kinds, scale=scale),
        grid=(model // width,),
        in_specs=[whole(p) for p in parts] + [whole(swap)] + specs,
        out_specs=[pl.BlockSpec((length, model), lambda g: (0, 0))] + [cols] * len(kinds),
        out_shape=[out] * (1 + len(kinds)),
        compiler_params=pltpu.CompilerParams(vmem_limit_bytes=40 << 20),
        cost_estimate=lasting(3),
        name="front",
    )(*parts, swap, *operands)


def back_kernel(res_ref, swap_ref, *refs):
    pairs, out_ref = refs[:-1], refs[-1]
    x = res_ref[...]
    for i in range(0, len(pairs), 2):
        x = x + dot_nt(pairs[i][...], pairs[i + 1][...])
    out_ref[...] = dot(swap_ref[...], x.astype(BF16)).astype(BF16)


def back(res, swap, *pairs):
    length, model = res.shape
    width = 2 * LANES
    cols = pl.BlockSpec((length, width), lambda g: (0, g))
    grads = pl.BlockSpec((length, model), lambda g: (0, 0))
    weights = pl.BlockSpec((width, model), lambda g: (g, 0))
    return pl.pallas_call(
        back_kernel,
        grid=(model // width,),
        in_specs=[cols, pl.BlockSpec(swap.shape, lambda g: (0, 0))] + [grads, weights] * (len(pairs) // 2),
        out_specs=cols,
        out_shape=jax.ShapeDtypeStruct((length, model), BF16),
        compiler_params=pltpu.CompilerParams(vmem_limit_bytes=50 << 20),
        cost_estimate=lasting(4.5),
        name="back",
    )(res, swap, *pairs)


def normalize(z):
    mean = jnp.mean(z, -1, keepdims=True)
    centered = z - mean
    rstd = lax.rsqrt(jnp.mean(centered * centered, -1, keepdims=True) + EPS)
    return centered * rstd, rstd


def normalize_back(cot, gain, hat, rstd):
    s = gain * cot
    return (s - jnp.mean(s, -1, keepdims=True) - hat * jnp.mean(s * hat, -1, keepdims=True)) * rstd


def gelu_pair(u):
    cdf = 0.5 + 0.5 * lax.erf(u * 0.7071067811865476)
    return u * cdf, cdf + u * (jnp.exp(u * u * -0.5) * 0.3989422804014327)


def ffn_kernel(
    x_ref, mix_ref, cot_ref, wo_ref, bo_ref, g1_ref, s1_ref, wu_ref, bu_ref, wd_ref, bd_ref, g2_ref, s2_ref, *refs,
    chunk,
):
    (
        out_ref, dres_ref, dmix_ref, hid_ref, act_ref, dred_ref, dexp_ref, dproj_ref, small_ref, slope,
    ) = refs[-10:]
    ff = wu_ref.shape[1]

    @pl.when(pl.program_id(0) == 0)
    def _():
        small_ref[...] = jnp.zeros_like(small_ref)

    def add_small(i, rows):
        small_ref[i : i + 1, :] += jnp.sum(rows, 0, keepdims=True)

    res = x_ref[...].astype(F32) + dot(mix_ref[...], wo_ref[...]) + bo_ref[...]
    hat1, rstd1 = normalize(res)
    hidden = hat1 * g1_ref[...] + s1_ref[...]
    low = hidden.astype(BF16)
    hid_ref[...] = low
    summed = hidden + bd_ref[...]
    for c in range(0, ff, chunk):
        at = slice(c, c + chunk)
        active, grad = gelu_pair(dot(low, wu_ref[:, at]) + bu_ref[at])
        active = active.astype(BF16)
        act_ref[:, at] = active
        slope[:, at] = grad
        summed = summed + dot(active, wd_ref[at, :])
    hat2, rstd2 = normalize(summed)
    out_ref[...] = (hat2 * g2_ref[...] + s2_ref[...]).astype(BF16)
    cot = cot_ref[...].astype(F32)
    d_summed = normalize_back(cot, g2_ref[...], hat2, rstd2)
    d_red = d_summed.astype(BF16)
    dred_ref[...] = d_red
    add_small(0, cot * hat2)
    add_small(1, cot)
    add_small(2, d_red.astype(F32))
    d_hidden = d_summed
    for c in range(0, ff, chunk):
        at = slice(c, c + chunk)
        d_exp = (dot_nt(d_red, wd_ref[at, :]) * slope[:, at]).astype(BF16)
        dexp_ref[:, at] = d_exp
        add_small(8 + c // chunk, d_exp.astype(F32))
        d_hidden = d_hidden + dot_nt(d_exp, wu_ref[:, at])
    d_res = normalize_back(d_hidden, g1_ref[...], hat1, rstd1)
    dres_ref[...] = d_res
    d_proj = d_res.astype(BF16)
    dproj_ref[...] = d_proj
    add_small(3, d_hidden * hat1)
    add_small(4, d_hidden)
    add_small(5, d_proj.astype(F32))
    dmix_ref[...] = dot_nt(d_proj, wo_ref[...]).astype(BF16)


def ffn(x, mixed, cot, w_out, b_out, gain_one, shift_one, w_up, b_up, w_down, b_down, gain_two, shift_two, which, filled):
    tokens, model = x.shape
    ff = w_up.shape[1]
    tile = min(256, tokens)
    chunk = model
    steps = tokens // tile
    rows = lambda n: pl.BlockSpec((tile, n), lambda i: (i, 0))
    half = lambda n: pl.BlockSpec((tile, n), lambda i: (i + which * steps, 0))
    whole = lambda shape: pl.BlockSpec(shape, lambda i: (0,) * len(shape))
    args = (
        x, mixed, cot, w_out, b_out, gain_one, shift_one, w_up, b_up, w_down, b_down, gain_two, shift_two,
    )
    own = lambda n, kind: jax.ShapeDtypeStruct((tokens, n), kind)
    shared = lambda n: jax.ShapeDtypeStruct((2 * tokens, n), BF16)
    return pl.pallas_call(
        partial(ffn_kernel, chunk=chunk),
        grid=(steps,),
        in_specs=[rows(model)] * 3
        + [pl.BlockSpec(memory_space=pltpu.VMEM) if a.ndim == 2 else whole(a.shape) for a in args[3:]]
        + [pl.BlockSpec(memory_space=pl.ANY)] * len(filled),
        out_specs=[
            rows(model), rows(model), rows(model), half(model), half(ff), half(model), half(ff), half(model),
            whole((16, model)),
        ],
        out_shape=[
            own(model, BF16), own(model, F32), own(model, BF16), shared(model), shared(ff), shared(model), shared(ff),
            shared(model), jax.ShapeDtypeStruct((16, model), F32),
        ],
        scratch_shapes=[pltpu.VMEM((tile, ff), F32)],
        input_output_aliases={len(args) + i: 3 + i for i in range(len(filled))},
        compiler_params=pltpu.CompilerParams(vmem_limit_bytes=48 << 20),
        cost_estimate=lasting(21),
        name="ffn",
    )(*args, *filled)


def partner(x, axis, mask):
    return lax.ppermute(x, axis, [(i, i ^ mask) for i in range(lax.axis_size(axis))])


def pick(x, i):
    return lax.dynamic_index_in_dim(x, i, 0, keepdims=False)


def index_bits(n):
    return [1 << b for b in reversed(range(bits(n)))]


def row_parts(x, me):
    return [pick(x, me ^ m) for m in range(x.shape[0])]


def exchange(parts):
    return [parts[0]] + [partner(parts[m], "seq", m) for m in range(1, len(parts))]


def arrange(parts, me):
    count = len(parts)
    rows = []
    for r in range(count):
        row = parts[r]
        for m in range(1, count):
            row = jnp.where(me == m, parts[r ^ m], row)
        rows.append(row)
    return jnp.stack(rows)


def hold(x, *after):
    return lax.optimization_barrier((x, after))[0]


def bits(n):
    return n.bit_length() - 1


def device_bits():
    dp, seq = lax.axis_size("dp"), lax.axis_size("seq")
    return [("dp", b) for b in reversed(range(bits(dp)))] + [("seq", b) for b in reversed(range(bits(seq)))]


def full_order(order):
    known = device_bits()
    return [n for n in order if n in known] + [n for n in known if n not in order]


def relative_places(order):
    seq = lax.axis_size("seq")
    count = lax.axis_size("dp") * seq
    me = lax.axis_index("dp") * seq + lax.axis_index("seq")
    apart = jnp.arange(count, dtype=jnp.int32) ^ me
    place = jnp.zeros_like(apart)
    for axis, bit in order:
        place = place * 2 + ((apart >> (bit + (bits(seq) if axis == "dp" else 0))) & 1)
    return place


def fold_kernel(keep_ref, got_ref, *out_refs, cuts, bits_at):
    both = (keep_ref[...].astype(F32) + got_ref[...].astype(F32)).astype(BF16)
    for i, at in enumerate(bits_at):
        part = both[:, cuts[i] : cuts[i + 1]]
        part = part.reshape((2**at, 2, -1) + part.shape[1:])
        for j in range(2):
            out_refs[2 * i + j][...] = part[:, j].reshape(out_refs[2 * i + j].shape)


def fold(keep, got, cuts, bits_at):
    places, rows, columns = keep.shape
    if any(c % 16 for c in cuts) or places < 4:
        pairs = []
        for i, at in enumerate(bits_at):
            at_rows = slice(cuts[i], cuts[i + 1])
            both = (keep[:, at_rows].astype(F32) + got[:, at_rows].astype(F32)).astype(BF16)
            both = both.reshape((2**at, 2, -1) + both.shape[1:])
            pairs.append([both[:, j].reshape(-1, *both.shape[3:]) for j in range(2)])
        return pairs
    whole = lambda shape: pl.BlockSpec(shape, lambda g: (0, 0, 0))
    shapes = [(places // 2, cuts[i + 1] - cuts[i], columns) for i in range(len(bits_at)) for j in range(2)]
    folded = pl.pallas_call(
        partial(fold_kernel, cuts=cuts, bits_at=bits_at),
        grid=(1,),
        in_specs=[whole(keep.shape)] * 2,
        out_specs=[whole(shape) for shape in shapes],
        out_shape=[jax.ShapeDtypeStruct(shape, BF16) for shape in shapes],
        compiler_params=pltpu.CompilerParams(vmem_limit_bytes=FOLD_VMEM << 20),
        cost_estimate=lasting(1.5),
        name="fold",
    )(keep, got)
    return [folded[2 * i : 2 * i + 2] for i in range(len(bits_at))]


class Share:
    def __init__(self, keep, send, left, todo=None):
        self.left, self.todo = list(left), list(todo or left)
        self.keep, self.send = keep, send

    def arrive(self, after):
        axis, bit = self.todo.pop(0)
        self.left.remove((axis, bit))
        return hold(partner(self.send, axis, 1 << bit), after)

    def step(self, after):
        got = self.arrive(after)
        if self.todo:
            cuts = [0, self.keep.shape[1]]
            ((self.keep, self.send),) = fold(self.keep, got, cuts, [self.left.index(self.todo[0])])
            return self.send
        self.keep = (self.keep.astype(F32) + got.astype(F32))[0]
        return self.keep

    def finish(self, token):
        while self.todo:
            token = self.step(token)
        return token

    def split(self, cuts, orders, after):
        got = self.arrive(after)
        todos = [[n for n in order if n in self.left] + [n for n in self.left if n not in order] for order in orders]
        pairs = fold(self.keep, got, cuts, [self.left.index(todo[0]) for todo in todos])
        return [Share(*pair, self.left, todo) for pair, todo in zip(pairs, todos)]

    def merged(self, other, after):
        mine, theirs = self.arrive(after), other.arrive(after)
        both = [
            (share.keep.astype(F32) + got.astype(F32)).astype(BF16) for share, got in ((self, mine), (other, theirs))
        ]
        both = jnp.concatenate(both, 1)
        both = both.reshape((2 ** self.left.index(self.todo[0]), 2, -1) + both.shape[1:])
        return Share(*[both[:, j].reshape(-1, *both.shape[3:]) for j in range(2)], self.left, self.todo)


class Return:
    def __init__(self, blocks):
        self.todo = [1 << b for b in reversed(range(bits(len(blocks))))]
        self.rows = {0: dict(enumerate(blocks))}
        self.pack()

    def pack(self):
        m = self.todo[0]
        self.gone = [(r, i) for r in self.rows for i in self.rows[r] if i & m]
        self.send = jnp.concatenate([self.rows[r][i] for r, i in self.gone], 0)

    def step(self, after):
        m = self.todo.pop(0)
        got = hold(partner(self.send, "seq", m), after)
        size = got.shape[0] // len(self.gone)
        rows = {r: {i: b for i, b in row.items() if not i & m} for r, row in self.rows.items()}
        for n, (r, i) in enumerate(self.gone):
            rows.setdefault(r ^ m, {})[i ^ m] = got[n * size : (n + 1) * size]
        self.rows = rows
        if self.todo:
            self.pack()
            return self.send
        return [rows[r][0] for r in sorted(rows)]


def fold_columns(g):
    half = g.shape[1] // 2
    return jnp.concatenate([g[:, :half], g[:, half:]], 0)


def unfold_columns(g):
    half = g.shape[0] // 2
    return jnp.concatenate([g[:half], g[half:]], 1)


def store_part(place_ref, device, piece, keep_ref, send_ref):
    place = place_ref[device]
    half = keep_ref.shape[0]

    @pl.when(place < half)
    def _():
        keep_ref[place] = piece

    @pl.when(place >= half)
    def _():
        send_ref[place - half] = piece


def split_by_place(place, parts):
    ordered = jnp.zeros_like(parts).at[place].set(parts)
    half = parts.shape[0] // 2
    return ordered[:half], ordered[half:]


def folded_parts(g, count):
    parts = g.astype(BF16).reshape(count, g.shape[0] // count, 2, -1)
    return jnp.swapaxes(parts, 1, 2).reshape(count, -1, parts.shape[-1])


def tall_kernel(place_ref, a_ref, b_ref, keep_ref, send_ref):
    rows = keep_ref.shape[1]
    g = dot_tn(a_ref[...], b_ref[...]).astype(BF16)
    here = g.shape[0] // rows
    for k in range(here):
        store_part(place_ref, pl.program_id(0) * here + k, g[k * rows : (k + 1) * rows], keep_ref, send_ref)


def tall_grad(place, a, b):
    count = place.shape[0]
    tokens, high = a.shape
    wide = b.shape[1]
    if high // count % 16:
        return split_by_place(place, dot_tn(a, b).astype(BF16).reshape(count, -1, wide))
    steps = high // wide
    shape = (count // 2, high // count, wide)
    whole = pl.BlockSpec(shape, lambda g, p: (0, 0, 0))
    return pl.pallas_call(
        tall_kernel,
        grid_spec=pltpu.PrefetchScalarGridSpec(
            num_scalar_prefetch=1,
            grid=(steps,),
            in_specs=[
                pl.BlockSpec((tokens, wide), lambda g, p: (0, g)),
                pl.BlockSpec((tokens, wide), lambda g, p: (0, 0)),
            ],
            out_specs=[whole, whole],
        ),
        out_shape=[jax.ShapeDtypeStruct(shape, BF16)] * 2,
        compiler_params=pltpu.CompilerParams(vmem_limit_bytes=40 << 20),
        cost_estimate=lasting(9),
        name="tall_grad",
    )(place, a, b)


def store_all(place_ref, g, keep_ref, send_ref):
    count = 2 * keep_ref.shape[0]
    rows = g.shape[0] // count
    for k in range(count):
        store_part(
            place_ref, k, fold_columns(g[k * rows : (k + 1) * rows]).astype(BF16), keep_ref, send_ref
        )


def wide_kernel(place_ref, hid_ref, exp_ref, mix_ref, proj_ref, keep_ref, send_ref):
    last = pl.num_programs(0) - 1

    @pl.when(pl.program_id(0) < last)
    def _():
        store_all(place_ref, dot_tn(hid_ref[...], exp_ref[...]), keep_ref, send_ref)

    @pl.when(pl.program_id(0) == last)
    def _():
        store_all(place_ref, dot_tn(mix_ref[...], proj_ref[...]), keep_ref, send_ref)


def wide_grad(place, hidden, d_exp, mixed, d_proj):
    count = place.shape[0]
    tokens, model = hidden.shape
    steps = d_exp.shape[1] // model
    rows = 2 * model // count
    if rows % 16:
        pieces = [dot_tn(hidden, d_exp[:, i * model : (i + 1) * model]) for i in range(steps)] + [dot_tn(mixed, d_proj)]
        return split_by_place(place, jnp.concatenate([folded_parts(g, count) for g in pieces], 1))
    shape = (count // 2, (steps + 1) * rows, model // 2)
    square = pl.BlockSpec((tokens, model), lambda g, p: (0, 0))
    out = pl.BlockSpec((count // 2, rows, model // 2), lambda g, p: (0, g, 0))
    return pl.pallas_call(
        wide_kernel,
        grid_spec=pltpu.PrefetchScalarGridSpec(
            num_scalar_prefetch=1,
            grid=(steps + 1,),
            in_specs=[
                square,
                pl.BlockSpec((tokens, model), lambda g, p: (0, jnp.minimum(g, steps - 1))),
                square,
                square,
            ],
            out_specs=[out, out],
        ),
        out_shape=[jax.ShapeDtypeStruct(shape, BF16)] * 2,
        compiler_params=pltpu.CompilerParams(vmem_limit_bytes=40 << 20),
        cost_estimate=lasting(13),
        name="wide_grad",
    )(place, hidden, d_exp, mixed, d_proj)


def last_kernel(place_ref, xc_ref, xq_ref, qc_ref, qq_ref, k_ref, v_ref, keep_ref, send_ref):
    step = pl.program_id(0)

    @pl.when(step == 0)
    def _():
        g = dot_tn(xc_ref[...], qc_ref[...]) + dot_tn(xq_ref[...], qq_ref[...])
        store_all(place_ref, g, keep_ref, send_ref)

    @pl.when(step == 1)
    def _():
        store_all(place_ref, dot_tn(xc_ref[...], k_ref[...]), keep_ref, send_ref)

    @pl.when(step == 2)
    def _():
        store_all(place_ref, dot_tn(xc_ref[...], v_ref[...]), keep_ref, send_ref)


def last_grad(place, x_c, x_q, dq_c, dq_q, d_keys, d_values):
    count = place.shape[0]
    tokens, model = x_c.shape
    rows = 2 * model // count
    if rows % 16:
        pieces = [dot_tn(x_c, dq_c) + dot_tn(x_q, dq_q), dot_tn(x_c, d_keys), dot_tn(x_c, d_values)]
        return split_by_place(place, jnp.concatenate([folded_parts(g, count) for g in pieces], 1))
    shape = (count // 2, 3 * rows, model // 2)
    square = pl.BlockSpec((tokens, model), lambda g, p: (0, 0))
    out = pl.BlockSpec((count // 2, rows, model // 2), lambda g, p: (0, g, 0))
    return pl.pallas_call(
        last_kernel,
        grid_spec=pltpu.PrefetchScalarGridSpec(
            num_scalar_prefetch=1, grid=(3,), in_specs=[square] * 6, out_specs=[out, out]
        ),
        out_shape=[jax.ShapeDtypeStruct(shape, BF16)] * 2,
        compiler_params=pltpu.CompilerParams(vmem_limit_bytes=40 << 20),
        cost_estimate=lasting(6),
        name="last_grad",
    )(place, x_c, x_q, dq_c, dq_q, d_keys, d_values)


def all_steps():
    return [(axis, b) for axis in ("seq", "dp") for b in range(bits(lax.axis_size(axis)))]


def local(
    content, query, order, lengths, predicted, distance_bucket, w_query, b_query, w_key, w_value, b_value, w_out, b_out,
    gain_one, shift_one, w_up, b_up, w_down, b_down, gain_two, shift_two, bias_table, d_content, d_query,
):
    count = lax.axis_size("seq")
    me = lax.axis_index("seq")
    rows, block, model = content.shape
    length = order.shape[1]
    buckets, heads = bias_table.shape
    size = model // heads
    ff = w_up.shape[1]
    picked = predicted[:, :, None] == 1

    got_content = exchange(row_parts(content, me))

    own_order = pick(order, me)
    there = [(me ^ m) * block for m in range(count)]
    order_cat = jnp.concatenate([lax.dynamic_slice_in_dim(own_order, t, block, 0) for t in there])
    place_cat = jnp.concatenate([t + jnp.arange(block, dtype=jnp.int32) for t in there])
    initial = jnp.arange(length, dtype=jnp.int32)
    at_place = order_cat[None, :] == initial[:, None]
    swap = at_place.astype(BF16)
    place = jnp.sum(jnp.where(at_place, place_cat[None, :], 0), 1)
    ends = jnp.cumsum(pick(lengths, me), dtype=jnp.int32)
    seg = jnp.sum((ends[None, :] <= initial[:, None]).astype(jnp.int32), 1)

    blocks = length // LANES
    by_distance = jnp.pad(distance_bucket, (1, 0), constant_values=-1)
    onehot = (by_distance[:, None] == jnp.arange(buckets, dtype=jnp.int32)[None, :]).astype(F32)
    table = jnp.einsum("db,bh->hd", onehot, bias_table, precision=lax.Precision.HIGHEST)
    tiles = bias_tiles((table * LOG2_E).reshape(heads, 2 * blocks, LANES))

    swap_back = (order_cat[:, None] == initial[None, :]).astype(BF16)
    scale = size**-0.5

    def in_order(parts):
        return dot(swap, jnp.concatenate(parts, 0)).astype(BF16)

    def blocks_of(x):
        return [x[i * block : (i + 1) * block] for i in range(count)]

    params = (w_out, b_out, gain_one, shift_one, w_up, b_up, w_down, b_down, gain_two, shift_two)
    core, y, x, z, far = ("seq", 0), ("seq", 1), ("dp", 0), ("dp", 1), ("dp", 2)
    steps_one = full_order([core, z, x, y, far])
    steps_two = full_order([core, x, y, z, far])
    steps_three = full_order([core, x, y, z, far])
    places = [relative_places(o) for o in (steps_one, steps_two, steps_three)]

    x_c, q_c, keys, values = front(
        hold(got_content, tiles, seg, place),
        swap,
        [(w_query, b_query), (w_key, jnp.zeros((model,), F32)), (w_value, b_value)],
        (True, False, False),
        scale,
    )
    query_parts = row_parts(hold(query, got_content), me)
    got_query = exchange(query_parts)
    mixed_c, *weights_c = attend(hold(q_c, query_parts), keys, values, tiles, seg, place, size)
    x_q, q_q = front(hold(got_query, mixed_c), swap, [(w_query, b_query)], (True,), scale)
    d_content_parts = row_parts(hold(d_content, got_query, mixed_c), me)
    got_d_content = exchange(d_content_parts)
    mixed_q, *weights_q = attend(hold(q_q, d_content_parts), keys, values, tiles, seg, place, size)
    cot_c = in_order(hold(got_d_content, mixed_q))
    d_query_parts = row_parts(jnp.where(picked, hold(d_query, got_d_content, mixed_q), jnp.zeros((), BF16)), me)
    got_d_query = exchange(d_query_parts)
    normed_c, res_c, dmix_c, *filled, small_c = ffn(x_c, mixed_c, hold(cot_c, d_query_parts), *params, 0, ())
    filled = filled[:5]
    own_c = hold(blocks_of(dot(swap_back, normed_c).astype(BF16)), got_d_query)
    sent_c = exchange(own_c)
    cot_q = in_order(hold(got_d_query, own_c))
    normed_q, res_q, dmix_q, hidden, active, d_red, d_exp, d_proj, small_q = ffn(
        x_q, mixed_q, hold(cot_q, own_c), *params, 1, filled
    )
    own_q = Return(blocks_of(dot(swap_back, hold(normed_q, sent_c)).astype(BF16)))
    content_out = arrange(hold(sent_c, normed_q), me)
    mixed = jnp.concatenate([mixed_c, mixed_q], 0)
    down = Share(*tall_grad(places[0], hold(active, content_out, own_q.send), d_red), steps_one)
    up = Share(*wide_grad(places[1], hold(hidden, down.send), d_exp, mixed, d_proj), steps_two)
    token = down.step(up.send)
    dq_q, dk, dv, circ_q, sums_q = attend_back(q_q, keys, values, mixed_q, hold(dmix_q, token), weights_q, size)
    third = 2 * model // (count * lax.axis_size("dp"))
    token = own_q.step(dq_q)
    up_one, up_two = up.split([0, 3 * third, 5 * third], [[x, y, z, far], [y, x, z, far]], token)
    back_q = Return(blocks_of(back(res_q, swap_back, hold(dq_q, up_one.send, up_two.send), w_query)))
    sent_q = own_q.step(back_q.send)
    query_out = jnp.where(picked, arrange(sent_q, me), query)
    token = down.step(query_out)
    dq_c, d_keys, d_values, circ_c, sums_c = attend_back(
        q_c, keys, values, mixed_c, hold(dmix_c, token), weights_c, size, (dk, dv)
    )
    token = up_one.step(dq_c)
    token = up_two.step(token)
    late = Share(*last_grad(places[2], hold(x_c, token), x_q, dq_c, dq_q, d_keys, d_values), steps_three)
    token = back_q.step(late.send)
    token = down.step(token)
    back_c = back(res_c, swap_back, hold(dq_c, token), w_query, d_keys, w_key, d_values, w_value)
    up = up_one.merged(up_two, back_c)
    back_c = Return(blocks_of(hold(back_c, up.send)))
    first, second = late.split([0, third, 3 * third], [[z, y, x, far], [x, y, z, far]], back_c.send)
    g_table = jnp.einsum(
        "hd,db->hb", hold(circ_c, back_c.send).reshape(heads, -1) + circ_q.reshape(heads, -1), onehot,
        precision=lax.Precision.HIGHEST,
    )
    packed = jnp.concatenate(
        [
            hold(small_c, back_c.send) + small_q + sums_c + sums_q,
            jnp.pad(g_table, ((0, 16 - heads), (0, LANES - buckets))),
        ],
        1,
    )
    exchanges = all_steps()

    def sum_step(packed, after):
        if not exchanges:
            return packed
        axis, bit = exchanges.pop(0)
        return packed + hold(partner(packed, axis, 1 << bit), after)

    sent_back_q = back_q.step(second.send)
    d_query_in = arrange(sent_back_q, me).astype(F32) + jnp.where(picked, 0.0, d_query.astype(F32))
    packed = sum_step(packed, d_query_in)
    token = first.step(packed)
    token = down.finish(token)
    packed = sum_step(packed, token)
    token = up.step(packed)
    token = back_c.step(token)
    packed = sum_step(packed, token)
    token = first.step(packed)
    token = second.step(token)
    token = up.finish(token)
    sent_c = back_c.step(token)
    d_content_in = arrange(sent_c, me).astype(F32)
    packed = sum_step(packed, d_content_in)
    token = second.step(packed)
    packed = sum_step(packed, token)
    late = first.merged(second, packed)
    while exchanges:
        packed = sum_step(packed, late.send)
    late.finish(late.send)
    up_out, key_value = up.keep, late.keep

    def flat(*parts):
        return jnp.concatenate([unfold_columns(p) for p in parts], 1).reshape(-1)

    vec = [packed[i, :model] for i in range(8)]
    g_b_up = packed[8 : 8 + ff // model, :model].reshape(-1)
    g_bias_table = packed[:heads, model : model + buckets].T
    return (
        content_out, query_out, d_content_in, d_query_in,
        flat(key_value[:third]), flat(key_value[third : 2 * third]), flat(key_value[2 * third :]),
        flat(up_out[-third:]), flat(*(up_out[i : i + third] for i in range(0, ff // model * third, third))),
        down.keep.reshape(-1),
        vec[6], vec[7], vec[5], vec[3], vec[4], g_b_up, vec[2], vec[0], vec[1], g_bias_table,
    )


def solution(mesh):
    tokens = P("dp", "seq", None)
    split = P(("dp", "seq"))
    in_specs = (tokens, tokens, P("dp", None), P("dp", None), P("dp", "seq")) + (P(),) * 17 + (tokens, tokens)
    out_specs = (tokens,) * 4 + (split,) * 6 + (P(),) * 10
    return jax.shard_map(local, mesh=mesh, in_specs=in_specs, out_specs=out_specs, check_vma=False)
```

```python
from functools import partial

import jax
import jax.numpy as jnp
from jax import lax
from jax.experimental import pallas as pl
from jax.experimental.pallas import tpu as pltpu
from jax.sharding import PartitionSpec as P

F32 = jnp.float32
BF16 = jnp.bfloat16
LANES = 128
EPS = 1e-5
LOG2_E = 1.4426950408889634
FOLD_VMEM = 24


def lasting(us):
    return pl.CostEstimate(flops=int(us * SHARE * 1.1e9), bytes_accessed=int(us * SHARE * 3.5e6), transcendentals=0)


SHARE = 1.0


def dot(a, b):
    return jnp.dot(a, b, preferred_element_type=F32)


def dot_nt(a, b):
    return lax.dot_general(a, b, (((1,), (1,)), ((), ())), preferred_element_type=F32)


def dot_tn(a, b):
    return lax.dot_general(a, b, (((0,), (0,)), ((), ())), preferred_element_type=F32)


def tiles_kernel(t_ref, tiles_ref):
    blocks = t_ref.shape[1] // 2
    row = lax.broadcasted_iota(jnp.int32, (LANES, LANES), 0)
    col = lax.broadcasted_iota(jnp.int32, (LANES, LANES), 1)
    for h in range(t_ref.shape[0]):
        circ = [
            pltpu.roll(jnp.broadcast_to(t_ref[h, b : b + 1, :], (LANES, LANES)), 0, 1, stride=1, stride_axis=0)
            for b in range(2 * blocks)
        ]
        for b in range(2 * blocks - 1):
            tiles_ref[h, b] = jnp.where(col >= row, circ[b + 1], circ[b])


def bias_tiles(table):
    heads, many, _ = table.shape
    step = 2
    return pl.pallas_call(
        tiles_kernel,
        grid=(heads // step,),
        in_specs=[pl.BlockSpec((step, many, LANES), lambda g: (g, 0, 0))],
        out_specs=pl.BlockSpec((step, many - 1, LANES, LANES), lambda g: (g, 0, 0, 0)),
        out_shape=jax.ShapeDtypeStruct((heads, many - 1, LANES, LANES), F32),
        compiler_params=pltpu.CompilerParams(vmem_limit_bytes=24 << 20),
        cost_estimate=lasting(2),
        name="bias_tiles",
    )(table)


def attend_kernel(
    q_ref, k_ref, v_ref, tiles_ref, segc_ref, segr_ref, plc_ref, plr_ref, mix_ref, e_ref, inv_ref, mask, line, *, size
):
    length, width = q_ref.shape
    blocks = length // LANES

    @pl.when(pl.program_id(0) == 0)
    def _():
        allowed = (segc_ref[...] == segr_ref[...]) & (plc_ref[...] <= plr_ref[...])
        mask[...] = jnp.where(allowed, 0.0, -1e30)

    owner = lax.broadcasted_iota(jnp.int32, (1, width), 1) // size
    scaled = q_ref[...].astype(F32) * LOG2_E
    high = scaled.astype(BF16).astype(F32)
    low = pltpu.roll(scaled - high, size, 1)
    keys = k_ref[...].astype(F32)
    turned = pltpu.roll(keys, size, 1)
    values = v_ref[...].astype(F32).T.astype(BF16)
    ones = jnp.ones((16, length), BF16)
    mixed = []
    for h in range(width // size):
        scores = dot_nt(
            jnp.where(owner == h, keys, turned).astype(BF16), jnp.where(owner == h, high, low).astype(BF16)
        )
        top = None
        for j in range(blocks):
            at = slice(j * LANES, (j + 1) * LANES)
            bias = jnp.concatenate([tiles_ref[h, i - j + blocks - 1] for i in range(blocks)], 1)
            part = scores[at] + bias + mask[at]
            line[h, at] = part
            part = jnp.max(part.reshape(LANES // 8, 8, length), 0)
            top = part if top is None else jnp.maximum(top, part)
        e = jnp.exp2(line[h] - jnp.max(top, 0, keepdims=True)).astype(BF16)
        e_ref[h] = e
        o = dot(jnp.concatenate([values[h * size : (h + 1) * size], ones], 0), e)
        inv = 1.0 / o[size : size + 1]
        mixed.append(o[:size] * inv)
        inv_ref[0, h : h + 1, :] = inv
    mix_ref[...] = jnp.concatenate(mixed, 0).T.astype(BF16)


def attend(queries, keys, values, tiles, seg, place, size):
    length, model = queries.shape
    width = LANES
    heads = width // size
    col = pl.BlockSpec((length, width), lambda g: (0, g))
    whole = lambda shape: pl.BlockSpec(shape, lambda g: (0, 0))
    return pl.pallas_call(
        partial(attend_kernel, size=size),
        grid=(model // width,),
        in_specs=[
            col,
            col,
            col,
            pl.BlockSpec((heads,) + tiles.shape[1:], lambda g: (g, 0, 0, 0)),
            whole((length, 1)),
            whole((1, length)),
            whole((length, 1)),
            whole((1, length)),
        ],
        out_specs=[
            col,
            pl.BlockSpec((heads, length, length), lambda g: (g, 0, 0)),
            pl.BlockSpec((1, heads, length), lambda g: (g, 0, 0)),
        ],
        out_shape=[
            jax.ShapeDtypeStruct(queries.shape, BF16),
            jax.ShapeDtypeStruct((model // size, length, length), BF16),
            jax.ShapeDtypeStruct((model // width, heads, length), F32),
        ],
        scratch_shapes=[pltpu.VMEM((length, length), F32), pltpu.VMEM((heads, length, length), F32)],
        compiler_params=pltpu.CompilerParams(vmem_limit_bytes=48 << 20),
        cost_estimate=lasting(11),
        name="attend",
    )(queries, keys, values, tiles, seg[:, None], seg[None, :], place[:, None], place[None, :])


def attend_back_kernel(q_ref, k_ref, v_ref, mix_ref, dmix_ref, e_ref, inv_ref, *refs, size, scale):
    prior, (dq_ref, dk_ref, dv_ref, gt_ref, sum_ref) = refs[:-5], refs[-5:]
    length, width = q_ref.shape
    blocks = length // LANES
    owner = lax.broadcasted_iota(jnp.int32, (1, width), 1) // size
    row = lax.broadcasted_iota(jnp.int32, (LANES, LANES), 0)
    col = lax.broadcasted_iota(jnp.int32, (LANES, LANES), 1)
    sub = lax.broadcasted_iota(jnp.int32, (8, LANES), 0)
    keys = k_ref[...].astype(F32).T.astype(BF16)
    values = v_ref[...]
    mixed = mix_ref[...].astype(F32).T
    d_mixed = dmix_ref[...].astype(F32).T
    dq = []
    dk = jnp.zeros((length, width), F32)
    dv = jnp.zeros((length, width), F32)
    for h in range(width // size):
        own = slice(h * size, (h + 1) * size)
        scaled = (d_mixed[own] * inv_ref[0, h : h + 1, :]).astype(BF16)
        inner = jnp.sum(scaled.astype(F32) * mixed[own], 0, keepdims=True)
        zeros = [jnp.zeros((h * size, length), BF16), jnp.zeros((width - (h + 1) * size, length), BF16)]
        scaled = jnp.concatenate([z for z in (zeros[0], scaled, zeros[1]) if z.shape[0]], 0)
        e = e_ref[h]
        ds = e.astype(F32) * (dot(values, scaled) - inner)
        low = ds.astype(BF16)
        dq.append(dot(keys[own], low) * scale)
        dk = dk + dot(low, jnp.where(owner == h, q_ref[...], jnp.zeros((), BF16)))
        dv = dv + dot_nt(e, scaled)
        diag = [None] * (2 * blocks + 1)
        for j in range(blocks):
            for i in range(blocks):
                part = ds[j * LANES : (j + 1) * LANES, i * LANES : (i + 1) * LANES]
                b = i - j + blocks
                diag[b] = part if diag[b] is None else diag[b] + part
        none = jnp.zeros((LANES, LANES), F32)
        diag[0] = none
        diag[2 * blocks] = none
        for b in range(2 * blocks):
            part = jnp.where(col >= row, diag[b], diag[b + 1])
            lines = part[:8]
            for r in range(8, LANES, 8):
                lines = lines + pltpu.roll(part[r : r + 8], LANES - r, 1)
            for m in (1, 2, 4):
                lines = jnp.where(sub & m != 0, pltpu.roll(lines, LANES - m, 1), lines)
            gt_ref[h, b : b + 1, :] = jnp.sum(lines, 0, keepdims=True)
    dq = jnp.concatenate(dq, 0).T.astype(BF16)
    dq_ref[...] = dq
    if prior:
        dk = dk + prior[0][...]
        dv = dv + prior[1][...]
    dv = dv.astype(dv_ref.dtype)
    dk_ref[...] = dk.astype(dk_ref.dtype)
    dv_ref[...] = dv
    sum_ref[...] = jnp.zeros_like(sum_ref)
    sum_ref[6:7, :] = jnp.sum(dq.astype(F32), 0, keepdims=True)
    if prior:
        sum_ref[7:8, :] = jnp.sum(dv.astype(F32), 0, keepdims=True)


def attend_back(queries, keys, values, mixed, d_mixed, weights, size, prior=()):
    length, model = queries.shape
    width = LANES
    heads = width // size
    blocks = length // LANES
    col = pl.BlockSpec((length, width), lambda g: (0, g))
    square = pl.BlockSpec((heads, length, length), lambda g: (g, 0, 0))
    kind = BF16 if prior else F32
    return pl.pallas_call(
        partial(attend_back_kernel, size=size, scale=size**-0.5),
        grid=(model // width,),
        in_specs=[col] * 5 + [square, pl.BlockSpec((1, heads, length), lambda g: (g, 0, 0))] + [col] * len(prior),
        out_specs=[col, col, col, pl.BlockSpec((heads, 2 * blocks, LANES), lambda g: (g, 0, 0)), pl.BlockSpec((16, width), lambda g: (0, g))],
        out_shape=[
            jax.ShapeDtypeStruct(queries.shape, BF16),
            jax.ShapeDtypeStruct(keys.shape, kind),
            jax.ShapeDtypeStruct(keys.shape, kind),
            jax.ShapeDtypeStruct((model // size, 2 * blocks, LANES), F32),
            jax.ShapeDtypeStruct((16, model), F32),
        ],
        compiler_params=pltpu.CompilerParams(vmem_limit_bytes=50 << 20),
        cost_estimate=lasting(11.5),
        name="attend_back",
    )(queries, keys, values, mixed, d_mixed, *weights, *prior)


def front_kernel(*refs, count, kinds, scale):
    parts, swap_ref, weights = refs[:count], refs[count], refs[count + 1 : count + 1 + 2 * len(kinds)]
    x_ref, outs = refs[count + 1 + 2 * len(kinds)], refs[count + 2 + 2 * len(kinds) :]

    @pl.when(pl.program_id(0) == 0)
    def _():
        x_ref[...] = dot(swap_ref[...], jnp.concatenate([p[...] for p in parts], 0)).astype(BF16)

    for i, kind in enumerate(kinds):
        out = dot(x_ref[...], weights[2 * i][...]) + weights[2 * i + 1][...]
        out = out.astype(BF16)
        outs[i][...] = out * jnp.asarray(scale, BF16) if kind else out


def front(parts, swap, weights, kinds, scale):
    length, model = swap.shape[0], parts[0].shape[1]
    width = 2 * LANES
    whole = lambda a: pl.BlockSpec(a.shape, lambda g: (0, 0))
    cols = pl.BlockSpec((length, width), lambda g: (0, g))
    operands, specs = [], []
    for w, b in weights:
        operands += [w, b]
        specs += [pl.BlockSpec((model, width), lambda g: (0, g)), pl.BlockSpec((width,), lambda g: (g,))]
    out = jax.ShapeDtypeStruct((length, model), BF16)
    return pl.pallas_call(
        partial(front_kernel, count=len(parts), kinds=kinds, scale=scale),
        grid=(model // width,),
        in_specs=[whole(p) for p in parts] + [whole(swap)] + specs,
        out_specs=[pl.BlockSpec((length, model), lambda g: (0, 0))] + [cols] * len(kinds),
        out_shape=[out] * (1 + len(kinds)),
        compiler_params=pltpu.CompilerParams(vmem_limit_bytes=40 << 20),
        cost_estimate=lasting(3),
        name="front",
    )(*parts, swap, *operands)


def back_kernel(res_ref, swap_ref, *refs):
    pairs, out_ref = refs[:-1], refs[-1]
    x = res_ref[...]
    for i in range(0, len(pairs), 2):
        x = x + dot_nt(pairs[i][...], pairs[i + 1][...])
    out_ref[...] = dot(swap_ref[...], x.astype(BF16)).astype(BF16)


def back(res, swap, *pairs):
    length, model = res.shape
    width = 2 * LANES
    cols = pl.BlockSpec((length, width), lambda g: (0, g))
    grads = pl.BlockSpec((length, model), lambda g: (0, 0))
    weights = pl.BlockSpec((width, model), lambda g: (g, 0))
    return pl.pallas_call(
        back_kernel,
        grid=(model // width,),
        in_specs=[cols, pl.BlockSpec(swap.shape, lambda g: (0, 0))] + [grads, weights] * (len(pairs) // 2),
        out_specs=cols,
        out_shape=jax.ShapeDtypeStruct((length, model), BF16),
        compiler_params=pltpu.CompilerParams(vmem_limit_bytes=50 << 20),
        cost_estimate=lasting(4.5),
        name="back",
    )(res, swap, *pairs)


def normalize(z):
    mean = jnp.mean(z, -1, keepdims=True)
    centered = z - mean
    rstd = lax.rsqrt(jnp.mean(centered * centered, -1, keepdims=True) + EPS)
    return centered * rstd, rstd


def normalize_back(cot, gain, hat, rstd):
    s = gain * cot
    return (s - jnp.mean(s, -1, keepdims=True) - hat * jnp.mean(s * hat, -1, keepdims=True)) * rstd


def gelu_pair(u):
    cdf = 0.5 + 0.5 * lax.erf(u * 0.7071067811865476)
    return u * cdf, cdf + u * (jnp.exp(u * u * -0.5) * 0.3989422804014327)


def ffn_kernel(
    x_ref, mix_ref, cot_ref, wo_ref, bo_ref, g1_ref, s1_ref, wu_ref, bu_ref, wd_ref, bd_ref, g2_ref, s2_ref, *refs,
    chunk,
):
    (
        out_ref, dres_ref, dmix_ref, hid_ref, act_ref, dred_ref, dexp_ref, dproj_ref, small_ref, slope,
    ) = refs[-10:]
    ff = wu_ref.shape[1]

    @pl.when(pl.program_id(0) == 0)
    def _():
        small_ref[...] = jnp.zeros_like(small_ref)

    def add_small(i, rows):
        small_ref[i : i + 1, :] += jnp.sum(rows, 0, keepdims=True)

    res = x_ref[...].astype(F32) + dot(mix_ref[...], wo_ref[...]) + bo_ref[...]
    hat1, rstd1 = normalize(res)
    hidden = hat1 * g1_ref[...] + s1_ref[...]
    low = hidden.astype(BF16)
    hid_ref[...] = low
    summed = hidden + bd_ref[...]
    for c in range(0, ff, chunk):
        at = slice(c, c + chunk)
        active, grad = gelu_pair(dot(low, wu_ref[:, at]) + bu_ref[at])
        active = active.astype(BF16)
        act_ref[:, at] = active
        slope[:, at] = grad
        summed = summed + dot(active, wd_ref[at, :])
    hat2, rstd2 = normalize(summed)
    out_ref[...] = (hat2 * g2_ref[...] + s2_ref[...]).astype(BF16)
    cot = cot_ref[...].astype(F32)
    d_summed = normalize_back(cot, g2_ref[...], hat2, rstd2)
    d_red = d_summed.astype(BF16)
    dred_ref[...] = d_red
    add_small(0, cot * hat2)
    add_small(1, cot)
    add_small(2, d_red.astype(F32))
    d_hidden = d_summed
    for c in range(0, ff, chunk):
        at = slice(c, c + chunk)
        d_exp = (dot_nt(d_red, wd_ref[at, :]) * slope[:, at]).astype(BF16)
        dexp_ref[:, at] = d_exp
        add_small(8 + c // chunk, d_exp.astype(F32))
        d_hidden = d_hidden + dot_nt(d_exp, wu_ref[:, at])
    d_res = normalize_back(d_hidden, g1_ref[...], hat1, rstd1)
    dres_ref[...] = d_res
    d_proj = d_res.astype(BF16)
    dproj_ref[...] = d_proj
    add_small(3, d_hidden * hat1)
    add_small(4, d_hidden)
    add_small(5, d_proj.astype(F32))
    dmix_ref[...] = dot_nt(d_proj, wo_ref[...]).astype(BF16)


def ffn(x, mixed, cot, w_out, b_out, gain_one, shift_one, w_up, b_up, w_down, b_down, gain_two, shift_two, which, filled):
    tokens, model = x.shape
    ff = w_up.shape[1]
    tile = min(256, tokens)
    chunk = model
    steps = tokens // tile
    rows = lambda n: pl.BlockSpec((tile, n), lambda i: (i, 0))
    half = lambda n: pl.BlockSpec((tile, n), lambda i: (i + which * steps, 0))
    whole = lambda shape: pl.BlockSpec(shape, lambda i: (0,) * len(shape))
    args = (
        x, mixed, cot, w_out, b_out, gain_one, shift_one, w_up, b_up, w_down, b_down, gain_two, shift_two,
    )
    own = lambda n, kind: jax.ShapeDtypeStruct((tokens, n), kind)
    shared = lambda n: jax.ShapeDtypeStruct((2 * tokens, n), BF16)
    return pl.pallas_call(
        partial(ffn_kernel, chunk=chunk),
        grid=(steps,),
        in_specs=[rows(model)] * 3
        + [pl.BlockSpec(memory_space=pltpu.VMEM) if a.ndim == 2 else whole(a.shape) for a in args[3:]]
        + [pl.BlockSpec(memory_space=pl.ANY)] * len(filled),
        out_specs=[
            rows(model), rows(model), rows(model), half(model), half(ff), half(model), half(ff), half(model),
            whole((16, model)),
        ],
        out_shape=[
            own(model, BF16), own(model, F32), own(model, BF16), shared(model), shared(ff), shared(model), shared(ff),
            shared(model), jax.ShapeDtypeStruct((16, model), F32),
        ],
        scratch_shapes=[pltpu.VMEM((tile, ff), F32)],
        input_output_aliases={len(args) + i: 3 + i for i in range(len(filled))},
        compiler_params=pltpu.CompilerParams(vmem_limit_bytes=48 << 20),
        cost_estimate=lasting(21),
        name="ffn",
    )(*args, *filled)


def partner(x, axis, mask):
    return lax.ppermute(x, axis, [(i, i ^ mask) for i in range(lax.axis_size(axis))])


def pick(x, i):
    return lax.dynamic_index_in_dim(x, i, 0, keepdims=False)


def index_bits(n):
    return [1 << b for b in reversed(range(bits(n)))]


def row_parts(x, me):
    return [pick(x, me ^ m) for m in range(x.shape[0])]


def exchange(parts):
    return [parts[0]] + [partner(parts[m], "seq", m) for m in range(1, len(parts))]


def arrange(parts, me):
    count = len(parts)
    rows = []
    for r in range(count):
        row = parts[r]
        for m in range(1, count):
            row = jnp.where(me == m, parts[r ^ m], row)
        rows.append(row)
    return jnp.stack(rows)


def hold(x, *after):
    return lax.optimization_barrier((x, after))[0]


def bits(n):
    return n.bit_length() - 1


def device_bits():
    dp, seq = lax.axis_size("dp"), lax.axis_size("seq")
    return [("dp", b) for b in reversed(range(bits(dp)))] + [("seq", b) for b in reversed(range(bits(seq)))]


def full_order(order):
    known = device_bits()
    return [n for n in order if n in known] + [n for n in known if n not in order]


def relative_places(order):
    seq = lax.axis_size("seq")
    count = lax.axis_size("dp") * seq
    me = lax.axis_index("dp") * seq + lax.axis_index("seq")
    apart = jnp.arange(count, dtype=jnp.int32) ^ me
    place = jnp.zeros_like(apart)
    for axis, bit in order:
        place = place * 2 + ((apart >> (bit + (bits(seq) if axis == "dp" else 0))) & 1)
    return place


def fold_kernel(keep_ref, got_ref, *out_refs, cuts, bits_at):
    both = (keep_ref[...].astype(F32) + got_ref[...].astype(F32)).astype(BF16)
    for i, at in enumerate(bits_at):
        part = both[:, cuts[i] : cuts[i + 1]]
        part = part.reshape((2**at, 2, -1) + part.shape[1:])
        for j in range(2):
            out_refs[2 * i + j][...] = part[:, j].reshape(out_refs[2 * i + j].shape)


def fold(keep, got, cuts, bits_at):
    places, rows, columns = keep.shape
    if any(c % 16 for c in cuts) or places < 4:
        pairs = []
        for i, at in enumerate(bits_at):
            at_rows = slice(cuts[i], cuts[i + 1])
            both = (keep[:, at_rows].astype(F32) + got[:, at_rows].astype(F32)).astype(BF16)
            both = both.reshape((2**at, 2, -1) + both.shape[1:])
            pairs.append([both[:, j].reshape(-1, *both.shape[3:]) for j in range(2)])
        return pairs
    whole = lambda shape: pl.BlockSpec(shape, lambda g: (0, 0, 0))
    shapes = [(places // 2, cuts[i + 1] - cuts[i], columns) for i in range(len(bits_at)) for j in range(2)]
    folded = pl.pallas_call(
        partial(fold_kernel, cuts=cuts, bits_at=bits_at),
        grid=(1,),
        in_specs=[whole(keep.shape)] * 2,
        out_specs=[whole(shape) for shape in shapes],
        out_shape=[pltpu.HBM(shape, BF16) for shape in shapes],
        compiler_params=pltpu.CompilerParams(vmem_limit_bytes=FOLD_VMEM << 20),
        cost_estimate=lasting(1.5),
        name="fold",
    )(keep, got)
    return [folded[2 * i : 2 * i + 2] for i in range(len(bits_at))]


class Share:
    def __init__(self, keep, send, left, todo=None):
        self.left, self.todo = list(left), list(todo or left)
        self.keep, self.send = keep, send

    def arrive(self, after):
        axis, bit = self.todo.pop(0)
        self.left.remove((axis, bit))
        return hold(partner(self.send, axis, 1 << bit), after)

    def step(self, after):
        got = self.arrive(after)
        if self.todo:
            cuts = [0, self.keep.shape[1]]
            ((self.keep, self.send),) = fold(self.keep, got, cuts, [self.left.index(self.todo[0])])
            return self.send
        self.keep = (self.keep.astype(F32) + got.astype(F32))[0]
        return self.keep

    def finish(self, token):
        while self.todo:
            token = self.step(token)
        return token

    def split(self, cuts, orders, after):
        got = self.arrive(after)
        todos = [[n for n in order if n in self.left] + [n for n in self.left if n not in order] for order in orders]
        pairs = fold(self.keep, got, cuts, [self.left.index(todo[0]) for todo in todos])
        return [Share(*pair, self.left, todo) for pair, todo in zip(pairs, todos)]

    def merged(self, other, after):
        mine, theirs = self.arrive(after), other.arrive(after)
        both = [
            (share.keep.astype(F32) + got.astype(F32)).astype(BF16) for share, got in ((self, mine), (other, theirs))
        ]
        both = jnp.concatenate(both, 1)
        both = both.reshape((2 ** self.left.index(self.todo[0]), 2, -1) + both.shape[1:])
        return Share(*[both[:, j].reshape(-1, *both.shape[3:]) for j in range(2)], self.left, self.todo)


class Return:
    def __init__(self, blocks):
        self.todo = [1 << b for b in reversed(range(bits(len(blocks))))]
        self.rows = {0: dict(enumerate(blocks))}
        self.pack()

    def pack(self):
        m = self.todo[0]
        self.gone = [(r, i) for r in self.rows for i in self.rows[r] if i & m]
        self.send = jnp.concatenate([self.rows[r][i] for r, i in self.gone], 0)

    def step(self, after):
        m = self.todo.pop(0)
        got = hold(partner(self.send, "seq", m), after)
        size = got.shape[0] // len(self.gone)
        rows = {r: {i: b for i, b in row.items() if not i & m} for r, row in self.rows.items()}
        for n, (r, i) in enumerate(self.gone):
            rows.setdefault(r ^ m, {})[i ^ m] = got[n * size : (n + 1) * size]
        self.rows = rows
        if self.todo:
            self.pack()
            return self.send
        return [rows[r][0] for r in sorted(rows)]


def fold_columns(g):
    half = g.shape[1] // 2
    return jnp.concatenate([g[:, :half], g[:, half:]], 0)


def unfold_columns(g):
    half = g.shape[0] // 2
    return jnp.concatenate([g[:half], g[half:]], 1)


def store_part(place_ref, device, piece, keep_ref, send_ref):
    place = place_ref[device]
    half = keep_ref.shape[0]

    @pl.when(place < half)
    def _():
        keep_ref[place] = piece

    @pl.when(place >= half)
    def _():
        send_ref[place - half] = piece


def split_by_place(place, parts):
    ordered = jnp.zeros_like(parts).at[place].set(parts)
    half = parts.shape[0] // 2
    return ordered[:half], ordered[half:]


def folded_parts(g, count):
    parts = g.astype(BF16).reshape(count, g.shape[0] // count, 2, -1)
    return jnp.swapaxes(parts, 1, 2).reshape(count, -1, parts.shape[-1])


def tall_kernel(place_ref, a_ref, b_ref, keep_ref, send_ref):
    rows = keep_ref.shape[1]
    g = dot_tn(a_ref[...], b_ref[...]).astype(BF16)
    here = g.shape[0] // rows
    for k in range(here):
        store_part(place_ref, pl.program_id(0) * here + k, g[k * rows : (k + 1) * rows], keep_ref, send_ref)


def tall_grad(place, a, b):
    count = place.shape[0]
    tokens, high = a.shape
    wide = b.shape[1]
    if high // count % 16:
        return split_by_place(place, dot_tn(a, b).astype(BF16).reshape(count, -1, wide))
    steps = high // wide
    shape = (count // 2, high // count, wide)
    whole = pl.BlockSpec(shape, lambda g, p: (0, 0, 0))
    return pl.pallas_call(
        tall_kernel,
        grid_spec=pltpu.PrefetchScalarGridSpec(
            num_scalar_prefetch=1,
            grid=(steps,),
            in_specs=[
                pl.BlockSpec((tokens, wide), lambda g, p: (0, g)),
                pl.BlockSpec((tokens, wide), lambda g, p: (0, 0)),
            ],
            out_specs=[whole, whole],
        ),
        out_shape=[pltpu.HBM(shape, BF16)] * 2,
        compiler_params=pltpu.CompilerParams(vmem_limit_bytes=40 << 20),
        cost_estimate=lasting(9),
        name="tall_grad",
    )(place, a, b)


def store_all(place_ref, g, keep_ref, send_ref):
    count = 2 * keep_ref.shape[0]
    rows = g.shape[0] // count
    for k in range(count):
        store_part(
            place_ref, k, fold_columns(g[k * rows : (k + 1) * rows]).astype(BF16), keep_ref, send_ref
        )


def wide_kernel(place_ref, hid_ref, exp_ref, mix_ref, proj_ref, keep_ref, send_ref):
    last = pl.num_programs(0) - 1

    @pl.when(pl.program_id(0) < last)
    def _():
        store_all(place_ref, dot_tn(hid_ref[...], exp_ref[...]), keep_ref, send_ref)

    @pl.when(pl.program_id(0) == last)
    def _():
        store_all(place_ref, dot_tn(mix_ref[...], proj_ref[...]), keep_ref, send_ref)


def wide_grad(place, hidden, d_exp, mixed, d_proj):
    count = place.shape[0]
    tokens, model = hidden.shape
    steps = d_exp.shape[1] // model
    rows = 2 * model // count
    if rows % 16:
        pieces = [dot_tn(hidden, d_exp[:, i * model : (i + 1) * model]) for i in range(steps)] + [dot_tn(mixed, d_proj)]
        return split_by_place(place, jnp.concatenate([folded_parts(g, count) for g in pieces], 1))
    shape = (count // 2, (steps + 1) * rows, model // 2)
    square = pl.BlockSpec((tokens, model), lambda g, p: (0, 0))
    out = pl.BlockSpec((count // 2, rows, model // 2), lambda g, p: (0, g, 0))
    return pl.pallas_call(
        wide_kernel,
        grid_spec=pltpu.PrefetchScalarGridSpec(
            num_scalar_prefetch=1,
            grid=(steps + 1,),
            in_specs=[
                square,
                pl.BlockSpec((tokens, model), lambda g, p: (0, jnp.minimum(g, steps - 1))),
                square,
                square,
            ],
            out_specs=[out, out],
        ),
        out_shape=[pltpu.HBM(shape, BF16)] * 2,
        compiler_params=pltpu.CompilerParams(vmem_limit_bytes=40 << 20),
        cost_estimate=lasting(13),
        name="wide_grad",
    )(place, hidden, d_exp, mixed, d_proj)


def last_kernel(place_ref, xc_ref, xq_ref, qc_ref, qq_ref, k_ref, v_ref, keep_ref, send_ref):
    step = pl.program_id(0)

    @pl.when(step == 0)
    def _():
        g = dot_tn(xc_ref[...], qc_ref[...]) + dot_tn(xq_ref[...], qq_ref[...])
        store_all(place_ref, g, keep_ref, send_ref)

    @pl.when(step == 1)
    def _():
        store_all(place_ref, dot_tn(xc_ref[...], k_ref[...]), keep_ref, send_ref)

    @pl.when(step == 2)
    def _():
        store_all(place_ref, dot_tn(xc_ref[...], v_ref[...]), keep_ref, send_ref)


def last_grad(place, x_c, x_q, dq_c, dq_q, d_keys, d_values):
    count = place.shape[0]
    tokens, model = x_c.shape
    rows = 2 * model // count
    if rows % 16:
        pieces = [dot_tn(x_c, dq_c) + dot_tn(x_q, dq_q), dot_tn(x_c, d_keys), dot_tn(x_c, d_values)]
        return split_by_place(place, jnp.concatenate([folded_parts(g, count) for g in pieces], 1))
    shape = (count // 2, 3 * rows, model // 2)
    square = pl.BlockSpec((tokens, model), lambda g, p: (0, 0))
    out = pl.BlockSpec((count // 2, rows, model // 2), lambda g, p: (0, g, 0))
    return pl.pallas_call(
        last_kernel,
        grid_spec=pltpu.PrefetchScalarGridSpec(
            num_scalar_prefetch=1, grid=(3,), in_specs=[square] * 6, out_specs=[out, out]
        ),
        out_shape=[pltpu.HBM(shape, BF16)] * 2,
        compiler_params=pltpu.CompilerParams(vmem_limit_bytes=40 << 20),
        cost_estimate=lasting(6),
        name="last_grad",
    )(place, x_c, x_q, dq_c, dq_q, d_keys, d_values)


def all_steps():
    return [(axis, b) for axis in ("seq", "dp") for b in range(bits(lax.axis_size(axis)))]


def local(
    content, query, order, lengths, predicted, distance_bucket, w_query, b_query, w_key, w_value, b_value, w_out, b_out,
    gain_one, shift_one, w_up, b_up, w_down, b_down, gain_two, shift_two, bias_table, d_content, d_query,
):
    count = lax.axis_size("seq")
    me = lax.axis_index("seq")
    rows, block, model = content.shape
    length = order.shape[1]
    buckets, heads = bias_table.shape
    size = model // heads
    ff = w_up.shape[1]
    picked = predicted[:, :, None] == 1

    got_content = exchange(row_parts(content, me))

    own_order = pick(order, me)
    there = [(me ^ m) * block for m in range(count)]
    order_cat = jnp.concatenate([lax.dynamic_slice_in_dim(own_order, t, block, 0) for t in there])
    place_cat = jnp.concatenate([t + jnp.arange(block, dtype=jnp.int32) for t in there])
    initial = jnp.arange(length, dtype=jnp.int32)
    at_place = order_cat[None, :] == initial[:, None]
    swap = at_place.astype(BF16)
    place = jnp.sum(jnp.where(at_place, place_cat[None, :], 0), 1)
    ends = jnp.cumsum(pick(lengths, me), dtype=jnp.int32)
    seg = jnp.sum((ends[None, :] <= initial[:, None]).astype(jnp.int32), 1)

    blocks = length // LANES
    by_distance = jnp.pad(distance_bucket, (1, 0), constant_values=-1)
    onehot = (by_distance[:, None] == jnp.arange(buckets, dtype=jnp.int32)[None, :]).astype(F32)
    table = jnp.einsum("db,bh->hd", onehot, bias_table, precision=lax.Precision.HIGHEST)
    tiles = bias_tiles((table * LOG2_E).reshape(heads, 2 * blocks, LANES))

    swap_back = (order_cat[:, None] == initial[None, :]).astype(BF16)
    scale = size**-0.5

    def in_order(parts):
        return dot(swap, jnp.concatenate(parts, 0)).astype(BF16)

    def blocks_of(x):
        return [x[i * block : (i + 1) * block] for i in range(count)]

    params = (w_out, b_out, gain_one, shift_one, w_up, b_up, w_down, b_down, gain_two, shift_two)
    core, y, x, z, far = ("seq", 0), ("seq", 1), ("dp", 0), ("dp", 1), ("dp", 2)
    steps_one = full_order([core, z, x, y, far])
    steps_two = full_order([core, x, y, z, far])
    steps_three = full_order([core, x, y, z, far])
    places = [relative_places(o) for o in (steps_one, steps_two, steps_three)]

    x_c, q_c, keys, values = front(
        hold(got_content, tiles, seg, place),
        swap,
        [(w_query, b_query), (w_key, jnp.zeros((model,), F32)), (w_value, b_value)],
        (True, False, False),
        scale,
    )
    query_parts = row_parts(hold(query, got_content), me)
    got_query = exchange(query_parts)
    mixed_c, *weights_c = attend(hold(q_c, query_parts), keys, values, tiles, seg, place, size)
    x_q, q_q = front(hold(got_query, mixed_c), swap, [(w_query, b_query)], (True,), scale)
    d_content_parts = row_parts(hold(d_content, got_query, mixed_c), me)
    got_d_content = exchange(d_content_parts)
    mixed_q, *weights_q = attend(hold(q_q, d_content_parts), keys, values, tiles, seg, place, size)
    cot_c = in_order(hold(got_d_content, mixed_q))
    d_query_parts = row_parts(jnp.where(picked, hold(d_query, got_d_content, mixed_q), jnp.zeros((), BF16)), me)
    got_d_query = exchange(d_query_parts)
    normed_c, res_c, dmix_c, *filled, small_c = ffn(x_c, mixed_c, hold(cot_c, d_query_parts), *params, 0, ())
    filled = filled[:5]
    own_c = hold(blocks_of(dot(swap_back, normed_c).astype(BF16)), got_d_query)
    sent_c = exchange(own_c)
    cot_q = in_order(hold(got_d_query, own_c))
    normed_q, res_q, dmix_q, hidden, active, d_red, d_exp, d_proj, small_q = ffn(
        x_q, mixed_q, hold(cot_q, own_c), *params, 1, filled
    )
    own_q = Return(blocks_of(dot(swap_back, hold(normed_q, sent_c)).astype(BF16)))
    content_out = arrange(hold(sent_c, normed_q), me)
    mixed = jnp.concatenate([mixed_c, mixed_q], 0)
    down = Share(*tall_grad(places[0], hold(active, content_out, own_q.send), d_red), steps_one)
    up = Share(*wide_grad(places[1], hold(hidden, down.send), d_exp, mixed, d_proj), steps_two)
    token = down.step(up.send)
    dq_q, dk, dv, circ_q, sums_q = attend_back(q_q, keys, values, mixed_q, hold(dmix_q, token), weights_q, size)
    third = 2 * model // (count * lax.axis_size("dp"))
    token = own_q.step(dq_q)
    up_one, up_two = up.split([0, 3 * third, 5 * third], [[x, y, z, far], [y, x, z, far]], token)
    back_q = Return(blocks_of(back(res_q, swap_back, hold(dq_q, up_one.send, up_two.send), w_query)))
    sent_q = own_q.step(back_q.send)
    query_out = jnp.where(picked, arrange(sent_q, me), query)
    token = down.step(query_out)
    dq_c, d_keys, d_values, circ_c, sums_c = attend_back(
        q_c, keys, values, mixed_c, hold(dmix_c, token), weights_c, size, (dk, dv)
    )
    token = up_one.step(dq_c)
    token = up_two.step(token)
    late = Share(*last_grad(places[2], hold(x_c, token), x_q, dq_c, dq_q, d_keys, d_values), steps_three)
    token = back_q.step(late.send)
    token = down.step(token)
    back_c = back(res_c, swap_back, hold(dq_c, token), w_query, d_keys, w_key, d_values, w_value)
    up = up_one.merged(up_two, back_c)
    first, second = late.split([0, third, 3 * third], [[z, y, x, far], [x, y, z, far]], up.send)
    sent_back_q = back_q.step(second.send)
    back_c = Return(blocks_of(hold(back_c, sent_back_q)))
    g_table = jnp.einsum(
        "hd,db->hb", hold(circ_c, back_c.send).reshape(heads, -1) + circ_q.reshape(heads, -1), onehot,
        precision=lax.Precision.HIGHEST,
    )
    packed = jnp.concatenate(
        [
            hold(small_c, back_c.send) + small_q + sums_c + sums_q,
            jnp.pad(g_table, ((0, 16 - heads), (0, LANES - buckets))),
        ],
        1,
    )
    exchanges = all_steps()

    def sum_step(packed, after):
        if not exchanges:
            return packed
        axis, bit = exchanges.pop(0)
        return packed + hold(partner(packed, axis, 1 << bit), after)

    token = down.step(back_c.send)
    sent_back_q = hold(sent_back_q, token)
    d_query_in = arrange(sent_back_q, me).astype(F32) + jnp.where(picked, 0.0, d_query.astype(F32))
    token = up.step(d_query_in)
    token = down.finish(token)
    packed = hold(packed, token)
    token = first.step(packed)
    packed = sum_step(packed, token)
    token = back_c.step(packed)
    token = second.step(token)
    packed = sum_step(packed, token)
    token = up.finish(packed)
    sent_c = back_c.step(token)
    d_content_in = arrange(sent_c, me).astype(F32)
    token = first.step(d_content_in)
    packed = sum_step(packed, token)
    token = second.step(packed)
    packed = sum_step(packed, token)
    late = first.merged(second, packed)
    while exchanges:
        packed = sum_step(packed, late.send)
    late.finish(late.send)
    up_out, key_value = up.keep, late.keep

    def flat(*parts):
        return jnp.concatenate([unfold_columns(p) for p in parts], 1).reshape(-1)

    vec = [packed[i, :model] for i in range(8)]
    g_b_up = packed[8 : 8 + ff // model, :model].reshape(-1)
    g_bias_table = packed[:heads, model : model + buckets].T
    return (
        content_out, query_out, d_content_in, d_query_in,
        flat(key_value[:third]), flat(key_value[third : 2 * third]), flat(key_value[2 * third :]),
        flat(up_out[-third:]), flat(*(up_out[i : i + third] for i in range(0, ff // model * third, third))),
        down.keep.reshape(-1),
        vec[6], vec[7], vec[5], vec[3], vec[4], g_b_up, vec[2], vec[0], vec[1], g_bias_table,
    )


def solution(mesh):
    tokens = P("dp", "seq", None)
    split = P(("dp", "seq"))
    in_specs = (tokens, tokens, P("dp", None), P("dp", None), P("dp", "seq")) + (P(),) * 17 + (tokens, tokens)
    out_specs = (tokens,) * 4 + (split,) * 6 + (P(),) * 10
    return jax.shard_map(local, mesh=mesh, in_specs=in_specs, out_specs=out_specs, check_vma=False)
```

```python
from functools import partial

import jax
import jax.numpy as jnp
from jax import lax
from jax.experimental import pallas as pl
from jax.experimental.pallas import tpu as pltpu
from jax.sharding import PartitionSpec as P

F32 = jnp.float32
BF16 = jnp.bfloat16
LANES = 128
EPS = 1e-5
LOG2_E = 1.4426950408889634
FOLD_VMEM = 24


def lasting(us):
    return pl.CostEstimate(flops=int(us * SHARE * 1.1e9), bytes_accessed=int(us * SHARE * 3.5e6), transcendentals=0)


SHARE = 1.0


def dot(a, b):
    return jnp.dot(a, b, preferred_element_type=F32)


def dot_nt(a, b):
    return lax.dot_general(a, b, (((1,), (1,)), ((), ())), preferred_element_type=F32)


def dot_tn(a, b):
    return lax.dot_general(a, b, (((0,), (0,)), ((), ())), preferred_element_type=F32)


def tiles_kernel(t_ref, tiles_ref):
    blocks = t_ref.shape[1] // 2
    row = lax.broadcasted_iota(jnp.int32, (LANES, LANES), 0)
    col = lax.broadcasted_iota(jnp.int32, (LANES, LANES), 1)
    for h in range(t_ref.shape[0]):
        circ = [
            pltpu.roll(jnp.broadcast_to(t_ref[h, b : b + 1, :], (LANES, LANES)), 0, 1, stride=1, stride_axis=0)
            for b in range(2 * blocks)
        ]
        for b in range(2 * blocks - 1):
            tiles_ref[h, b] = jnp.where(col >= row, circ[b + 1], circ[b])


def bias_tiles(table):
    heads, many, _ = table.shape
    step = 2
    return pl.pallas_call(
        tiles_kernel,
        grid=(heads // step,),
        in_specs=[pl.BlockSpec((step, many, LANES), lambda g: (g, 0, 0))],
        out_specs=pl.BlockSpec((step, many - 1, LANES, LANES), lambda g: (g, 0, 0, 0)),
        out_shape=jax.ShapeDtypeStruct((heads, many - 1, LANES, LANES), F32),
        compiler_params=pltpu.CompilerParams(vmem_limit_bytes=24 << 20),
        cost_estimate=lasting(2),
        name="bias_tiles",
    )(table)


def attend_kernel(
    q_ref, k_ref, v_ref, tiles_ref, segc_ref, segr_ref, plc_ref, plr_ref, mix_ref, e_ref, inv_ref, mask, line, *, size
):
    length, width = q_ref.shape
    blocks = length // LANES

    @pl.when(pl.program_id(0) == 0)
    def _():
        allowed = (segc_ref[...] == segr_ref[...]) & (plc_ref[...] <= plr_ref[...])
        mask[...] = jnp.where(allowed, 0.0, -1e30)

    owner = lax.broadcasted_iota(jnp.int32, (1, width), 1) // size
    scaled = q_ref[...].astype(F32) * LOG2_E
    high = scaled.astype(BF16).astype(F32)
    low = pltpu.roll(scaled - high, size, 1)
    keys = k_ref[...].astype(F32)
    turned = pltpu.roll(keys, size, 1)
    values = v_ref[...].astype(F32).T.astype(BF16)
    ones = jnp.ones((16, length), BF16)
    mixed = []
    for h in range(width // size):
        scores = dot_nt(
            jnp.where(owner == h, keys, turned).astype(BF16), jnp.where(owner == h, high, low).astype(BF16)
        )
        top = None
        for j in range(blocks):
            at = slice(j * LANES, (j + 1) * LANES)
            bias = jnp.concatenate([tiles_ref[h, i - j + blocks - 1] for i in range(blocks)], 1)
            part = scores[at] + bias + mask[at]
            line[h, at] = part
            part = jnp.max(part.reshape(LANES // 8, 8, length), 0)
            top = part if top is None else jnp.maximum(top, part)
        e = jnp.exp2(line[h] - jnp.max(top, 0, keepdims=True)).astype(BF16)
        e_ref[h] = e
        o = dot(jnp.concatenate([values[h * size : (h + 1) * size], ones], 0), e)
        inv = 1.0 / o[size : size + 1]
        mixed.append(o[:size] * inv)
        inv_ref[0, h : h + 1, :] = inv
    mix_ref[...] = jnp.concatenate(mixed, 0).T.astype(BF16)


def attend(queries, keys, values, tiles, seg, place, size):
    length, model = queries.shape
    width = LANES
    heads = width // size
    col = pl.BlockSpec((length, width), lambda g: (0, g))
    whole = lambda shape: pl.BlockSpec(shape, lambda g: (0, 0))
    return pl.pallas_call(
        partial(attend_kernel, size=size),
        grid=(model // width,),
        in_specs=[
            col,
            col,
            col,
            pl.BlockSpec((heads,) + tiles.shape[1:], lambda g: (g, 0, 0, 0)),
            whole((length, 1)),
            whole((1, length)),
            whole((length, 1)),
            whole((1, length)),
        ],
        out_specs=[
            col,
            pl.BlockSpec((heads, length, length), lambda g: (g, 0, 0)),
            pl.BlockSpec((1, heads, length), lambda g: (g, 0, 0)),
        ],
        out_shape=[
            jax.ShapeDtypeStruct(queries.shape, BF16),
            jax.ShapeDtypeStruct((model // size, length, length), BF16),
            jax.ShapeDtypeStruct((model // width, heads, length), F32),
        ],
        scratch_shapes=[pltpu.VMEM((length, length), F32), pltpu.VMEM((heads, length, length), F32)],
        compiler_params=pltpu.CompilerParams(vmem_limit_bytes=48 << 20),
        cost_estimate=lasting(11),
        name="attend",
    )(queries, keys, values, tiles, seg[:, None], seg[None, :], place[:, None], place[None, :])


def attend_back_kernel(q_ref, k_ref, v_ref, mix_ref, dmix_ref, e_ref, inv_ref, *refs, size, scale):
    prior, (dq_ref, dk_ref, dv_ref, gt_ref, sum_ref) = refs[:-5], refs[-5:]
    length, width = q_ref.shape
    blocks = length // LANES
    owner = lax.broadcasted_iota(jnp.int32, (1, width), 1) // size
    row = lax.broadcasted_iota(jnp.int32, (LANES, LANES), 0)
    col = lax.broadcasted_iota(jnp.int32, (LANES, LANES), 1)
    sub = lax.broadcasted_iota(jnp.int32, (8, LANES), 0)
    keys = k_ref[...].astype(F32).T.astype(BF16)
    values = v_ref[...]
    mixed = mix_ref[...].astype(F32).T
    d_mixed = dmix_ref[...].astype(F32).T
    dq = []
    dk = jnp.zeros((length, width), F32)
    dv = jnp.zeros((length, width), F32)
    for h in range(width // size):
        own = slice(h * size, (h + 1) * size)
        scaled = (d_mixed[own] * inv_ref[0, h : h + 1, :]).astype(BF16)
        inner = jnp.sum(scaled.astype(F32) * mixed[own], 0, keepdims=True)
        zeros = [jnp.zeros((h * size, length), BF16), jnp.zeros((width - (h + 1) * size, length), BF16)]
        scaled = jnp.concatenate([z for z in (zeros[0], scaled, zeros[1]) if z.shape[0]], 0)
        e = e_ref[h]
        ds = e.astype(F32) * (dot(values, scaled) - inner)
        low = ds.astype(BF16)
        dq.append(dot(keys[own], low) * scale)
        dk = dk + dot(low, jnp.where(owner == h, q_ref[...], jnp.zeros((), BF16)))
        dv = dv + dot_nt(e, scaled)
        diag = [None] * (2 * blocks + 1)
        for j in range(blocks):
            for i in range(blocks):
                part = ds[j * LANES : (j + 1) * LANES, i * LANES : (i + 1) * LANES]
                b = i - j + blocks
                diag[b] = part if diag[b] is None else diag[b] + part
        none = jnp.zeros((LANES, LANES), F32)
        diag[0] = none
        diag[2 * blocks] = none
        for b in range(2 * blocks):
            part = jnp.where(col >= row, diag[b], diag[b + 1])
            lines = part[:8]
            for r in range(8, LANES, 8):
                lines = lines + pltpu.roll(part[r : r + 8], LANES - r, 1)
            for m in (1, 2, 4):
                lines = jnp.where(sub & m != 0, pltpu.roll(lines, LANES - m, 1), lines)
            gt_ref[h, b : b + 1, :] = jnp.sum(lines, 0, keepdims=True)
    dq = jnp.concatenate(dq, 0).T.astype(BF16)
    dq_ref[...] = dq
    if prior:
        dk = dk + prior[0][...]
        dv = dv + prior[1][...]
    dv = dv.astype(dv_ref.dtype)
    dk_ref[...] = dk.astype(dk_ref.dtype)
    dv_ref[...] = dv
    sum_ref[...] = jnp.zeros_like(sum_ref)
    sum_ref[6:7, :] = jnp.sum(dq.astype(F32), 0, keepdims=True)
    if prior:
        sum_ref[7:8, :] = jnp.sum(dv.astype(F32), 0, keepdims=True)


def attend_back(queries, keys, values, mixed, d_mixed, weights, size, prior=()):
    length, model = queries.shape
    width = LANES
    heads = width // size
    blocks = length // LANES
    col = pl.BlockSpec((length, width), lambda g: (0, g))
    square = pl.BlockSpec((heads, length, length), lambda g: (g, 0, 0))
    kind = BF16 if prior else F32
    return pl.pallas_call(
        partial(attend_back_kernel, size=size, scale=size**-0.5),
        grid=(model // width,),
        in_specs=[col] * 5 + [square, pl.BlockSpec((1, heads, length), lambda g: (g, 0, 0))] + [col] * len(prior),
        out_specs=[col, col, col, pl.BlockSpec((heads, 2 * blocks, LANES), lambda g: (g, 0, 0)), pl.BlockSpec((16, width), lambda g: (0, g))],
        out_shape=[
            jax.ShapeDtypeStruct(queries.shape, BF16),
            jax.ShapeDtypeStruct(keys.shape, kind),
            jax.ShapeDtypeStruct(keys.shape, kind),
            jax.ShapeDtypeStruct((model // size, 2 * blocks, LANES), F32),
            jax.ShapeDtypeStruct((16, model), F32),
        ],
        compiler_params=pltpu.CompilerParams(vmem_limit_bytes=44 << 20),
        cost_estimate=lasting(11.5),
        name="attend_back",
    )(queries, keys, values, mixed, d_mixed, *weights, *prior)


def front_kernel(*refs, count, kinds, scale):
    parts, swap_ref, weights = refs[:count], refs[count], refs[count + 1 : count + 1 + 2 * len(kinds)]
    x_ref, outs = refs[count + 1 + 2 * len(kinds)], refs[count + 2 + 2 * len(kinds) :]

    @pl.when(pl.program_id(0) == 0)
    def _():
        x_ref[...] = dot(swap_ref[...], jnp.concatenate([p[...] for p in parts], 0)).astype(BF16)

    for i, kind in enumerate(kinds):
        out = dot(x_ref[...], weights[2 * i][...]) + weights[2 * i + 1][...]
        out = out.astype(BF16)
        outs[i][...] = out * jnp.asarray(scale, BF16) if kind else out


def front(parts, swap, weights, kinds, scale):
    length, model = swap.shape[0], parts[0].shape[1]
    width = 2 * LANES
    whole = lambda a: pl.BlockSpec(a.shape, lambda g: (0, 0))
    cols = pl.BlockSpec((length, width), lambda g: (0, g))
    operands, specs = [], []
    for w, b in weights:
        operands += [w, b]
        specs += [pl.BlockSpec((model, width), lambda g: (0, g)), pl.BlockSpec((width,), lambda g: (g,))]
    out = jax.ShapeDtypeStruct((length, model), BF16)
    return pl.pallas_call(
        partial(front_kernel, count=len(parts), kinds=kinds, scale=scale),
        grid=(model // width,),
        in_specs=[whole(p) for p in parts] + [whole(swap)] + specs,
        out_specs=[pl.BlockSpec((length, model), lambda g: (0, 0))] + [cols] * len(kinds),
        out_shape=[out] * (1 + len(kinds)),
        compiler_params=pltpu.CompilerParams(vmem_limit_bytes=40 << 20),
        cost_estimate=lasting(3),
        name="front",
    )(*parts, swap, *operands)


def back_kernel(res_ref, swap_ref, *refs):
    pairs, out_ref = refs[:-1], refs[-1]
    x = res_ref[...]
    for i in range(0, len(pairs), 2):
        x = x + dot_nt(pairs[i][...], pairs[i + 1][...])
    out_ref[...] = dot(swap_ref[...], x.astype(BF16)).astype(BF16)


def back(res, swap, *pairs):
    length, model = res.shape
    width = 2 * LANES
    cols = pl.BlockSpec((length, width), lambda g: (0, g))
    grads = pl.BlockSpec((length, model), lambda g: (0, 0))
    weights = pl.BlockSpec((width, model), lambda g: (g, 0))
    return pl.pallas_call(
        back_kernel,
        grid=(model // width,),
        in_specs=[cols, pl.BlockSpec(swap.shape, lambda g: (0, 0))] + [grads, weights] * (len(pairs) // 2),
        out_specs=cols,
        out_shape=jax.ShapeDtypeStruct((length, model), BF16),
        compiler_params=pltpu.CompilerParams(vmem_limit_bytes=50 << 20),
        cost_estimate=lasting(4.5),
        name="back",
    )(res, swap, *pairs)


def normalize(z):
    mean = jnp.mean(z, -1, keepdims=True)
    centered = z - mean
    rstd = lax.rsqrt(jnp.mean(centered * centered, -1, keepdims=True) + EPS)
    return centered * rstd, rstd


def normalize_back(cot, gain, hat, rstd):
    s = gain * cot
    return (s - jnp.mean(s, -1, keepdims=True) - hat * jnp.mean(s * hat, -1, keepdims=True)) * rstd


def gelu_pair(u):
    cdf = 0.5 + 0.5 * lax.erf(u * 0.7071067811865476)
    return u * cdf, cdf + u * (jnp.exp(u * u * -0.5) * 0.3989422804014327)


def ffn_kernel(
    x_ref, mix_ref, cot_ref, wo_ref, bo_ref, g1_ref, s1_ref, wu_ref, bu_ref, wd_ref, bd_ref, g2_ref, s2_ref, *refs,
    chunk,
):
    (
        out_ref, dres_ref, dmix_ref, hid_ref, act_ref, dred_ref, dexp_ref, dproj_ref, small_ref, slope,
    ) = refs[-10:]
    ff = wu_ref.shape[1]

    @pl.when(pl.program_id(0) == 0)
    def _():
        small_ref[...] = jnp.zeros_like(small_ref)

    def add_small(i, rows):
        small_ref[i : i + 1, :] += jnp.sum(rows, 0, keepdims=True)

    res = x_ref[...].astype(F32) + dot(mix_ref[...], wo_ref[...]) + bo_ref[...]
    hat1, rstd1 = normalize(res)
    hidden = hat1 * g1_ref[...] + s1_ref[...]
    low = hidden.astype(BF16)
    hid_ref[...] = low
    summed = hidden + bd_ref[...]
    for c in range(0, ff, chunk):
        at = slice(c, c + chunk)
        active, grad = gelu_pair(dot(low, wu_ref[:, at]) + bu_ref[at])
        active = active.astype(BF16)
        act_ref[:, at] = active
        slope[:, at] = grad
        summed = summed + dot(active, wd_ref[at, :])
    hat2, rstd2 = normalize(summed)
    out_ref[...] = (hat2 * g2_ref[...] + s2_ref[...]).astype(BF16)
    cot = cot_ref[...].astype(F32)
    d_summed = normalize_back(cot, g2_ref[...], hat2, rstd2)
    d_red = d_summed.astype(BF16)
    dred_ref[...] = d_red
    add_small(0, cot * hat2)
    add_small(1, cot)
    add_small(2, d_red.astype(F32))
    d_hidden = d_summed
    for c in range(0, ff, chunk):
        at = slice(c, c + chunk)
        d_exp = (dot_nt(d_red, wd_ref[at, :]) * slope[:, at]).astype(BF16)
        dexp_ref[:, at] = d_exp
        add_small(8 + c // chunk, d_exp.astype(F32))
        d_hidden = d_hidden + dot_nt(d_exp, wu_ref[:, at])
    d_res = normalize_back(d_hidden, g1_ref[...], hat1, rstd1)
    dres_ref[...] = d_res
    d_proj = d_res.astype(BF16)
    dproj_ref[...] = d_proj
    add_small(3, d_hidden * hat1)
    add_small(4, d_hidden)
    add_small(5, d_proj.astype(F32))
    dmix_ref[...] = dot_nt(d_proj, wo_ref[...]).astype(BF16)


def ffn(x, mixed, cot, w_out, b_out, gain_one, shift_one, w_up, b_up, w_down, b_down, gain_two, shift_two, which, filled):
    tokens, model = x.shape
    ff = w_up.shape[1]
    tile = min(256, tokens)
    chunk = model
    steps = tokens // tile
    rows = lambda n: pl.BlockSpec((tile, n), lambda i: (i, 0))
    half = lambda n: pl.BlockSpec((tile, n), lambda i: (i + which * steps, 0))
    whole = lambda shape: pl.BlockSpec(shape, lambda i: (0,) * len(shape))
    args = (
        x, mixed, cot, w_out, b_out, gain_one, shift_one, w_up, b_up, w_down, b_down, gain_two, shift_two,
    )
    own = lambda n, kind: jax.ShapeDtypeStruct((tokens, n), kind)
    shared = lambda n: jax.ShapeDtypeStruct((2 * tokens, n), BF16)
    return pl.pallas_call(
        partial(ffn_kernel, chunk=chunk),
        grid=(steps,),
        in_specs=[rows(model)] * 3
        + [pl.BlockSpec(memory_space=pltpu.VMEM) if a.ndim == 2 else whole(a.shape) for a in args[3:]]
        + [pl.BlockSpec(memory_space=pl.ANY)] * len(filled),
        out_specs=[
            rows(model), rows(model), rows(model), half(model), half(ff), half(model), half(ff), half(model),
            whole((16, model)),
        ],
        out_shape=[
            own(model, BF16), own(model, F32), own(model, BF16), shared(model), shared(ff), shared(model), shared(ff),
            shared(model), jax.ShapeDtypeStruct((16, model), F32),
        ],
        scratch_shapes=[pltpu.VMEM((tile, ff), F32)],
        input_output_aliases={len(args) + i: 3 + i for i in range(len(filled))},
        compiler_params=pltpu.CompilerParams(vmem_limit_bytes=48 << 20),
        cost_estimate=lasting(21),
        name="ffn",
    )(*args, *filled)


def partner(x, axis, mask):
    return lax.ppermute(x, axis, [(i, i ^ mask) for i in range(lax.axis_size(axis))])


def pick(x, i):
    return lax.dynamic_index_in_dim(x, i, 0, keepdims=False)


def index_bits(n):
    return [1 << b for b in reversed(range(bits(n)))]


class Gather:
    def __init__(self, x, me):
        self.me = me
        self.todo = [1 << b for b in range(bits(x.shape[0]))]
        self.cut(x[:, None])

    def cut(self, x):
        pairs = x.reshape((x.shape[0] // 2, 2) + x.shape[1:])
        mine = (self.me // self.todo[0]) % 2
        self.keep = lax.dynamic_index_in_dim(pairs, mine, 1, False)
        self.send = lax.dynamic_index_in_dim(pairs, 1 - mine, 1, False)

    def step(self, *after):
        m = self.todo.pop(0)
        got = partner(self.send, "seq", m)
        if after:
            got = hold(got, *after)
        if self.todo:
            self.cut(jnp.concatenate([self.keep, got], 1))
            return self.send
        return [p.reshape(-1, p.shape[-1]) for p in (self.keep, got)]


def row_parts(x, me):
    return [pick(x, me ^ m) for m in range(x.shape[0])]


def exchange(parts):
    return [parts[0]] + [partner(parts[m], "seq", m) for m in range(1, len(parts))]


def arrange(parts, me):
    count = len(parts)
    rows = []
    for r in range(count):
        row = parts[r]
        for m in range(1, count):
            row = jnp.where(me == m, parts[r ^ m], row)
        rows.append(row)
    return jnp.stack(rows)


def hold(x, *after):
    return lax.optimization_barrier((x, after))[0]


def bits(n):
    return n.bit_length() - 1


def device_bits():
    dp, seq = lax.axis_size("dp"), lax.axis_size("seq")
    return [("dp", b) for b in reversed(range(bits(dp)))] + [("seq", b) for b in reversed(range(bits(seq)))]


def full_order(order):
    known = device_bits()
    return [n for n in order if n in known] + [n for n in known if n not in order]


def relative_places(order):
    seq = lax.axis_size("seq")
    count = lax.axis_size("dp") * seq
    me = lax.axis_index("dp") * seq + lax.axis_index("seq")
    apart = jnp.arange(count, dtype=jnp.int32) ^ me
    place = jnp.zeros_like(apart)
    for axis, bit in order:
        place = place * 2 + ((apart >> (bit + (bits(seq) if axis == "dp" else 0))) & 1)
    return place


def fold_kernel(keep_ref, got_ref, *out_refs, cuts, bits_at):
    both = (keep_ref[...].astype(F32) + got_ref[...].astype(F32)).astype(BF16)
    for i, at in enumerate(bits_at):
        part = both[:, cuts[i] : cuts[i + 1]]
        part = part.reshape((2**at, 2, -1) + part.shape[1:])
        for j in range(2):
            out_refs[2 * i + j][...] = part[:, j].reshape(out_refs[2 * i + j].shape)


def fold(keep, got, cuts, bits_at):
    places, rows, columns = keep.shape
    if any(c % 16 for c in cuts) or places < 4:
        pairs = []
        for i, at in enumerate(bits_at):
            at_rows = slice(cuts[i], cuts[i + 1])
            both = (keep[:, at_rows].astype(F32) + got[:, at_rows].astype(F32)).astype(BF16)
            both = both.reshape((2**at, 2, -1) + both.shape[1:])
            pairs.append([both[:, j].reshape(-1, *both.shape[3:]) for j in range(2)])
        return pairs
    whole = lambda shape: pl.BlockSpec(shape, lambda g: (0, 0, 0))
    shapes = [(places // 2, cuts[i + 1] - cuts[i], columns) for i in range(len(bits_at)) for j in range(2)]
    folded = pl.pallas_call(
        partial(fold_kernel, cuts=cuts, bits_at=bits_at),
        grid=(1,),
        in_specs=[whole(keep.shape)] * 2,
        out_specs=[whole(shape) for shape in shapes],
        out_shape=[pltpu.HBM(shape, BF16) for shape in shapes],
        compiler_params=pltpu.CompilerParams(vmem_limit_bytes=FOLD_VMEM << 20),
        cost_estimate=lasting(1.5),
        name="fold",
    )(keep, got)
    return [folded[2 * i : 2 * i + 2] for i in range(len(bits_at))]


class Share:
    def __init__(self, keep, send, left, todo=None):
        self.left, self.todo = list(left), list(todo or left)
        self.keep, self.send = keep, send

    def arrive(self, after):
        axis, bit = self.todo.pop(0)
        self.left.remove((axis, bit))
        return hold(partner(self.send, axis, 1 << bit), after)

    def step(self, after):
        got = self.arrive(after)
        if self.todo:
            cuts = [0, self.keep.shape[1]]
            ((self.keep, self.send),) = fold(self.keep, got, cuts, [self.left.index(self.todo[0])])
            return self.send
        self.keep = (self.keep.astype(F32) + got.astype(F32))[0]
        return self.keep

    def finish(self, token):
        while self.todo:
            token = self.step(token)
        return token

    def split(self, cuts, orders, after):
        got = self.arrive(after)
        todos = [[n for n in order if n in self.left] + [n for n in self.left if n not in order] for order in orders]
        pairs = fold(self.keep, got, cuts, [self.left.index(todo[0]) for todo in todos])
        return [Share(*pair, self.left, todo) for pair, todo in zip(pairs, todos)]

    def merged(self, other, after):
        mine, theirs = self.arrive(after), other.arrive(after)
        both = [
            (share.keep.astype(F32) + got.astype(F32)).astype(BF16) for share, got in ((self, mine), (other, theirs))
        ]
        both = jnp.concatenate(both, 1)
        both = both.reshape((2 ** self.left.index(self.todo[0]), 2, -1) + both.shape[1:])
        return Share(*[both[:, j].reshape(-1, *both.shape[3:]) for j in range(2)], self.left, self.todo)


class Return:
    def __init__(self, blocks):
        self.todo = [1 << b for b in reversed(range(bits(len(blocks))))]
        self.rows = {0: dict(enumerate(blocks))}
        self.pack()

    def pack(self):
        m = self.todo[0]
        self.gone = [(r, i) for r in self.rows for i in self.rows[r] if i & m]
        self.send = jnp.concatenate([self.rows[r][i] for r, i in self.gone], 0)

    def step(self, after):
        m = self.todo.pop(0)
        got = hold(partner(self.send, "seq", m), after)
        size = got.shape[0] // len(self.gone)
        rows = {r: {i: b for i, b in row.items() if not i & m} for r, row in self.rows.items()}
        for n, (r, i) in enumerate(self.gone):
            rows.setdefault(r ^ m, {})[i ^ m] = got[n * size : (n + 1) * size]
        self.rows = rows
        if self.todo:
            self.pack()
            return self.send
        return [rows[r][0] for r in sorted(rows)]


def fold_columns(g):
    half = g.shape[1] // 2
    return jnp.concatenate([g[:, :half], g[:, half:]], 0)


def unfold_columns(g):
    half = g.shape[0] // 2
    return jnp.concatenate([g[:half], g[half:]], 1)


def store_part(place_ref, device, piece, keep_ref, send_ref):
    place = place_ref[device]
    half = keep_ref.shape[0]

    @pl.when(place < half)
    def _():
        keep_ref[place] = piece

    @pl.when(place >= half)
    def _():
        send_ref[place - half] = piece


def split_by_place(place, parts):
    ordered = jnp.zeros_like(parts).at[place].set(parts)
    half = parts.shape[0] // 2
    return ordered[:half], ordered[half:]


def folded_parts(g, count):
    parts = g.astype(BF16).reshape(count, g.shape[0] // count, 2, -1)
    return jnp.swapaxes(parts, 1, 2).reshape(count, -1, parts.shape[-1])


def tall_kernel(place_ref, a_ref, b_ref, keep_ref, send_ref):
    rows = keep_ref.shape[1]
    g = dot_tn(a_ref[...], b_ref[...]).astype(BF16)
    here = g.shape[0] // rows
    for k in range(here):
        store_part(place_ref, pl.program_id(0) * here + k, g[k * rows : (k + 1) * rows], keep_ref, send_ref)


def tall_grad(place, a, b):
    count = place.shape[0]
    tokens, high = a.shape
    wide = b.shape[1]
    if high // count % 16:
        return split_by_place(place, dot_tn(a, b).astype(BF16).reshape(count, -1, wide))
    steps = high // wide
    shape = (count // 2, high // count, wide)
    whole = pl.BlockSpec(shape, lambda g, p: (0, 0, 0))
    return pl.pallas_call(
        tall_kernel,
        grid_spec=pltpu.PrefetchScalarGridSpec(
            num_scalar_prefetch=1,
            grid=(steps,),
            in_specs=[
                pl.BlockSpec((tokens, wide), lambda g, p: (0, g)),
                pl.BlockSpec((tokens, wide), lambda g, p: (0, 0)),
            ],
            out_specs=[whole, whole],
        ),
        out_shape=[pltpu.HBM(shape, BF16)] * 2,
        compiler_params=pltpu.CompilerParams(vmem_limit_bytes=40 << 20),
        cost_estimate=lasting(9),
        name="tall_grad",
    )(place, a, b)


def store_all(place_ref, g, keep_ref, send_ref):
    count = 2 * keep_ref.shape[0]
    rows = g.shape[0] // count
    for k in range(count):
        store_part(
            place_ref, k, fold_columns(g[k * rows : (k + 1) * rows]).astype(BF16), keep_ref, send_ref
        )


def wide_kernel(place_ref, hid_ref, exp_ref, mix_ref, proj_ref, keep_ref, send_ref):
    last = pl.num_programs(0) - 1

    @pl.when(pl.program_id(0) < last)
    def _():
        store_all(place_ref, dot_tn(hid_ref[...], exp_ref[...]), keep_ref, send_ref)

    @pl.when(pl.program_id(0) == last)
    def _():
        store_all(place_ref, dot_tn(mix_ref[...], proj_ref[...]), keep_ref, send_ref)


def wide_grad(place, hidden, d_exp, mixed, d_proj):
    count = place.shape[0]
    tokens, model = hidden.shape
    steps = d_exp.shape[1] // model
    rows = 2 * model // count
    if rows % 16:
        pieces = [dot_tn(hidden, d_exp[:, i * model : (i + 1) * model]) for i in range(steps)] + [dot_tn(mixed, d_proj)]
        return split_by_place(place, jnp.concatenate([folded_parts(g, count) for g in pieces], 1))
    shape = (count // 2, (steps + 1) * rows, model // 2)
    square = pl.BlockSpec((tokens, model), lambda g, p: (0, 0))
    out = pl.BlockSpec((count // 2, rows, model // 2), lambda g, p: (0, g, 0))
    return pl.pallas_call(
        wide_kernel,
        grid_spec=pltpu.PrefetchScalarGridSpec(
            num_scalar_prefetch=1,
            grid=(steps + 1,),
            in_specs=[
                square,
                pl.BlockSpec((tokens, model), lambda g, p: (0, jnp.minimum(g, steps - 1))),
                square,
                square,
            ],
            out_specs=[out, out],
        ),
        out_shape=[pltpu.HBM(shape, BF16)] * 2,
        compiler_params=pltpu.CompilerParams(vmem_limit_bytes=40 << 20),
        cost_estimate=lasting(13),
        name="wide_grad",
    )(place, hidden, d_exp, mixed, d_proj)


def last_kernel(place_ref, xc_ref, xq_ref, qc_ref, qq_ref, k_ref, v_ref, keep_ref, send_ref):
    step = pl.program_id(0)

    @pl.when(step == 0)
    def _():
        g = dot_tn(xc_ref[...], qc_ref[...]) + dot_tn(xq_ref[...], qq_ref[...])
        store_all(place_ref, g, keep_ref, send_ref)

    @pl.when(step == 1)
    def _():
        store_all(place_ref, dot_tn(xc_ref[...], k_ref[...]), keep_ref, send_ref)

    @pl.when(step == 2)
    def _():
        store_all(place_ref, dot_tn(xc_ref[...], v_ref[...]), keep_ref, send_ref)


def last_grad(place, x_c, x_q, dq_c, dq_q, d_keys, d_values):
    count = place.shape[0]
    tokens, model = x_c.shape
    rows = 2 * model // count
    if rows % 16:
        pieces = [dot_tn(x_c, dq_c) + dot_tn(x_q, dq_q), dot_tn(x_c, d_keys), dot_tn(x_c, d_values)]
        return split_by_place(place, jnp.concatenate([folded_parts(g, count) for g in pieces], 1))
    shape = (count // 2, 3 * rows, model // 2)
    square = pl.BlockSpec((tokens, model), lambda g, p: (0, 0))
    out = pl.BlockSpec((count // 2, rows, model // 2), lambda g, p: (0, g, 0))
    return pl.pallas_call(
        last_kernel,
        grid_spec=pltpu.PrefetchScalarGridSpec(
            num_scalar_prefetch=1, grid=(3,), in_specs=[square] * 6, out_specs=[out, out]
        ),
        out_shape=[pltpu.HBM(shape, BF16)] * 2,
        compiler_params=pltpu.CompilerParams(vmem_limit_bytes=40 << 20),
        cost_estimate=lasting(6),
        name="last_grad",
    )(place, x_c, x_q, dq_c, dq_q, d_keys, d_values)


def all_steps():
    return [(axis, b) for axis in ("seq", "dp") for b in range(bits(lax.axis_size(axis)))]


def local(
    content, query, order, lengths, predicted, distance_bucket, w_query, b_query, w_key, w_value, b_value, w_out, b_out,
    gain_one, shift_one, w_up, b_up, w_down, b_down, gain_two, shift_two, bias_table, d_content, d_query,
):
    count = lax.axis_size("seq")
    me = lax.axis_index("seq")
    rows, block, model = content.shape
    length = order.shape[1]
    buckets, heads = bias_table.shape
    size = model // heads
    ff = w_up.shape[1]
    picked = predicted[:, :, None] == 1

    content_parts = row_parts(content, me)
    got_content = exchange(content_parts)
    query_rows = Gather(hold(query, content_parts), me)
    d_content_rows = Gather(hold(d_content, query_rows.send), me)

    own_order = pick(order, me)
    there = [(me ^ m) * block for m in range(count)]
    order_cat = jnp.concatenate([lax.dynamic_slice_in_dim(own_order, t, block, 0) for t in there])
    place_cat = jnp.concatenate([t + jnp.arange(block, dtype=jnp.int32) for t in there])
    initial = jnp.arange(length, dtype=jnp.int32)
    at_place = order_cat[None, :] == initial[:, None]
    swap = at_place.astype(BF16)
    place = jnp.sum(jnp.where(at_place, place_cat[None, :], 0), 1)
    ends = jnp.cumsum(pick(lengths, me), dtype=jnp.int32)
    seg = jnp.sum((ends[None, :] <= initial[:, None]).astype(jnp.int32), 1)

    blocks = length // LANES
    by_distance = jnp.pad(distance_bucket, (1, 0), constant_values=-1)
    onehot = (by_distance[:, None] == jnp.arange(buckets, dtype=jnp.int32)[None, :]).astype(F32)
    table = jnp.einsum("db,bh->hd", onehot, bias_table, precision=lax.Precision.HIGHEST)
    tiles = bias_tiles((table * LOG2_E).reshape(heads, 2 * blocks, LANES))

    swap_back = (order_cat[:, None] == initial[None, :]).astype(BF16)
    scale = size**-0.5

    def in_order(parts):
        return dot(swap, jnp.concatenate(parts, 0)).astype(BF16)

    def blocks_of(x):
        return [x[i * block : (i + 1) * block] for i in range(count)]

    params = (w_out, b_out, gain_one, shift_one, w_up, b_up, w_down, b_down, gain_two, shift_two)
    core, y, x, z, far = ("seq", 0), ("seq", 1), ("dp", 0), ("dp", 1), ("dp", 2)
    steps_one = full_order([core, z, x, y, far])
    steps_two = full_order([core, x, y, z, far])
    steps_three = full_order([core, x, y, z, far])
    places = [relative_places(o) for o in (steps_one, steps_two, steps_three)]

    while len(query_rows.todo) > 1:
        query_rows.step(seg)
    while len(d_content_rows.todo) > 1:
        d_content_rows.step(query_rows.send)
    got_content = hold(got_content, d_content_rows.send)
    x_c, q_c, keys, values = front(
        hold(got_content, tiles, seg, place),
        swap,
        [(w_query, b_query), (w_key, jnp.zeros((model,), F32)), (w_value, b_value)],
        (True, False, False),
        scale,
    )
    query_rows.send = hold(query_rows.send, got_content)
    got_query = query_rows.step()
    d_query_rows = Gather(jnp.where(picked, hold(d_query, query_rows.send), jnp.zeros((), BF16)), me)
    mixed_c, *weights_c = attend(hold(q_c, d_query_rows.send), keys, values, tiles, seg, place, size)
    x_q, q_q = front(hold(got_query, mixed_c), swap, [(w_query, b_query)], (True,), scale)
    d_content_rows.send = hold(d_content_rows.send, got_query, mixed_c)
    got_d_content = d_content_rows.step()
    while len(d_query_rows.todo) > 1:
        d_query_rows.step(d_content_rows.send)
    mixed_q, *weights_q = attend(hold(q_q, d_query_rows.send), keys, values, tiles, seg, place, size)
    cot_c = in_order(hold(got_d_content, mixed_q))
    d_query_rows.send = hold(d_query_rows.send, got_d_content, mixed_q)
    got_d_query = d_query_rows.step()
    normed_c, res_c, dmix_c, *filled, small_c = ffn(x_c, mixed_c, hold(cot_c, d_query_rows.send), *params, 0, ())
    filled = filled[:5]
    own_c = hold(blocks_of(dot(swap_back, normed_c).astype(BF16)), got_d_query)
    sent_c = exchange(own_c)
    cot_q = in_order(hold(got_d_query, own_c))
    normed_q, res_q, dmix_q, hidden, active, d_red, d_exp, d_proj, small_q = ffn(
        x_q, mixed_q, hold(cot_q, own_c), *params, 1, filled
    )
    own_q = Return(blocks_of(dot(swap_back, hold(normed_q, sent_c)).astype(BF16)))
    content_out = arrange(hold(sent_c, normed_q), me)
    mixed = jnp.concatenate([mixed_c, mixed_q], 0)
    down = Share(*tall_grad(places[0], hold(active, content_out, own_q.send), d_red), steps_one)
    up = Share(*wide_grad(places[1], hold(hidden, down.send), d_exp, mixed, d_proj), steps_two)
    token = down.step(up.send)
    dq_q, dk, dv, circ_q, sums_q = attend_back(q_q, keys, values, mixed_q, hold(dmix_q, token), weights_q, size)
    third = 2 * model // (count * lax.axis_size("dp"))
    token = own_q.step(dq_q)
    up_one, up_two = up.split([0, 3 * third, 5 * third], [[x, y, z, far], [y, x, z, far]], token)
    back_q = Return(blocks_of(back(res_q, swap_back, hold(dq_q, up_one.send, up_two.send), w_query)))
    sent_q = own_q.step(back_q.send)
    query_out = jnp.where(picked, arrange(sent_q, me), query)
    token = down.step(query_out)
    dq_c, d_keys, d_values, circ_c, sums_c = attend_back(
        q_c, keys, values, mixed_c, hold(dmix_c, token), weights_c, size, (dk, dv)
    )
    token = up_one.step(dq_c)
    token = up_two.step(token)
    late = Share(*last_grad(places[2], hold(x_c, token), x_q, dq_c, dq_q, d_keys, d_values), steps_three)
    token = back_q.step(late.send)
    token = down.step(token)
    back_c = back(res_c, swap_back, hold(dq_c, token), w_query, d_keys, w_key, d_values, w_value)
    up = up_one.merged(up_two, back_c)
    first, second = late.split([0, third, 3 * third], [[z, y, x, far], [x, y, z, far]], up.send)
    sent_back_q = back_q.step(second.send)
    back_c = Return(blocks_of(hold(back_c, sent_back_q)))
    g_table = jnp.einsum(
        "hd,db->hb", hold(circ_c, back_c.send).reshape(heads, -1) + circ_q.reshape(heads, -1), onehot,
        precision=lax.Precision.HIGHEST,
    )
    packed = jnp.concatenate(
        [
            hold(small_c, back_c.send) + small_q + sums_c + sums_q,
            jnp.pad(g_table, ((0, 16 - heads), (0, LANES - buckets))),
        ],
        1,
    )
    exchanges = all_steps()

    def sum_step(packed, after):
        if not exchanges:
            return packed
        axis, bit = exchanges.pop(0)
        return packed + hold(partner(packed, axis, 1 << bit), after)

    token = down.step(back_c.send)
    sent_back_q = hold(sent_back_q, token)
    d_query_in = arrange(sent_back_q, me).astype(F32) + jnp.where(picked, 0.0, d_query.astype(F32))
    token = up.step(d_query_in)
    token = down.finish(token)
    packed = hold(packed, token)
    token = first.step(packed)
    packed = sum_step(packed, token)
    token = back_c.step(packed)
    token = second.step(token)
    packed = sum_step(packed, token)
    token = up.finish(packed)
    sent_c = back_c.step(token)
    d_content_in = arrange(sent_c, me).astype(F32)
    token = first.step(d_content_in)
    packed = sum_step(packed, token)
    token = second.step(packed)
    packed = sum_step(packed, token)
    late = first.merged(second, packed)
    while exchanges:
        packed = sum_step(packed, late.send)
    late.finish(late.send)
    up_out, key_value = up.keep, late.keep

    def flat(*parts):
        return jnp.concatenate([unfold_columns(p) for p in parts], 1).reshape(-1)

    vec = [packed[i, :model] for i in range(8)]
    g_b_up = packed[8 : 8 + ff // model, :model].reshape(-1)
    g_bias_table = packed[:heads, model : model + buckets].T
    return (
        content_out, query_out, d_content_in, d_query_in,
        flat(key_value[:third]), flat(key_value[third : 2 * third]), flat(key_value[2 * third :]),
        flat(up_out[-third:]), flat(*(up_out[i : i + third] for i in range(0, ff // model * third, third))),
        down.keep.reshape(-1),
        vec[6], vec[7], vec[5], vec[3], vec[4], g_b_up, vec[2], vec[0], vec[1], g_bias_table,
    )


def solution(mesh):
    tokens = P("dp", "seq", None)
    split = P(("dp", "seq"))
    in_specs = (tokens, tokens, P("dp", None), P("dp", None), P("dp", "seq")) + (P(),) * 17 + (tokens, tokens)
    out_specs = (tokens,) * 4 + (split,) * 6 + (P(),) * 10
    return jax.shard_map(local, mesh=mesh, in_specs=in_specs, out_specs=out_specs, check_vma=False)
```

```python
from functools import partial

import jax
import jax.numpy as jnp
from jax import lax
from jax.experimental import pallas as pl
from jax.experimental.pallas import tpu as pltpu
from jax.sharding import PartitionSpec as P

F32 = jnp.float32
BF16 = jnp.bfloat16
LANES = 128
EPS = 1e-5
LOG2_E = 1.4426950408889634
FOLD_VMEM = 24


def lasting(us):
    return pl.CostEstimate(flops=int(us * SHARE * 1.1e9), bytes_accessed=int(us * SHARE * 3.5e6), transcendentals=0)


SHARE = 1.0


def dot(a, b):
    return jnp.dot(a, b, preferred_element_type=F32)


def dot_nt(a, b):
    return lax.dot_general(a, b, (((1,), (1,)), ((), ())), preferred_element_type=F32)


def dot_tn(a, b):
    return lax.dot_general(a, b, (((0,), (0,)), ((), ())), preferred_element_type=F32)


def tiles_kernel(t_ref, tiles_ref):
    blocks = t_ref.shape[1] // 2
    row = lax.broadcasted_iota(jnp.int32, (LANES, LANES), 0)
    col = lax.broadcasted_iota(jnp.int32, (LANES, LANES), 1)
    for h in range(t_ref.shape[0]):
        circ = [
            pltpu.roll(jnp.broadcast_to(t_ref[h, b : b + 1, :], (LANES, LANES)), 0, 1, stride=1, stride_axis=0)
            for b in range(2 * blocks)
        ]
        for b in range(2 * blocks - 1):
            tiles_ref[h, b] = jnp.where(col >= row, circ[b + 1], circ[b])


def bias_tiles(table):
    heads, many, _ = table.shape
    step = 2
    return pl.pallas_call(
        tiles_kernel,
        grid=(heads // step,),
        in_specs=[pl.BlockSpec((step, many, LANES), lambda g: (g, 0, 0))],
        out_specs=pl.BlockSpec((step, many - 1, LANES, LANES), lambda g: (g, 0, 0, 0)),
        out_shape=jax.ShapeDtypeStruct((heads, many - 1, LANES, LANES), F32),
        compiler_params=pltpu.CompilerParams(vmem_limit_bytes=24 << 20),
        cost_estimate=lasting(2),
        name="bias_tiles",
    )(table)


def attend_kernel(
    q_ref, k_ref, v_ref, tiles_ref, segc_ref, segr_ref, plc_ref, plr_ref, mix_ref, e_ref, inv_ref, mask, line, *, size
):
    length, width = q_ref.shape
    blocks = length // LANES

    @pl.when(pl.program_id(0) == 0)
    def _():
        allowed = (segc_ref[...] == segr_ref[...]) & (plc_ref[...] <= plr_ref[...])
        mask[...] = jnp.where(allowed, 0.0, -1e30)

    owner = lax.broadcasted_iota(jnp.int32, (1, width), 1) // size
    scaled = q_ref[...].astype(F32) * LOG2_E
    high = scaled.astype(BF16).astype(F32)
    low = pltpu.roll(scaled - high, size, 1)
    keys = k_ref[...].astype(F32)
    turned = pltpu.roll(keys, size, 1)
    values = v_ref[...].astype(F32).T.astype(BF16)
    ones = jnp.ones((16, length), BF16)
    mixed = []
    for h in range(width // size):
        scores = dot_nt(
            jnp.where(owner == h, keys, turned).astype(BF16), jnp.where(owner == h, high, low).astype(BF16)
        )
        top = None
        for j in range(blocks):
            at = slice(j * LANES, (j + 1) * LANES)
            bias = jnp.concatenate([tiles_ref[h, i - j + blocks - 1] for i in range(blocks)], 1)
            part = scores[at] + bias + mask[at]
            line[h, at] = part
            part = jnp.max(part.reshape(LANES // 8, 8, length), 0)
            top = part if top is None else jnp.maximum(top, part)
        e = jnp.exp2(line[h] - jnp.max(top, 0, keepdims=True)).astype(BF16)
        e_ref[h] = e
        o = dot(jnp.concatenate([values[h * size : (h + 1) * size], ones], 0), e)
        inv = 1.0 / o[size : size + 1]
        mixed.append(o[:size] * inv)
        inv_ref[0, h : h + 1, :] = inv
    mix_ref[...] = jnp.concatenate(mixed, 0).T.astype(BF16)


def attend(queries, keys, values, tiles, seg, place, size):
    length, model = queries.shape
    width = LANES
    heads = width // size
    col = pl.BlockSpec((length, width), lambda g: (0, g))
    whole = lambda shape: pl.BlockSpec(shape, lambda g: (0, 0))
    return pl.pallas_call(
        partial(attend_kernel, size=size),
        grid=(model // width,),
        in_specs=[
            col,
            col,
            col,
            pl.BlockSpec((heads,) + tiles.shape[1:], lambda g: (g, 0, 0, 0)),
            whole((length, 1)),
            whole((1, length)),
            whole((length, 1)),
            whole((1, length)),
        ],
        out_specs=[
            col,
            pl.BlockSpec((heads, length, length), lambda g: (g, 0, 0)),
            pl.BlockSpec((1, heads, length), lambda g: (g, 0, 0)),
        ],
        out_shape=[
            jax.ShapeDtypeStruct(queries.shape, BF16),
            jax.ShapeDtypeStruct((model // size, length, length), BF16),
            jax.ShapeDtypeStruct((model // width, heads, length), F32),
        ],
        scratch_shapes=[pltpu.VMEM((length, length), F32), pltpu.VMEM((heads, length, length), F32)],
        compiler_params=pltpu.CompilerParams(vmem_limit_bytes=48 << 20),
        cost_estimate=lasting(11),
        name="attend",
    )(queries, keys, values, tiles, seg[:, None], seg[None, :], place[:, None], place[None, :])


def attend_back_kernel(q_ref, k_ref, v_ref, mix_ref, dmix_ref, e_ref, inv_ref, *refs, size, scale):
    prior, (dq_ref, dk_ref, dv_ref, gt_ref, sum_ref) = refs[:-5], refs[-5:]
    length, width = q_ref.shape
    blocks = length // LANES
    owner = lax.broadcasted_iota(jnp.int32, (1, width), 1) // size
    row = lax.broadcasted_iota(jnp.int32, (LANES, LANES), 0)
    col = lax.broadcasted_iota(jnp.int32, (LANES, LANES), 1)
    sub = lax.broadcasted_iota(jnp.int32, (8, LANES), 0)
    keys = k_ref[...].astype(F32).T.astype(BF16)
    values = v_ref[...]
    mixed = mix_ref[...].astype(F32).T
    d_mixed = dmix_ref[...].astype(F32).T
    dq = []
    dk = jnp.zeros((length, width), F32)
    dv = jnp.zeros((length, width), F32)
    for h in range(width // size):
        own = slice(h * size, (h + 1) * size)
        scaled = (d_mixed[own] * inv_ref[0, h : h + 1, :]).astype(BF16)
        inner = jnp.sum(scaled.astype(F32) * mixed[own], 0, keepdims=True)
        zeros = [jnp.zeros((h * size, length), BF16), jnp.zeros((width - (h + 1) * size, length), BF16)]
        scaled = jnp.concatenate([z for z in (zeros[0], scaled, zeros[1]) if z.shape[0]], 0)
        e = e_ref[h]
        ds = e.astype(F32) * (dot(values, scaled) - inner)
        low = ds.astype(BF16)
        dq.append(dot(keys[own], low) * scale)
        dk = dk + dot(low, jnp.where(owner == h, q_ref[...], jnp.zeros((), BF16)))
        dv = dv + dot_nt(e, scaled)
        diag = [None] * (2 * blocks + 1)
        for j in range(blocks):
            for i in range(blocks):
                part = ds[j * LANES : (j + 1) * LANES, i * LANES : (i + 1) * LANES]
                b = i - j + blocks
                diag[b] = part if diag[b] is None else diag[b] + part
        none = jnp.zeros((LANES, LANES), F32)
        diag[0] = none
        diag[2 * blocks] = none
        for b in range(2 * blocks):
            part = jnp.where(col >= row, diag[b], diag[b + 1])
            lines = part[:8]
            for r in range(8, LANES, 8):
                lines = lines + pltpu.roll(part[r : r + 8], LANES - r, 1)
            for m in (1, 2, 4):
                lines = jnp.where(sub & m != 0, pltpu.roll(lines, LANES - m, 1), lines)
            gt_ref[h, b : b + 1, :] = jnp.sum(lines, 0, keepdims=True)
    dq = jnp.concatenate(dq, 0).T.astype(BF16)
    dq_ref[...] = dq
    if prior:
        dk = dk + prior[0][...]
        dv = dv + prior[1][...]
    dv = dv.astype(dv_ref.dtype)
    dk_ref[...] = dk.astype(dk_ref.dtype)
    dv_ref[...] = dv
    sum_ref[...] = jnp.zeros_like(sum_ref)
    sum_ref[6:7, :] = jnp.sum(dq.astype(F32), 0, keepdims=True)
    if prior:
        sum_ref[7:8, :] = jnp.sum(dv.astype(F32), 0, keepdims=True)


def attend_back(queries, keys, values, mixed, d_mixed, weights, size, prior=()):
    length, model = queries.shape
    width = LANES
    heads = width // size
    blocks = length // LANES
    col = pl.BlockSpec((length, width), lambda g: (0, g))
    square = pl.BlockSpec((heads, length, length), lambda g: (g, 0, 0))
    kind = BF16 if prior else F32
    return pl.pallas_call(
        partial(attend_back_kernel, size=size, scale=size**-0.5),
        grid=(model // width,),
        in_specs=[col] * 5 + [square, pl.BlockSpec((1, heads, length), lambda g: (g, 0, 0))] + [col] * len(prior),
        out_specs=[col, col, col, pl.BlockSpec((heads, 2 * blocks, LANES), lambda g: (g, 0, 0)), pl.BlockSpec((16, width), lambda g: (0, g))],
        out_shape=[
            jax.ShapeDtypeStruct(queries.shape, BF16),
            jax.ShapeDtypeStruct(keys.shape, kind),
            jax.ShapeDtypeStruct(keys.shape, kind),
            jax.ShapeDtypeStruct((model // size, 2 * blocks, LANES), F32),
            jax.ShapeDtypeStruct((16, model), F32),
        ],
        compiler_params=pltpu.CompilerParams(vmem_limit_bytes=44 << 20),
        cost_estimate=lasting(11.5),
        name="attend_back",
    )(queries, keys, values, mixed, d_mixed, *weights, *prior)


def front_kernel(*refs, count, kinds, scale):
    parts, swap_ref, weights = refs[:count], refs[count], refs[count + 1 : count + 1 + 2 * len(kinds)]
    x_ref, outs = refs[count + 1 + 2 * len(kinds)], refs[count + 2 + 2 * len(kinds) :]

    @pl.when(pl.program_id(0) == 0)
    def _():
        x_ref[...] = dot(swap_ref[...], jnp.concatenate([p[...] for p in parts], 0)).astype(BF16)

    for i, kind in enumerate(kinds):
        out = dot(x_ref[...], weights[2 * i][...]) + weights[2 * i + 1][...]
        out = out.astype(BF16)
        outs[i][...] = out * jnp.asarray(scale, BF16) if kind else out


def front(parts, swap, weights, kinds, scale):
    length, model = swap.shape[0], parts[0].shape[1]
    width = 2 * LANES
    whole = lambda a: pl.BlockSpec(a.shape, lambda g: (0, 0))
    cols = pl.BlockSpec((length, width), lambda g: (0, g))
    operands, specs = [], []
    for w, b in weights:
        operands += [w, b]
        specs += [pl.BlockSpec((model, width), lambda g: (0, g)), pl.BlockSpec((width,), lambda g: (g,))]
    out = jax.ShapeDtypeStruct((length, model), BF16)
    return pl.pallas_call(
        partial(front_kernel, count=len(parts), kinds=kinds, scale=scale),
        grid=(model // width,),
        in_specs=[whole(p) for p in parts] + [whole(swap)] + specs,
        out_specs=[pl.BlockSpec((length, model), lambda g: (0, 0))] + [cols] * len(kinds),
        out_shape=[out] * (1 + len(kinds)),
        compiler_params=pltpu.CompilerParams(vmem_limit_bytes=40 << 20),
        cost_estimate=lasting(3),
        name="front",
    )(*parts, swap, *operands)


def back_kernel(res_ref, swap_ref, *refs):
    pairs, out_ref = refs[:-1], refs[-1]
    x = res_ref[...]
    for i in range(0, len(pairs), 2):
        x = x + dot_nt(pairs[i][...], pairs[i + 1][...])
    out_ref[...] = dot(swap_ref[...], x.astype(BF16)).astype(BF16)


def back(res, swap, *pairs):
    length, model = res.shape
    width = 2 * LANES
    cols = pl.BlockSpec((length, width), lambda g: (0, g))
    grads = pl.BlockSpec((length, model), lambda g: (0, 0))
    weights = pl.BlockSpec((width, model), lambda g: (g, 0))
    return pl.pallas_call(
        back_kernel,
        grid=(model // width,),
        in_specs=[cols, pl.BlockSpec(swap.shape, lambda g: (0, 0))] + [grads, weights] * (len(pairs) // 2),
        out_specs=cols,
        out_shape=jax.ShapeDtypeStruct((length, model), BF16),
        compiler_params=pltpu.CompilerParams(vmem_limit_bytes=50 << 20),
        cost_estimate=lasting(4.5),
        name="back",
    )(res, swap, *pairs)


def normalize(z):
    mean = jnp.mean(z, -1, keepdims=True)
    centered = z - mean
    rstd = lax.rsqrt(jnp.mean(centered * centered, -1, keepdims=True) + EPS)
    return centered * rstd, rstd


def normalize_back(cot, gain, hat, rstd):
    s = gain * cot
    return (s - jnp.mean(s, -1, keepdims=True) - hat * jnp.mean(s * hat, -1, keepdims=True)) * rstd


def gelu_pair(u):
    cdf = 0.5 + 0.5 * lax.erf(u * 0.7071067811865476)
    return u * cdf, cdf + u * (jnp.exp(u * u * -0.5) * 0.3989422804014327)


def ffn_kernel(
    x_ref, mix_ref, cot_ref, wo_ref, bo_ref, g1_ref, s1_ref, wu_ref, bu_ref, wd_ref, bd_ref, g2_ref, s2_ref, *refs,
    chunk,
):
    (
        out_ref, dres_ref, dmix_ref, hid_ref, act_ref, dred_ref, dexp_ref, dproj_ref, small_ref, slope,
    ) = refs[-10:]
    ff = wu_ref.shape[1]

    @pl.when(pl.program_id(0) == 0)
    def _():
        small_ref[...] = jnp.zeros_like(small_ref)

    def add_small(i, rows):
        small_ref[i : i + 1, :] += jnp.sum(rows, 0, keepdims=True)

    res = x_ref[...].astype(F32) + dot(mix_ref[...], wo_ref[...]) + bo_ref[...]
    hat1, rstd1 = normalize(res)
    hidden = hat1 * g1_ref[...] + s1_ref[...]
    low = hidden.astype(BF16)
    hid_ref[...] = low
    summed = hidden + bd_ref[...]
    for c in range(0, ff, chunk):
        at = slice(c, c + chunk)
        active, grad = gelu_pair(dot(low, wu_ref[:, at]) + bu_ref[at])
        active = active.astype(BF16)
        act_ref[:, at] = active
        slope[:, at] = grad
        summed = summed + dot(active, wd_ref[at, :])
    hat2, rstd2 = normalize(summed)
    out_ref[...] = (hat2 * g2_ref[...] + s2_ref[...]).astype(BF16)
    cot = cot_ref[...].astype(F32)
    d_summed = normalize_back(cot, g2_ref[...], hat2, rstd2)
    d_red = d_summed.astype(BF16)
    dred_ref[...] = d_red
    add_small(0, cot * hat2)
    add_small(1, cot)
    add_small(2, d_red.astype(F32))
    d_hidden = d_summed
    for c in range(0, ff, chunk):
        at = slice(c, c + chunk)
        d_exp = (dot_nt(d_red, wd_ref[at, :]) * slope[:, at]).astype(BF16)
        dexp_ref[:, at] = d_exp
        add_small(8 + c // chunk, d_exp.astype(F32))
        d_hidden = d_hidden + dot_nt(d_exp, wu_ref[:, at])
    d_res = normalize_back(d_hidden, g1_ref[...], hat1, rstd1)
    dres_ref[...] = d_res
    d_proj = d_res.astype(BF16)
    dproj_ref[...] = d_proj
    add_small(3, d_hidden * hat1)
    add_small(4, d_hidden)
    add_small(5, d_proj.astype(F32))
    dmix_ref[...] = dot_nt(d_proj, wo_ref[...]).astype(BF16)


def ffn(x, mixed, cot, w_out, b_out, gain_one, shift_one, w_up, b_up, w_down, b_down, gain_two, shift_two, which, filled):
    tokens, model = x.shape
    ff = w_up.shape[1]
    tile = min(256, tokens)
    chunk = model
    steps = tokens // tile
    rows = lambda n: pl.BlockSpec((tile, n), lambda i: (i, 0))
    half = lambda n: pl.BlockSpec((tile, n), lambda i: (i + which * steps, 0))
    whole = lambda shape: pl.BlockSpec(shape, lambda i: (0,) * len(shape))
    args = (
        x, mixed, cot, w_out, b_out, gain_one, shift_one, w_up, b_up, w_down, b_down, gain_two, shift_two,
    )
    own = lambda n, kind: jax.ShapeDtypeStruct((tokens, n), kind)
    shared = lambda n: jax.ShapeDtypeStruct((2 * tokens, n), BF16)
    return pl.pallas_call(
        partial(ffn_kernel, chunk=chunk),
        grid=(steps,),
        in_specs=[rows(model)] * 3
        + [pl.BlockSpec(memory_space=pltpu.VMEM) if a.ndim == 2 else whole(a.shape) for a in args[3:]]
        + [pl.BlockSpec(memory_space=pl.ANY)] * len(filled),
        out_specs=[
            rows(model), rows(model), rows(model), half(model), half(ff), half(model), half(ff), half(model),
            whole((16, model)),
        ],
        out_shape=[
            own(model, BF16), own(model, F32), own(model, BF16), shared(model), shared(ff), shared(model), shared(ff),
            shared(model), jax.ShapeDtypeStruct((16, model), F32),
        ],
        scratch_shapes=[pltpu.VMEM((tile, ff), F32)],
        input_output_aliases={len(args) + i: 3 + i for i in range(len(filled))},
        compiler_params=pltpu.CompilerParams(vmem_limit_bytes=36 << 20),
        cost_estimate=lasting(21),
        name="ffn",
    )(*args, *filled)


def partner(x, axis, mask):
    return lax.ppermute(x, axis, [(i, i ^ mask) for i in range(lax.axis_size(axis))])


def pick(x, i):
    return lax.dynamic_index_in_dim(x, i, 0, keepdims=False)


def index_bits(n):
    return [1 << b for b in reversed(range(bits(n)))]


class Gather:
    def __init__(self, x, me):
        self.me = me
        self.todo = [1 << b for b in range(bits(x.shape[0]))]
        self.cut(x[:, None])

    def cut(self, x):
        pairs = x.reshape((x.shape[0] // 2, 2) + x.shape[1:])
        mine = (self.me // self.todo[0]) % 2
        self.keep = lax.dynamic_index_in_dim(pairs, mine, 1, False)
        self.send = lax.dynamic_index_in_dim(pairs, 1 - mine, 1, False)

    def step(self, *after):
        m = self.todo.pop(0)
        got = partner(self.send, "seq", m)
        if after:
            got = hold(got, *after)
        if self.todo:
            self.cut(jnp.concatenate([self.keep, got], 1))
            return self.send
        return [p.reshape(-1, p.shape[-1]) for p in (self.keep, got)]


def row_parts(x, me):
    return [pick(x, me ^ m) for m in range(x.shape[0])]


def exchange(parts):
    return [parts[0]] + [partner(parts[m], "seq", m) for m in range(1, len(parts))]


def arrange(parts, me):
    count = len(parts)
    rows = []
    for r in range(count):
        row = parts[r]
        for m in range(1, count):
            row = jnp.where(me == m, parts[r ^ m], row)
        rows.append(row)
    return jnp.stack(rows)


def hold(x, *after):
    return lax.optimization_barrier((x, after))[0]


def bits(n):
    return n.bit_length() - 1


def device_bits():
    dp, seq = lax.axis_size("dp"), lax.axis_size("seq")
    return [("dp", b) for b in reversed(range(bits(dp)))] + [("seq", b) for b in reversed(range(bits(seq)))]


def full_order(order):
    known = device_bits()
    return [n for n in order if n in known] + [n for n in known if n not in order]


def relative_places(order):
    seq = lax.axis_size("seq")
    count = lax.axis_size("dp") * seq
    me = lax.axis_index("dp") * seq + lax.axis_index("seq")
    apart = jnp.arange(count, dtype=jnp.int32) ^ me
    place = jnp.zeros_like(apart)
    for axis, bit in order:
        place = place * 2 + ((apart >> (bit + (bits(seq) if axis == "dp" else 0))) & 1)
    return place


def fold_kernel(keep_ref, got_ref, *out_refs, cuts, bits_at):
    both = (keep_ref[...].astype(F32) + got_ref[...].astype(F32)).astype(BF16)
    for i, at in enumerate(bits_at):
        part = both[:, cuts[i] : cuts[i + 1]]
        part = part.reshape((2**at, 2, -1) + part.shape[1:])
        for j in range(2):
            out_refs[2 * i + j][...] = part[:, j].reshape(out_refs[2 * i + j].shape)


def fold(keep, got, cuts, bits_at):
    places, rows, columns = keep.shape
    if any(c % 16 for c in cuts) or places < 4:
        pairs = []
        for i, at in enumerate(bits_at):
            at_rows = slice(cuts[i], cuts[i + 1])
            both = (keep[:, at_rows].astype(F32) + got[:, at_rows].astype(F32)).astype(BF16)
            both = both.reshape((2**at, 2, -1) + both.shape[1:])
            pairs.append([both[:, j].reshape(-1, *both.shape[3:]) for j in range(2)])
        return pairs
    whole = lambda shape: pl.BlockSpec(shape, lambda g: (0, 0, 0))
    shapes = [(places // 2, cuts[i + 1] - cuts[i], columns) for i in range(len(bits_at)) for j in range(2)]
    folded = pl.pallas_call(
        partial(fold_kernel, cuts=cuts, bits_at=bits_at),
        grid=(1,),
        in_specs=[whole(keep.shape)] * 2,
        out_specs=[whole(shape) for shape in shapes],
        out_shape=[pltpu.HBM(shape, BF16) for shape in shapes],
        compiler_params=pltpu.CompilerParams(vmem_limit_bytes=FOLD_VMEM << 20),
        cost_estimate=lasting(1.5),
        name="fold",
    )(keep, got)
    return [folded[2 * i : 2 * i + 2] for i in range(len(bits_at))]


class Share:
    def __init__(self, keep, send, left, todo=None):
        self.left, self.todo = list(left), list(todo or left)
        self.keep, self.send = keep, send

    def arrive(self, after):
        axis, bit = self.todo.pop(0)
        self.left.remove((axis, bit))
        return hold(partner(self.send, axis, 1 << bit), after)

    def step(self, after):
        got = self.arrive(after)
        if self.todo:
            cuts = [0, self.keep.shape[1]]
            ((self.keep, self.send),) = fold(self.keep, got, cuts, [self.left.index(self.todo[0])])
            return self.send
        self.keep = (self.keep.astype(F32) + got.astype(F32))[0]
        return self.keep

    def finish(self, token):
        while self.todo:
            token = self.step(token)
        return token

    def split(self, cuts, orders, after):
        got = self.arrive(after)
        todos = [[n for n in order if n in self.left] + [n for n in self.left if n not in order] for order in orders]
        pairs = fold(self.keep, got, cuts, [self.left.index(todo[0]) for todo in todos])
        return [Share(*pair, self.left, todo) for pair, todo in zip(pairs, todos)]

    def merged(self, other, after):
        mine, theirs = self.arrive(after), other.arrive(after)
        both = [
            (share.keep.astype(F32) + got.astype(F32)).astype(BF16) for share, got in ((self, mine), (other, theirs))
        ]
        both = jnp.concatenate(both, 1)
        both = both.reshape((2 ** self.left.index(self.todo[0]), 2, -1) + both.shape[1:])
        return Share(*[both[:, j].reshape(-1, *both.shape[3:]) for j in range(2)], self.left, self.todo)


class Return:
    def __init__(self, blocks):
        self.todo = [1 << b for b in reversed(range(bits(len(blocks))))]
        self.rows = {0: dict(enumerate(blocks))}
        self.pack()

    def pack(self):
        m = self.todo[0]
        self.gone = [(r, i) for r in self.rows for i in self.rows[r] if i & m]
        self.send = jnp.concatenate([self.rows[r][i] for r, i in self.gone], 0)

    def step(self, after):
        m = self.todo.pop(0)
        got = hold(partner(self.send, "seq", m), after)
        size = got.shape[0] // len(self.gone)
        rows = {r: {i: b for i, b in row.items() if not i & m} for r, row in self.rows.items()}
        for n, (r, i) in enumerate(self.gone):
            rows.setdefault(r ^ m, {})[i ^ m] = got[n * size : (n + 1) * size]
        self.rows = rows
        if self.todo:
            self.pack()
            return self.send
        return [rows[r][0] for r in sorted(rows)]


def fold_columns(g):
    half = g.shape[1] // 2
    return jnp.concatenate([g[:, :half], g[:, half:]], 0)


def unfold_columns(g):
    half = g.shape[0] // 2
    return jnp.concatenate([g[:half], g[half:]], 1)


def store_part(place_ref, device, piece, keep_ref, send_ref):
    place = place_ref[device]
    half = keep_ref.shape[0]

    @pl.when(place < half)
    def _():
        keep_ref[place] = piece

    @pl.when(place >= half)
    def _():
        send_ref[place - half] = piece


def split_by_place(place, parts):
    ordered = jnp.zeros_like(parts).at[place].set(parts)
    half = parts.shape[0] // 2
    return ordered[:half], ordered[half:]


def folded_parts(g, count):
    parts = g.astype(BF16).reshape(count, g.shape[0] // count, 2, -1)
    return jnp.swapaxes(parts, 1, 2).reshape(count, -1, parts.shape[-1])


def tall_kernel(place_ref, a_ref, b_ref, keep_ref, send_ref):
    rows = keep_ref.shape[1]
    g = dot_tn(a_ref[...], b_ref[...]).astype(BF16)
    here = g.shape[0] // rows
    for k in range(here):
        store_part(place_ref, pl.program_id(0) * here + k, g[k * rows : (k + 1) * rows], keep_ref, send_ref)


def tall_grad(place, a, b):
    count = place.shape[0]
    tokens, high = a.shape
    wide = b.shape[1]
    if high // count % 16:
        return split_by_place(place, dot_tn(a, b).astype(BF16).reshape(count, -1, wide))
    steps = high // wide
    shape = (count // 2, high // count, wide)
    whole = pl.BlockSpec(shape, lambda g, p: (0, 0, 0))
    return pl.pallas_call(
        tall_kernel,
        grid_spec=pltpu.PrefetchScalarGridSpec(
            num_scalar_prefetch=1,
            grid=(steps,),
            in_specs=[
                pl.BlockSpec((tokens, wide), lambda g, p: (0, g)),
                pl.BlockSpec((tokens, wide), lambda g, p: (0, 0)),
            ],
            out_specs=[whole, whole],
        ),
        out_shape=[pltpu.HBM(shape, BF16)] * 2,
        compiler_params=pltpu.CompilerParams(vmem_limit_bytes=40 << 20),
        cost_estimate=lasting(9),
        name="tall_grad",
    )(place, a, b)


def store_all(place_ref, g, keep_ref, send_ref):
    count = 2 * keep_ref.shape[0]
    rows = g.shape[0] // count
    for k in range(count):
        store_part(
            place_ref, k, fold_columns(g[k * rows : (k + 1) * rows]).astype(BF16), keep_ref, send_ref
        )


def wide_kernel(place_ref, hid_ref, exp_ref, mix_ref, proj_ref, keep_ref, send_ref):
    last = pl.num_programs(0) - 1

    @pl.when(pl.program_id(0) < last)
    def _():
        store_all(place_ref, dot_tn(hid_ref[...], exp_ref[...]), keep_ref, send_ref)

    @pl.when(pl.program_id(0) == last)
    def _():
        store_all(place_ref, dot_tn(mix_ref[...], proj_ref[...]), keep_ref, send_ref)


def wide_grad(place, hidden, d_exp, mixed, d_proj):
    count = place.shape[0]
    tokens, model = hidden.shape
    steps = d_exp.shape[1] // model
    rows = 2 * model // count
    if rows % 16:
        pieces = [dot_tn(hidden, d_exp[:, i * model : (i + 1) * model]) for i in range(steps)] + [dot_tn(mixed, d_proj)]
        return split_by_place(place, jnp.concatenate([folded_parts(g, count) for g in pieces], 1))
    shape = (count // 2, (steps + 1) * rows, model // 2)
    square = pl.BlockSpec((tokens, model), lambda g, p: (0, 0))
    out = pl.BlockSpec((count // 2, rows, model // 2), lambda g, p: (0, g, 0))
    return pl.pallas_call(
        wide_kernel,
        grid_spec=pltpu.PrefetchScalarGridSpec(
            num_scalar_prefetch=1,
            grid=(steps + 1,),
            in_specs=[
                square,
                pl.BlockSpec((tokens, model), lambda g, p: (0, jnp.minimum(g, steps - 1))),
                square,
                square,
            ],
            out_specs=[out, out],
        ),
        out_shape=[pltpu.HBM(shape, BF16)] * 2,
        compiler_params=pltpu.CompilerParams(vmem_limit_bytes=40 << 20),
        cost_estimate=lasting(13),
        name="wide_grad",
    )(place, hidden, d_exp, mixed, d_proj)


def last_kernel(place_ref, xc_ref, xq_ref, qc_ref, qq_ref, k_ref, v_ref, keep_ref, send_ref):
    step = pl.program_id(0)

    @pl.when(step == 0)
    def _():
        g = dot_tn(xc_ref[...], qc_ref[...]) + dot_tn(xq_ref[...], qq_ref[...])
        store_all(place_ref, g, keep_ref, send_ref)

    @pl.when(step == 1)
    def _():
        store_all(place_ref, dot_tn(xc_ref[...], k_ref[...]), keep_ref, send_ref)

    @pl.when(step == 2)
    def _():
        store_all(place_ref, dot_tn(xc_ref[...], v_ref[...]), keep_ref, send_ref)


def last_grad(place, x_c, x_q, dq_c, dq_q, d_keys, d_values):
    count = place.shape[0]
    tokens, model = x_c.shape
    rows = 2 * model // count
    if rows % 16:
        pieces = [dot_tn(x_c, dq_c) + dot_tn(x_q, dq_q), dot_tn(x_c, d_keys), dot_tn(x_c, d_values)]
        return split_by_place(place, jnp.concatenate([folded_parts(g, count) for g in pieces], 1))
    shape = (count // 2, 3 * rows, model // 2)
    square = pl.BlockSpec((tokens, model), lambda g, p: (0, 0))
    out = pl.BlockSpec((count // 2, rows, model // 2), lambda g, p: (0, g, 0))
    return pl.pallas_call(
        last_kernel,
        grid_spec=pltpu.PrefetchScalarGridSpec(
            num_scalar_prefetch=1, grid=(3,), in_specs=[square] * 6, out_specs=[out, out]
        ),
        out_shape=[pltpu.HBM(shape, BF16)] * 2,
        compiler_params=pltpu.CompilerParams(vmem_limit_bytes=40 << 20),
        cost_estimate=lasting(6),
        name="last_grad",
    )(place, x_c, x_q, dq_c, dq_q, d_keys, d_values)


def all_steps():
    return [(axis, b) for axis in ("seq", "dp") for b in range(bits(lax.axis_size(axis)))]


def local(
    content, query, order, lengths, predicted, distance_bucket, w_query, b_query, w_key, w_value, b_value, w_out, b_out,
    gain_one, shift_one, w_up, b_up, w_down, b_down, gain_two, shift_two, bias_table, d_content, d_query,
):
    count = lax.axis_size("seq")
    me = lax.axis_index("seq")
    rows, block, model = content.shape
    length = order.shape[1]
    buckets, heads = bias_table.shape
    size = model // heads
    ff = w_up.shape[1]
    picked = predicted[:, :, None] == 1

    content_parts = row_parts(content, me)
    got_content = exchange(content_parts)
    query_rows = Gather(hold(query, content_parts), me)
    d_content_rows = Gather(hold(d_content, query_rows.send), me)

    own_order = pick(order, me)
    there = [(me ^ m) * block for m in range(count)]
    order_cat = jnp.concatenate([lax.dynamic_slice_in_dim(own_order, t, block, 0) for t in there])
    place_cat = jnp.concatenate([t + jnp.arange(block, dtype=jnp.int32) for t in there])
    initial = jnp.arange(length, dtype=jnp.int32)
    at_place = order_cat[None, :] == initial[:, None]
    swap = at_place.astype(BF16)
    place = jnp.sum(jnp.where(at_place, place_cat[None, :], 0), 1)
    ends = jnp.cumsum(pick(lengths, me), dtype=jnp.int32)
    seg = jnp.sum((ends[None, :] <= initial[:, None]).astype(jnp.int32), 1)

    blocks = length // LANES
    by_distance = jnp.pad(distance_bucket, (1, 0), constant_values=-1)
    onehot = (by_distance[:, None] == jnp.arange(buckets, dtype=jnp.int32)[None, :]).astype(F32)
    table = jnp.einsum("db,bh->hd", onehot, bias_table, precision=lax.Precision.HIGHEST)
    tiles = bias_tiles((table * LOG2_E).reshape(heads, 2 * blocks, LANES))

    swap_back = (order_cat[:, None] == initial[None, :]).astype(BF16)
    scale = size**-0.5

    def in_order(parts):
        return dot(swap, jnp.concatenate(parts, 0)).astype(BF16)

    def blocks_of(x):
        return [x[i * block : (i + 1) * block] for i in range(count)]

    params = (w_out, b_out, gain_one, shift_one, w_up, b_up, w_down, b_down, gain_two, shift_two)
    core, y, x, z, far = ("seq", 0), ("seq", 1), ("dp", 0), ("dp", 1), ("dp", 2)
    steps_one = full_order([core, z, x, y, far])
    steps_two = full_order([core, x, y, z, far])
    steps_three = full_order([core, x, y, z, far])
    places = [relative_places(o) for o in (steps_one, steps_two, steps_three)]

    while len(query_rows.todo) > 1:
        query_rows.step(seg)
    while len(d_content_rows.todo) > 1:
        d_content_rows.step(query_rows.send)
    got_content = hold(got_content, d_content_rows.send)
    x_c, q_c, keys, values = front(
        hold(got_content, tiles, seg, place),
        swap,
        [(w_query, b_query), (w_key, jnp.zeros((model,), F32)), (w_value, b_value)],
        (True, False, False),
        scale,
    )
    query_rows.send = hold(query_rows.send, got_content)
    got_query = query_rows.step()
    d_query_rows = Gather(jnp.where(picked, hold(d_query, query_rows.send), jnp.zeros((), BF16)), me)
    mixed_c, *weights_c = attend(hold(q_c, d_query_rows.send), keys, values, tiles, seg, place, size)
    x_q, q_q = front(hold(got_query, mixed_c), swap, [(w_query, b_query)], (True,), scale)
    d_content_rows.send = hold(d_content_rows.send, got_query, mixed_c)
    got_d_content = d_content_rows.step()
    while len(d_query_rows.todo) > 1:
        d_query_rows.step(d_content_rows.send)
    mixed_q, *weights_q = attend(hold(q_q, d_query_rows.send), keys, values, tiles, seg, place, size)
    cot_c = in_order(hold(got_d_content, mixed_q))
    d_query_rows.send = hold(d_query_rows.send, got_d_content, mixed_q)
    got_d_query = d_query_rows.step()
    normed_c, res_c, dmix_c, *filled, small_c = ffn(x_c, mixed_c, hold(cot_c, d_query_rows.send), *params, 0, ())
    filled = filled[:5]
    own_c = hold(blocks_of(dot(swap_back, normed_c).astype(BF16)), got_d_query)
    sent_c = exchange(own_c)
    cot_q = in_order(hold(got_d_query, own_c))
    normed_q, res_q, dmix_q, hidden, active, d_red, d_exp, d_proj, small_q = ffn(
        x_q, mixed_q, hold(cot_q, own_c), *params, 1, filled
    )
    own_q = Return(blocks_of(dot(swap_back, hold(normed_q, sent_c)).astype(BF16)))
    content_out = arrange(hold(sent_c, normed_q), me)
    mixed = jnp.concatenate([mixed_c, mixed_q], 0)
    down = Share(*tall_grad(places[0], hold(active, content_out, own_q.send), d_red), steps_one)
    up = Share(*wide_grad(places[1], hold(hidden, down.send), d_exp, mixed, d_proj), steps_two)
    token = down.step(up.send)
    dq_q, dk, dv, circ_q, sums_q = attend_back(q_q, keys, values, mixed_q, hold(dmix_q, token), weights_q, size)
    third = 2 * model // (count * lax.axis_size("dp"))
    token = own_q.step(dq_q)
    up_one, up_two = up.split([0, 3 * third, 5 * third], [[x, y, z, far], [y, x, z, far]], token)
    back_q = Return(blocks_of(back(res_q, swap_back, hold(dq_q, up_one.send, up_two.send), w_query)))
    sent_q = own_q.step(back_q.send)
    query_out = jnp.where(picked, arrange(sent_q, me), query)
    token = down.step(query_out)
    dq_c, d_keys, d_values, circ_c, sums_c = attend_back(
        q_c, keys, values, mixed_c, hold(dmix_c, token), weights_c, size, (dk, dv)
    )
    token = up_one.step(dq_c)
    token = up_two.step(token)
    late = Share(*last_grad(places[2], hold(x_c, token), x_q, dq_c, dq_q, d_keys, d_values), steps_three)
    token = back_q.step(late.send)
    token = down.step(token)
    back_c = back(res_c, swap_back, hold(dq_c, token), w_query, d_keys, w_key, d_values, w_value)
    up = up_one.merged(up_two, back_c)
    first, second = late.split([0, third, 3 * third], [[z, y, x, far], [x, y, z, far]], up.send)
    sent_back_q = back_q.step(second.send)
    back_c = Return(blocks_of(hold(back_c, sent_back_q)))
    g_table = jnp.einsum(
        "hd,db->hb", hold(circ_c, back_c.send).reshape(heads, -1) + circ_q.reshape(heads, -1), onehot,
        precision=lax.Precision.HIGHEST,
    )
    packed = jnp.concatenate(
        [
            hold(small_c, back_c.send) + small_q + sums_c + sums_q,
            jnp.pad(g_table, ((0, 16 - heads), (0, LANES - buckets))),
        ],
        1,
    )
    exchanges = all_steps()

    def sum_step(packed, after):
        if not exchanges:
            return packed
        axis, bit = exchanges.pop(0)
        return packed + hold(partner(packed, axis, 1 << bit), after)

    token = down.step(back_c.send)
    sent_back_q = hold(sent_back_q, token)
    d_query_in = arrange(sent_back_q, me).astype(F32) + jnp.where(picked, 0.0, d_query.astype(F32))
    token = up.step(d_query_in)
    token = down.finish(token)
    packed = hold(packed, token)
    token = first.step(packed)
    packed = sum_step(packed, token)
    token = back_c.step(packed)
    token = second.step(token)
    packed = sum_step(packed, token)
    token = up.finish(packed)
    sent_c = back_c.step(token)
    d_content_in = arrange(sent_c, me).astype(F32)
    token = first.step(d_content_in)
    packed = sum_step(packed, token)
    token = second.step(packed)
    packed = sum_step(packed, token)
    late = first.merged(second, packed)
    while exchanges:
        packed = sum_step(packed, late.send)
    late.finish(late.send)
    up_out, key_value = up.keep, late.keep

    def flat(*parts):
        return jnp.concatenate([unfold_columns(p) for p in parts], 1).reshape(-1)

    vec = [packed[i, :model] for i in range(8)]
    g_b_up = packed[8 : 8 + ff // model, :model].reshape(-1)
    g_bias_table = packed[:heads, model : model + buckets].T
    return (
        content_out, query_out, d_content_in, d_query_in,
        flat(key_value[:third]), flat(key_value[third : 2 * third]), flat(key_value[2 * third :]),
        flat(up_out[-third:]), flat(*(up_out[i : i + third] for i in range(0, ff // model * third, third))),
        down.keep.reshape(-1),
        vec[6], vec[7], vec[5], vec[3], vec[4], g_b_up, vec[2], vec[0], vec[1], g_bias_table,
    )


def solution(mesh):
    tokens = P("dp", "seq", None)
    split = P(("dp", "seq"))
    in_specs = (tokens, tokens, P("dp", None), P("dp", None), P("dp", "seq")) + (P(),) * 17 + (tokens, tokens)
    out_specs = (tokens,) * 4 + (split,) * 6 + (P(),) * 10
    return jax.shard_map(local, mesh=mesh, in_specs=in_specs, out_specs=out_specs, check_vma=False)
```
